32 devices in a mesh: dp: 16 (over z, y, core), chan: 2 (over x).
Axes of the slice: x: 2, y: 2, z: 4, core: 2. Of those that a mesh axis runs over, the one named last changes fastest.
Arguments:
- hidden_in: bfloat16 [65536, 768], P(('dp', 'chan')), may hold values from -6 to 6
- norm_gain: float32 [768], replicated, may hold values from 0.5 to 1.5
- gate_value_weight: bfloat16 [768, 24, 128], P(None, 'chan'), may hold values from -0.21875 to 0.21875
- state_weight: bfloat16 [768, 128], replicated, may hold values from -0.21875 to 0.21875
- step_weight: bfloat16 [768, 24], P(None, 'chan'), may hold values from -0.21875 to 0.21875
- value_conv: float32 [4, 1536], P(None, 'chan'), may hold values from -3 to 3
- state_conv: float32 [4, 128], replicated, may hold values from -3 to 3
- step_bias: float32 [24], P('chan'), may hold values from -6 to -2
- decay_log: float32 [24], P('chan'), may hold values from 0 to 2.77
- skip_gain: float32 [24], P('chan'), may hold values from 0.5 to 1.5
- gate_gain: float32 [1536], P('chan'), may hold values from 0.5 to 1.5
- out_weight: bfloat16 [1536, 768], P('chan'), may hold values from -0.15625 to 0.15625
- seq_length: int32 [16], P('dp'), may hold values from 1024 to 4096, as said below
- seq_count: int32 [16], P('dp'), may hold values from 1 to 4, as said below
- out_grad: bfloat16 [65536, 768], P(('dp', 'chan')), may hold values from -6 to 6
Outputs:
- output: bfloat16 [65536, 768], P(('dp', 'chan'))
- input_grad: bfloat16 [65536, 768], P(('dp', 'chan'))
- norm_gain_grad: float32 [768], replicated
- gate_value_weight_grad: float32 [768, 24, 128], P(None, 'chan')
- state_weight_grad: float32 [768, 128], replicated
- step_weight_grad: float32 [768, 24], P(None, 'chan')
- value_conv_grad: float32 [4, 1536], P(None, 'chan')
- state_conv_grad: float32 [4, 128], replicated
- step_bias_grad: float32 [24], P('chan')
- decay_log_grad: float32 [24], P('chan')
- skip_gain_grad: float32 [24], P('chan')
- gate_gain_grad: float32 [1536], P('chan')
- out_weight_grad: float32 [1536, 768], P('chan')
The draws below stay inside these ranges and needn't reach their ends.
Inputs may be any that keep to these rules, and one draw needn't show every extreme that they name: `seq_length`: each index of dp holds sequences of one length, 1024, 2048 or 4096, laid end to end from its first slot. The first seq_count sequences of an index are live; its later slots are padding.
All inputs are finite; a program needn't handle non-finite values.
Results may differ from the reference program's by a relative error of at most 0.011.
Values may be sent and summed in bfloat16 or wider, within the bound.
A program may use at most 512 MiB of HBM per device.

```python
import jax
import jax.numpy as jnp
from jax import lax

D = 768
HEADS = 24
HEAD_DIM = 64
STATE = 64
SPAN = 128
KERNEL = 4
SEQ_MIN = 1024
TOK_DEV = 4096
INNER = 1536
GROUPS = 16
TOKENS = 65536


def length_factor(key):
    factor_bits = jax.random.randint(jax.random.fold_in(key, 11), (GROUPS,), 0, 3)
    factor_bits = factor_bits.at[0].set(2).at[1].set(0)
    return jnp.left_shift(jnp.ones_like(factor_bits), factor_bits)


def draw_seq_length(key, part):
    return (SEQ_MIN * length_factor(key)).astype(jnp.int32)


def draw_seq_count(key, part):
    limit_count = TOK_DEV // (SEQ_MIN * length_factor(key))
    fraction = jax.random.randint(jax.random.fold_in(key, 23), (GROUPS,), 0, 1048576)
    counts = 1 + jnp.right_shift(fraction * limit_count, 20)
    counts = counts.at[0].set(1).at[1].set(limit_count[1])
    return counts.astype(jnp.int32)


def steps_of(own_key, extent, cuts, least, top_value):
    gain, own = 1.0, jax.random.fold_in(own_key, 6)
    for axis_at, shards_of in cuts:
        steps = jnp.exp(jax.random.uniform(jax.random.fold_in(own, axis_at), (shards_of,), jnp.float32, least / len(cuts), top_value / len(cuts)))
        gain = gain * jnp.repeat(steps, extent[axis_at] // shards_of).reshape([-1 if axis == axis_at else 1 for axis in range(len(extent))])
    return gain


def gaussian(own_key, extent, scale, reach, cuts=(), held_as=jnp.bfloat16):
    loudness = steps_of(own_key, extent, cuts, -0.22, 0.18) if cuts else 1.0
    entries = jax.random.normal(own_key, extent, jnp.float32) * scale * loudness
    return jnp.minimum(jnp.maximum(entries, -reach), reach).astype(held_as)


def setup_inputs(seed: int = 0) -> dict:
    streams_of = jax.random.split(jax.random.key(seed), 16)
    return {
        "hidden_in": gaussian(streams_of[0], (TOKENS, D), 1.0, 6.0, ((0, 32),)),
        "norm_gain": jnp.clip(1.0 + 0.1 * jax.random.normal(streams_of[1], (D,), jnp.float32), 0.5, 1.5),
        "gate_value_weight": gaussian(streams_of[2], (D, HEADS, 2 * HEAD_DIM), D ** -0.5, 0.21875, ((1, 2),)),
        "state_weight": gaussian(streams_of[3], (D, 2 * STATE), D ** -0.5, 0.21875),
        "step_weight": gaussian(streams_of[4], (D, HEADS), D ** -0.5, 0.21875, ((1, 2),)),
        "value_conv": gaussian(streams_of[5], (KERNEL, INNER), KERNEL ** -0.5, 3.0, ((1, 2),), jnp.float32),
        "state_conv": gaussian(streams_of[6], (KERNEL, 2 * STATE), KERNEL ** -0.5, 3.0, (), jnp.float32),
        "step_bias": jnp.clip(-6.0 + 4.0 * jax.random.uniform(streams_of[7], (HEADS,), jnp.float32) ** steps_of(streams_of[7], (HEADS,), ((0, 2),), -0.2, 0.2), -6.0, -2.0),
        "decay_log": jnp.clip(2.77 * jax.random.uniform(streams_of[8], (HEADS,), jnp.float32) ** steps_of(streams_of[8], (HEADS,), ((0, 2),), -0.2, 0.2), 0.0, 2.77),
        "skip_gain": jnp.clip(0.5 + 1.0 * jax.random.uniform(streams_of[9], (HEADS,), jnp.float32) ** steps_of(streams_of[9], (HEADS,), ((0, 2),), -0.2, 0.2), 0.5, 1.5),
        "gate_gain": jnp.clip(1.0 + 0.1 * jax.random.normal(streams_of[10], (INNER,), jnp.float32), 0.5, 1.5),
        "out_weight": gaussian(streams_of[11], (INNER, D), INNER ** -0.5, 0.15625, ((0, 2),)),
        "seq_length": draw_seq_length(jax.random.fold_in(streams_of[15], 71), 0),
        "seq_count": draw_seq_count(jax.random.fold_in(streams_of[15], 71), 0),
        "out_grad": gaussian(streams_of[14], (TOKENS, D), 1.0, 6.0, ((0, 32),)),
    }


eps = 1e-05
highest = lax.Precision.HIGHEST

@jax.custom_vjp
def low(v):
    return lax.optimization_barrier(v.astype(jnp.bfloat16)).astype(jnp.float32)

@jax.custom_vjp
def low_back(v):
    return v

def low_keep(v):
    return (low(v), None)

def low_pass(kept, grad):
    return (grad,)

def back_keep(v):
    return (v, None)

def back_low(kept, grad):
    return (low(grad),)
low.defvjp(low_keep, low_pass)
low_back.defvjp(back_keep, back_low)

def causal_conv(values, kernel, places):
    length = values.shape[0]
    result = values * kernel[-1]
    for offset in range(1, kernel.shape[0]):
        shifted = jnp.pad(values, ((offset, 0), (0, 0)))[:length]
        inside = (places >= offset).astype(values.dtype)[:, None]
        result = result + shifted * inside * kernel[-1 - offset]
    return result

def direction_pass(reverse, value_blocks, in_blocks, out_blocks, step_blocks, decay_blocks, reset_flags):
    if reverse:
        summed = jnp.flip(jnp.cumsum(jnp.flip(decay_blocks, 1), axis=1), 1)
        edge_sum = summed[:, 0]
    else:
        summed = jnp.cumsum(decay_blocks, axis=1)
        edge_sum = summed[:, -1]
    block_rows = decay_blocks.shape[1]
    row_ids = lax.broadcasted_iota(jnp.int32, (block_rows, block_rows), 0)
    col_ids = lax.broadcasted_iota(jnp.int32, (block_rows, block_rows), 1)
    if reverse:
        allowed = row_ids < col_ids
    else:
        allowed = row_ids > col_ids
    allowed = allowed[None, None, :, :]
    summed_heads = jnp.transpose(summed, (0, 2, 1))
    step_heads = jnp.transpose(step_blocks, (0, 2, 1))
    spread = summed_heads[:, :, :, None] - summed_heads[:, :, None, :]
    factors = jnp.where(allowed, jnp.exp(jnp.where(allowed, spread, 0.0)), 0.0)
    affinity = jnp.einsum('bin,bjn->bij', out_blocks, in_blocks, precision=highest)
    weighted = factors * affinity[:, None, :, :] * step_heads[:, :, None, :]
    within = jnp.einsum('bhij,bjhp->bihp', weighted, value_blocks, precision=highest)
    edge_weights = jnp.exp(edge_sum[:, :, None] - summed_heads) * step_heads
    fresh = jnp.einsum('bhj,bjn,bjhp->bhnp', edge_weights, in_blocks, value_blocks, precision=highest)
    block_decay = jnp.exp(edge_sum)

    def carry_fn(state, inputs):
        fresh_block, decay_block, flag_block = inputs
        state_in = state * (1.0 - flag_block)
        return (decay_block[:, None, None] * state_in + fresh_block, state_in)
    zero_state = jnp.zeros(fresh.shape[1:], fresh.dtype)
    last_state, states_in = lax.scan(carry_fn, zero_state, (fresh, block_decay, reset_flags), reverse=reverse)
    carried = jnp.einsum('bin,bhnp->bihp', out_blocks, states_in, precision=highest) * jnp.exp(summed)[:, :, :, None]
    return within + carried

def mix_core(gate_in, proj_value, state_act, proj_step, value_conv, step_bias, decay_log, skip_gain, seq_len):
    tokens = proj_value.shape[0]
    head_count = proj_step.shape[1]
    state_dim = state_act.shape[1] // 2
    head_dim = proj_value.shape[1] // head_count
    blocks = tokens // SPAN
    places = jnp.arange(tokens, dtype=jnp.int32) % seq_len
    value_act = jax.nn.silu(causal_conv(proj_value, value_conv, places))
    step_size = jax.nn.softplus(proj_step + step_bias)
    log_decay = -step_size * jnp.exp(decay_log)
    value_blocks = value_act.reshape(blocks, SPAN, head_count, head_dim)
    in_blocks = state_act[:, :state_dim].reshape(blocks, SPAN, state_dim)
    out_blocks = state_act[:, state_dim:].reshape(blocks, SPAN, state_dim)
    step_blocks = step_size.reshape(blocks, SPAN, head_count)
    decay_blocks = log_decay.reshape(blocks, SPAN, head_count)
    starts = jnp.arange(blocks, dtype=jnp.int32) * SPAN
    first_flag = (starts % seq_len == 0).astype(value_act.dtype)
    last_flag = ((starts + SPAN) % seq_len == 0).astype(value_act.dtype)
    ahead_out = direction_pass(False, value_blocks, in_blocks, out_blocks, step_blocks, decay_blocks, first_flag)
    behind_out = direction_pass(True, value_blocks, in_blocks, out_blocks, step_blocks, decay_blocks, last_flag)
    direct = value_act.reshape(tokens, head_count, head_dim) * skip_gain[:, None]
    mixed_out = ahead_out.reshape(tokens, head_count, head_dim) + behind_out.reshape(tokens, head_count, head_dim) + direct
    return mixed_out.reshape(tokens, head_count * head_dim) * jax.nn.silu(gate_in)

def block(rows, params, seq_len, live_rows):
    norm_gain, gate_value_weight, state_weight, step_weight, value_conv, state_conv, step_bias, decay_log, skip_gain, gate_gain, out_weight = params
    width = gate_value_weight.shape[0]
    head_count = gate_value_weight.shape[1]
    head_dim = gate_value_weight.shape[2] // 2
    gate_weight = gate_value_weight[:, :, :head_dim].reshape(width, head_count * head_dim)
    value_weight = gate_value_weight[:, :, head_dim:].reshape(width, head_count * head_dim)
    row_scale = lax.rsqrt(lax.optimization_barrier(jnp.mean(rows * rows, axis=1, keepdims=True)) + eps)
    normed = low(rows * row_scale * norm_gain)
    gate_in = low_back(jnp.dot(normed, gate_weight, precision=highest))
    proj_value = low_back(jnp.dot(normed, value_weight, precision=highest))
    proj_state = low_back(jnp.dot(normed, state_weight, precision=highest))
    proj_step = low_back(jnp.dot(normed, step_weight, precision=highest))
    places = jnp.arange(rows.shape[0], dtype=jnp.int32) % seq_len
    state_act = jax.nn.silu(causal_conv(proj_state, state_conv, places))
    gated_out = mix_core(gate_in, proj_value, state_act, proj_step, value_conv, step_bias, decay_log, skip_gain, seq_len)
    gate_scale = lax.rsqrt(lax.optimization_barrier(jnp.mean(gated_out * gated_out, axis=1, keepdims=True)) + eps)
    gated_norm = low(gated_out * gate_scale * gate_gain)
    return rows + live_rows * jnp.dot(gated_norm, out_weight, precision=highest)

def reference(hidden_in, norm_gain, gate_value_weight, state_weight, step_weight, value_conv, state_conv, step_bias, decay_log, skip_gain, gate_gain, out_weight, seq_length, seq_count, out_grad):
    params = (norm_gain, gate_value_weight.astype(jnp.float32), state_weight.astype(jnp.float32), step_weight.astype(jnp.float32), value_conv, state_conv, step_bias, decay_log, skip_gain, gate_gain, out_weight.astype(jnp.float32))
    rows_all = hidden_in.reshape(GROUPS, TOK_DEV, D)
    cot_all = out_grad.reshape(GROUPS, TOK_DEV, D)

    def group_step(totals, group):
        rows, cot_rows, length, live_count = group
        live_rows = (jnp.arange(TOK_DEV, dtype=jnp.int32) // length < live_count).astype(jnp.float32)[:, None]

        def forward(inputs, weights):
            return block(inputs, weights, length, live_rows)
        result, pullback = jax.vjp(forward, rows.astype(jnp.float32), params)
        grad_rows, grad_params = pullback(cot_rows.astype(jnp.float32))
        totals = jax.tree.map(jnp.add, totals, grad_params)
        return (totals, (result.astype(jnp.bfloat16), grad_rows.astype(jnp.bfloat16)))
    zero_grads = jax.tree.map(jnp.zeros_like, params)
    totals, produced = lax.scan(group_step, zero_grads, (rows_all, cot_all, seq_length, seq_count))
    outputs, input_grads = produced
    return (outputs.reshape(TOKENS, D), input_grads.reshape(TOKENS, D), totals[0], totals[1], totals[2], totals[3], totals[4], totals[5], totals[6], totals[7], totals[8], totals[9], totals[10])
```

```python
import functools

import jax
import jax.numpy as jnp
import numpy as np
from jax import lax
from jax.experimental import pallas as pl
from jax.experimental.pallas import tpu as pltpu
from jax.sharding import PartitionSpec as P

HEAD_DIM = 64
STATE = 64
SPAN = 128
PAD = 16
GROUP = 32
TAPS = 4
EPS = 1e-05
LOG2E = float(np.log2(np.e))
BF = jnp.bfloat16
F32 = jnp.float32


def dot(a, b):
    return jnp.dot(a, b, preferred_element_type=F32)


def dot_nt(a, b):
    return lax.dot_general(a, b, (((1,), (1,)), ((), ())), preferred_element_type=F32)


def dot_tn(a, b):
    return lax.dot_general(a, b, (((0,), (0,)), ((), ())), preferred_element_type=F32)


def sigmoid(v):
    return 0.5 + 0.5 * jnp.tanh(0.5 * v)


def lanes_of(rows):
    return lax.broadcasted_iota(jnp.int32, (rows, 128), 1)


def shifted(ext, offset, rows):
    return ext[offset : offset + rows]


def full(shape):
    rank = len(shape)
    return pl.BlockSpec(shape, lambda i: (0,) * rank)


SMEM = pl.BlockSpec(memory_space=pltpu.SMEM)


def expanders(heads):
    channel = np.arange(heads * HEAD_DIM) // HEAD_DIM
    lane = np.arange(128)[:, None]
    return [np.asarray(lane == GROUP * g + channel[None], np.float32) for g in range(4)]


def project_kernel(
    tile, chunk, sc, hid, halo, edge, gain, wg, wv, ws, wst, cv, cs, bias, nal, tri, e0, e1,
    normed_o, gate_o, v_o, xpre_o, ps_o, pspre_o, bc_o, col_o, row_o, ff_o, sb_o, pb_o,
    sft_o, sbt_o, pft_o, pbt_o, vh_o, psh_o,
    sb_s, pb_s, sf_s, pf_s,
):
    step = pl.program_id(0)
    tiles = pl.num_programs(0)
    at = tiles - 1 - step
    length = sc[1]
    start = sc[0] + at * tile
    width = e0.shape[1]
    blocks = tile // SPAN

    @pl.when(step == 0)
    def _():
        sb_s[...] = jnp.zeros_like(sb_s)
        sf_s[...] = jnp.zeros_like(sf_s)
        pb_s[...] = jnp.ones_like(pb_s)
        pf_s[...] = jnp.ones_like(pf_s)

    before = jnp.where(at == 0, edge[...].astype(F32), halo[...].astype(F32))
    rows = jnp.concatenate([before, hid[...].astype(F32)], axis=0)
    scale = lax.rsqrt(jnp.mean(rows * rows, axis=1, keepdims=True) + EPS)
    normed = (rows * scale * gain[...]).astype(BF)
    own = normed[PAD:]
    normed_o[...] = own
    keep = jnp.where(lax.rem(start, length) == 0, 0.0, 1.0)
    row_id = lax.broadcasted_iota(jnp.int32, (tile + PAD, 1), 0)
    keep_rows = jnp.where(row_id < PAD, keep, 1.0)

    ps = dot(normed, ws[...]) * keep_rows
    ps_o[...] = ps[PAD:]
    pspre = ps[PAD:] * cs[TAPS - 1 : TAPS]
    for j in range(1, TAPS):
        pspre = pspre + shifted(ps, PAD - j, tile) * cs[TAPS - 1 - j : TAPS - j]
    pspre_o[...] = pspre
    bc = pspre * sigmoid(pspre)
    bc_o[...] = bc.astype(BF)

    z = dot(own, wst[...]) + bias[...]
    dt = jnp.maximum(z, 0.0) + jnp.log1p(jnp.exp(-jnp.abs(z)))
    sig = sigmoid(z)
    a2 = dt * nal[...]
    lane = lanes_of(SPAN)
    firsts, wmix, bts = [], [], []
    for b in range(blocks):
        sl = slice(b * SPAN, (b + 1) * SPAN)
        ab = a2[sl]
        ca = jnp.dot(tri[...], ab, precision=lax.Precision.HIGHEST, preferred_element_type=F32)
        ce = ca - ab
        col = jnp.where(lane < 32, ca, jnp.where(lane < 64, ce, jnp.where(lane < 96, dt[sl], sig[sl])))
        col_o[sl, :] = col
        row_o[sl, :] = jnp.transpose(col)
        end = ca[SPAN - 1 : SPAN]
        w = jnp.exp2(jnp.where(lane < 32, end - ca, ce)) * dt[sl]
        dec = jnp.broadcast_to(jnp.exp2(end), (8, 128))
        high = dec.astype(BF).astype(F32)
        wmix.append(jnp.concatenate([w, high, dec - high], axis=0).astype(BF))
        bts.append(jnp.transpose(bc[sl])[:STATE].astype(BF))

    for c in range(width // chunk):
        cl = slice(c * chunk, (c + 1) * chunk)
        gate_o[:, cl] = dot(own, wg[:, cl]).astype(BF)
        v = dot(normed, wv[:, cl]) * keep_rows
        v_o[:, cl] = v[PAD:].astype(BF)

        @pl.when(at == 0)
        def _():
            vh_o[:, cl] = v[:PAD]

        xpre = v[PAD:] * cv[TAPS - 1 : TAPS, cl]
        for j in range(1, TAPS):
            xpre = xpre + shifted(v, PAD - j, tile) * cv[TAPS - 1 - j : TAPS - j, cl]
        xpre_o[:, cl] = xpre.astype(BF)
        x = xpre * sigmoid(xpre)
        for b in reversed(range(blocks)):
            sl = slice(b * SPAN, (b + 1) * SPAN)
            we = dot(wmix[b], e0[:, cl])
            wbe = dot(wmix[b][:SPAN], e1[:, cl])
            dec = we[SPAN : SPAN + 1] + we[SPAN + 8 : SPAN + 9]
            xb = x[sl]
            fresh_f = dot(bts[b], (xb * we[:SPAN]).astype(BF))
            fresh_b = dot(bts[b], (xb * wbe).astype(BF))
            place = start + b * SPAN
            first = jnp.where(lax.rem(place, length) == 0, 0.0, 1.0)
            last = jnp.where(lax.rem(place + SPAN, length) == 0, 0.0, 1.0)
            ff_o[b, :, cl] = fresh_f.astype(BF)
            pf = pf_s[0:1, cl]
            sf_s[:, cl] = sf_s[:, cl] + pf * fresh_f
            pf_s[:, cl] = jnp.broadcast_to(pf * dec * first, (8, chunk))
            held = sb_s[:, cl] * last
            pb = pb_s[0:1, cl] * last
            sb_o[b, :, cl] = held.astype(BF)
            pb_o[b, :, cl] = jnp.broadcast_to(pb, (8, chunk))
            sb_s[:, cl] = held * dec + fresh_b
            pb_s[:, cl] = jnp.broadcast_to(pb * dec, (8, chunk))

    @pl.when(at == 0)
    def _():
        psh_o[...] = ps[:PAD]
        sft_o[...] = sf_s[...]
        sbt_o[...] = sb_s[...]
        pft_o[...] = pf_s[...]
        pbt_o[...] = pb_s[...]


def project(sc, hidden, edge, gain, wg, wv, ws, wst, cv, cs, bias, nal):
    tokens, width_in = hidden.shape
    width = wg.shape[1]
    heads = width // HEAD_DIM
    tile = min(256, tokens)
    tiles = tokens // tile
    per = tile // SPAN
    blocks = tokens // SPAN
    chunk = 256 if width % 256 == 0 else 128
    e0, e1, _, _ = expanders(heads)
    tri = np.tril(np.ones((SPAN, SPAN), np.float32))

    def back(shape):
        rank = len(shape)
        return pl.BlockSpec(shape, lambda i: (tiles - 1 - i,) + (0,) * (rank - 1))

    sds = jax.ShapeDtypeStruct
    outs = [
        (sds((tokens, width_in), BF), back((tile, width_in))),
        (sds((tokens, width), BF), back((tile, width))),
        (sds((tokens, width), BF), back((tile, width))),
        (sds((tokens, width), BF), back((tile, width))),
        (sds((tokens, 128), F32), back((tile, 128))),
        (sds((tokens, 128), F32), back((tile, 128))),
        (sds((tokens, 128), BF), back((tile, 128))),
        (sds((tokens, 128), F32), back((tile, 128))),
        (sds((tokens, 128), F32), back((tile, 128))),
        (sds((blocks, STATE, width), BF), back((per, STATE, width))),
        (sds((blocks, STATE, width), BF), back((per, STATE, width))),
        (sds((blocks, 8, width), F32), back((per, 8, width))),
        (sds((STATE, width), F32), full((STATE, width))),
        (sds((STATE, width), F32), full((STATE, width))),
        (sds((8, width), F32), full((8, width))),
        (sds((8, width), F32), full((8, width))),
        (sds((PAD, width), F32), full((PAD, width))),
        (sds((PAD, 128), F32), full((PAD, 128))),
    ]
    steps = tile // PAD
    in_specs = [
        SMEM,
        back((tile, width_in)),
        pl.BlockSpec((PAD, width_in), lambda i: (jnp.maximum((tiles - 1 - i) * steps - 1, 0), 0)),
        full((PAD, width_in)),
        full(gain.shape),
        full(wg.shape),
        full(wv.shape),
        full(ws.shape),
        full(wst.shape),
        full(cv.shape),
        full(cs.shape),
        full(bias.shape),
        full(nal.shape),
        full(tri.shape),
        full(e0.shape),
        full(e1.shape),
    ]
    return pl.pallas_call(
        functools.partial(project_kernel, tile, chunk),
        grid=(tiles,),
        in_specs=in_specs,
        out_specs=[spec for _, spec in outs],
        out_shape=[shape for shape, _ in outs],
        scratch_shapes=[
            pltpu.VMEM((STATE, width), F32),
            pltpu.VMEM((8, width), F32),
            pltpu.VMEM((STATE, width), F32),
            pltpu.VMEM((8, width), F32),
        ],
        compiler_params=pltpu.CompilerParams(vmem_limit_bytes=58 * 1024 * 1024),
        name="project",
    )(
        sc, hidden, hidden, edge, gain, wg, wv, ws, wst, cv, cs, bias, nal, tri,
        jnp.asarray(e0, BF), jnp.asarray(e1, BF),
    )


def mix_kernel(
    sc, gate, xpre, bc_r, col_r, row_r, ff, sbl, pb, sfd, sbd, hid, gout, ow, owt, ggain, skip,
    e0, e1, e2,
    out_o, gnorm_o, dy_o, dgate_o, sf_o, sb_o, gbl_o, pg_o, dff_o,
    gft_o, gbt_o, pgf_o, pgb_o, ggain_o, skip_o,
    sf_s, gb_s, gf_s, pg_s, q_s, y_s, dgn_s, exp_s,
):
    i = pl.program_id(0)
    length = sc[1]
    place = sc[0] + i * SPAN
    first = jnp.where(lax.rem(place, length) == 0, 0.0, 1.0)
    last = jnp.where(lax.rem(place + SPAN, length) == 0, 0.0, 1.0)
    live = jnp.where(lax.div(place, length) < sc[2], 1.0, 0.0)
    width = e0.shape[1]
    pairs = width // 128

    @pl.when(i == 0)
    def _():
        sf_s[...] = sfd[...].astype(F32)
        gb_s[...] = jnp.zeros_like(gb_s)
        gf_s[...] = jnp.zeros_like(gf_s)
        pg_s[...] = jnp.ones_like(pg_s)
        q_s[...] = jnp.ones_like(q_s)
        ggain_o[...] = jnp.zeros_like(ggain_o)
        skip_o[...] = jnp.zeros_like(skip_o)

    glow = gout[...].astype(F32) * live
    gl = glow.astype(BF)
    dgn_s[...] = dot(gl, owt[...])

    lane = lanes_of(SPAN)
    low_half = lane < HEAD_DIM
    col = col_r[...]
    row = row_r[...]
    end = jnp.broadcast_to(col[SPAN - 1 : SPAN], (8, 128))
    end1 = pltpu.roll(end, GROUP, 1)
    w = jnp.where(lane < 64, jnp.exp2(jnp.where(lane < 32, col, end1[0:1] - col)), col)
    dec = jnp.exp2(end)
    high = dec.astype(BF).astype(F32)
    wmix = jnp.concatenate([w, high, dec - high], axis=0).astype(BF)
    wtok = wmix[:SPAN]
    bc = bc_r[...]
    bm, cm = bc[:, :STATE], bc[:, STATE:]
    ct = jnp.transpose(bc.astype(F32))[STATE:].astype(BF)
    square_r = lax.broadcasted_iota(jnp.int32, (SPAN, SPAN), 0)
    aff = jnp.where(square_r == lane, 0.0, dot_nt(cm, bm))

    squares = jnp.zeros((SPAN, 128), F32)
    for p in range(pairs):
        sl = slice(p * 128, (p + 1) * 128)
        efd = dot(wmix, e0[:, sl])
        ef = efd[:SPAN]
        eb = dot(wtok, e1[:, sl])
        dte = dot(wtok, e2[:, sl])
        exp_s[0, :, sl] = ef
        exp_s[1, :, sl] = eb
        decay = efd[SPAN : SPAN + 1] + efd[SPAN + 8 : SPAN + 9]
        exp_s[2, 0:8, sl] = jnp.broadcast_to(decay, (8, 128))
        sf = sf_s[:, sl] * first
        sfb = sf.astype(BF)
        sf_o[0, :, sl] = sfb
        sb = (sbl[0, :, sl].astype(F32) + pb[0, 0:1, sl] * sbd[:, sl].astype(F32)) * last
        sbb = sb.astype(BF)
        sb_o[0, :, sl] = sbb
        sf_s[:, sl] = sf * decay + ff[0, :, sl].astype(F32)
        xp = xpre[:, sl].astype(F32)
        x = xp * sigmoid(xp)
        xd = x * dte
        bd = jnp.concatenate(
            [jnp.where(low_half, xd, 0.0), jnp.where(low_half, 0.0, xd)], axis=0
        ).astype(BF)
        ms = []
        for h in (2 * p, 2 * p + 1):
            spread = jnp.minimum(
                col[:, h : h + 1] - row[h : h + 1, :],
                row[GROUP + h : GROUP + h + 1, :] - col[:, GROUP + h : GROUP + h + 1],
            )
            ms.append((aff * jnp.exp2(spread)).astype(BF))
        y = dot(jnp.concatenate(ms, axis=1), bd)
        y = y + ef * dot(cm, sfb) + eb * dot(cm, sbb) + skip[:, sl] * x
        y_s[:, sl] = y
        g = gate[:, sl].astype(F32)
        gated = y * (g * sigmoid(g))
        squares = squares + gated * gated

    gsc = lax.rsqrt(jnp.sum(squares, axis=1, keepdims=True) * (1.0 / width) + EPS)
    inner = jnp.zeros((SPAN, 128), F32)
    for p in range(pairs):
        sl = slice(p * 128, (p + 1) * 128)
        g = gate[:, sl].astype(F32)
        gunit = y_s[:, sl] * (g * sigmoid(g)) * gsc
        gnorm_o[:, sl] = (gunit * ggain[:, sl]).astype(BF)
        dgn = dgn_s[:, sl]
        dgu = dgn * gunit
        ggain_o[:, sl] += jnp.sum(dgu, axis=0, keepdims=True)
        inner = inner + dgu * ggain[:, sl]
    mean = jnp.sum(inner, axis=1, keepdims=True) * (1.0 / width)
    out_o[...] = (hid[...].astype(F32) + live * dot(gnorm_o[...], ow[...])).astype(BF)

    for p in range(pairs):
        sl = slice(p * 128, (p + 1) * 128)
        g = gate[:, sl].astype(F32)
        sg = sigmoid(g)
        act = g * sg
        y = y_s[:, sl]
        gunit = y * act * gsc
        dgated = gsc * (dgn_s[:, sl] * ggain[:, sl] - gunit * mean)
        dy = dgated * act
        dy_o[:, sl] = dy.astype(BF)
        dgate_o[:, sl] = (dgated * y * (sg * (1.0 + g * (1.0 - sg)))).astype(BF)
        xp = xpre[:, sl].astype(F32)
        skip_o[:, sl] += jnp.sum(dy * (xp * sigmoid(xp)), axis=0, keepdims=True)
        decay = exp_s[2, 0:1, sl]
        dff = dot(ct, (exp_s[0, :, sl] * dy).astype(BF))
        dfb = dot(ct, (exp_s[1, :, sl] * dy).astype(BF))
        dff_o[0, :, sl] = dff.astype(BF)
        q = q_s[0:1, sl]
        gf_s[:, sl] = gf_s[:, sl] + q * dff
        q_s[:, sl] = jnp.broadcast_to(q * decay * last, (8, 128))
        gb = gb_s[:, sl] * first
        pg = pg_s[0:1, sl] * first
        gbl_o[0, :, sl] = gb.astype(BF)
        pg_o[0, :, sl] = jnp.broadcast_to(pg, (8, 128))
        gb_s[:, sl] = gb * decay + dfb
        pg_s[:, sl] = jnp.broadcast_to(pg * decay, (8, 128))

    @pl.when(i == pl.num_programs(0) - 1)
    def _():
        gft_o[...] = gf_s[...]
        gbt_o[...] = gb_s[...]
        pgf_o[...] = q_s[...]
        pgb_o[...] = pg_s[...]


def mix(sc, gate, xpre, bc, col, row, ff, sbl, pb, sfd, sbd, hidden, out_grad, ow, owt, ggain, skip):
    tokens, width_in = hidden.shape
    width = gate.shape[1]
    blocks = tokens // SPAN
    e0, e1, e2, _ = expanders(width // HEAD_DIM)

    def ahead(shape):
        rank = len(shape)
        return pl.BlockSpec(shape, lambda i: (i,) + (0,) * (rank - 1))

    sds = jax.ShapeDtypeStruct
    state = (1, STATE, width)
    outs = [
        (sds((tokens, width_in), BF), ahead((SPAN, width_in))),
        (sds((tokens, width), BF), ahead((SPAN, width))),
        (sds((tokens, width), BF), ahead((SPAN, width))),
        (sds((tokens, width), BF), ahead((SPAN, width))),
        (sds((blocks, STATE, width), BF), ahead(state)),
        (sds((blocks, STATE, width), BF), ahead(state)),
        (sds((blocks, STATE, width), BF), ahead(state)),
        (sds((blocks, 8, width), F32), ahead((1, 8, width))),
        (sds((blocks, STATE, width), BF), ahead(state)),
        (sds((STATE, width), F32), full((STATE, width))),
        (sds((STATE, width), F32), full((STATE, width))),
        (sds((8, width), F32), full((8, width))),
        (sds((8, width), F32), full((8, width))),
        (sds((1, width), F32), full((1, width))),
        (sds((1, width), F32), full((1, width))),
    ]
    in_specs = [
        SMEM,
        ahead((SPAN, width)),
        ahead((SPAN, width)),
        ahead((SPAN, 128)),
        ahead((SPAN, 128)),
        ahead((SPAN, 128)),
        ahead(state),
        ahead(state),
        ahead((1, 8, width)),
        full((STATE, width)),
        full((STATE, width)),
        ahead((SPAN, width_in)),
        ahead((SPAN, width_in)),
        full(ow.shape),
        full(owt.shape),
        full(ggain.shape),
        full(skip.shape),
        full(e0.shape),
        full(e0.shape),
        full(e0.shape),
    ]
    return pl.pallas_call(
        mix_kernel,
        grid=(blocks,),
        in_specs=in_specs,
        out_specs=[spec for _, spec in outs],
        out_shape=[shape for shape, _ in outs],
        scratch_shapes=[
            pltpu.VMEM((STATE, width), F32),
            pltpu.VMEM((STATE, width), F32),
            pltpu.VMEM((STATE, width), F32),
            pltpu.VMEM((8, width), F32),
            pltpu.VMEM((8, width), F32),
            pltpu.VMEM((SPAN, width), F32),
            pltpu.VMEM((SPAN, width), F32),
            pltpu.VMEM((3, SPAN, width), F32),
        ],
        compiler_params=pltpu.CompilerParams(vmem_limit_bytes=58 * 1024 * 1024),
        name="mix",
    )(
        sc, gate, xpre, bc, col, row, ff, sbl, pb, sfd, sbd, hidden, out_grad, ow, owt, ggain, skip,
        jnp.asarray(e0, BF), jnp.asarray(e1, BF), jnp.asarray(e2, BF),
    )


def back_kernel(
    heads, sc, xpre, v_r, dy_r, bc_r, ps_r, pspre_r, col_r, row_r, sf_r, sb_r, gbl, pg, dff, gfd, gbd,
    skip, cv, cs, nad, e0, e1, e2, seg, tris, rect,
    dv_o, dst_o, dz_o, cvg_o, csg_o, head_o, edge_o, edges_o,
    gf_s, edge_s, edges_s, da_s,
):
    step = pl.program_id(0)
    blocks = pl.num_programs(0)
    i = blocks - 1 - step
    length = sc[1]
    place = sc[0] + i * SPAN
    last = jnp.where(lax.rem(place + SPAN, length) == 0, 0.0, 1.0)
    width = e0.shape[1]
    pairs = width // 128

    @pl.when(step == 0)
    def _():
        gf_s[...] = gfd[...].astype(F32)
        edge_s[...] = jnp.zeros_like(edge_s)
        edges_s[...] = jnp.zeros_like(edges_s)
        da_s[...] = jnp.zeros_like(da_s)
        cvg_o[...] = jnp.zeros_like(cvg_o)
        csg_o[...] = jnp.zeros_like(csg_o)
        head_o[...] = jnp.zeros_like(head_o)

    lane = lanes_of(SPAN)
    low_half = lane < HEAD_DIM
    col = col_r[...]
    row = row_r[...]
    end = jnp.broadcast_to(col[SPAN - 1 : SPAN], (8, 128))
    end1 = pltpu.roll(end, GROUP, 1)
    w = jnp.where(lane < 64, jnp.exp2(jnp.where(lane < 32, col, end1[0:1] - col)), col)
    dec = jnp.exp2(end)
    high = dec.astype(BF).astype(F32)
    wmix = jnp.concatenate([w, high, dec - high], axis=0).astype(BF)
    wtok = wmix[:SPAN]
    winn = jnp.exp2(jnp.where(lane < 32, end[0:1] - col, col)).astype(BF)
    bc = bc_r[...]
    bm, cm = bc[:, :STATE], bc[:, STATE:]
    square_r = lax.broadcasted_iota(jnp.int32, (SPAN, SPAN), 0)
    off = square_r != lane
    aff = jnp.where(off, dot_nt(bm, cm), 0.0)

    daff = jnp.zeros((SPAN, SPAN), F32)
    red = jnp.zeros((SPAN, 128), F32)
    ddt = jnp.zeros((SPAN, 128), F32)
    span_sum = jnp.zeros((8, 128), F32)
    dc = jnp.zeros((SPAN, STATE), F32)
    db = jnp.zeros((SPAN, STATE), F32)
    for p in range(pairs):
        sl = slice(p * 128, (p + 1) * 128)
        efd = dot(wmix, e0[:, sl])
        ef = efd[:SPAN]
        decay = efd[SPAN : SPAN + 1] + efd[SPAN + 8 : SPAN + 9]
        eb = dot(wtok, e1[:, sl])
        dte = dot(wtok, e2[:, sl])
        wf = dot(winn, e0[:, sl])
        wb = dot(winn, e1[:, sl])
        sf, sb = sf_r[0, :, sl], sb_r[0, :, sl]
        gf32 = gf_s[:, sl] * last
        gb32 = gbl[0, :, sl].astype(F32) + pg[0, 0:1, sl] * gbd[:, sl].astype(F32)
        gf, gb = gf32.astype(BF), gb32.astype(BF)
        gf_s[:, sl] = gf32 * decay + dff[0, :, sl].astype(F32)
        cross = (sf.astype(F32) * gf32 + sb.astype(F32) * gb32) * decay
        crossed = jnp.broadcast_to(jnp.sum(cross, axis=0, keepdims=True), (8, 128))
        span_sum = span_sum + dot(crossed.astype(BF), seg[4, sl, :])
        xp = xpre[:, sl].astype(F32)
        sg = sigmoid(xp)
        x = xp * sg
        xd = x * dte
        dy = dy_r[:, sl].astype(F32)
        efdy, ebdy = ef * dy, eb * dy
        wfxd, wbxd = wf * xd, wb * xd
        cf = wf * dot(bm, gf)
        cb = wb * dot(bm, gb)
        dc = dc + dot_nt(efdy.astype(BF), sf) + dot_nt(ebdy.astype(BF), sb)
        db = db + dot_nt(wfxd.astype(BF), gf) + dot_nt(wbxd.astype(BF), gb)
        red = red + dot((efdy * dot(cm, sf)).astype(BF), seg[0, sl, :])
        red = red + dot((ebdy * dot(cm, sb)).astype(BF), seg[1, sl, :])
        red = red + dot((xd * cf).astype(BF), seg[2, sl, :])
        red = red + dot((xd * cb).astype(BF), seg[3, sl, :])
        bd = jnp.concatenate(
            [jnp.where(low_half, dy, 0.0), jnp.where(low_half, 0.0, dy)], axis=0
        ).astype(BF)
        dm = dot_nt(xd.astype(BF), bd)
        ms = []
        for k in range(2):
            h = 2 * p + k
            spread = jnp.minimum(
                row[h : h + 1, :] - col[:, h : h + 1],
                col[:, GROUP + h : GROUP + h + 1] - row[GROUP + h : GROUP + h + 1, :],
            )
            f = jnp.exp2(spread)
            m = aff * f
            ms.append(m.astype(BF))
            dmh = dm[:, k * 128 : (k + 1) * 128]
            daff = daff + f * dmh
            sums = dot((m * dmh).astype(BF), rect[...])
            inside = jnp.where(
                square_r < lane, sums[:, :SPAN], jnp.where(off, sums[:, SPAN:], 0.0)
            )
            da_s[h : h + 1, :] = jnp.sum(inside, axis=0, keepdims=True)
        dxd = dot(jnp.concatenate(ms, axis=1), bd) + cf + cb
        ddt = ddt + dot((x * dxd).astype(BF), seg[4, sl, :])
        dx = dte * dxd + skip[:, sl] * dy
        dxp = dx * (sg * (1.0 + xp * (1.0 - sg)))
        ext = jnp.concatenate([dxp, edge_s[:, sl] * last], axis=0)
        edge_s[:, sl] = dxp[:8]
        v = v_r[:, sl].astype(F32)
        dv = jnp.zeros((SPAN, 128), F32)
        for j in range(TAPS):
            moved = shifted(ext, j, SPAN)
            k = TAPS - 1 - j
            dv = dv + moved * cv[k : k + 1, sl]
            cvg_o[k : k + 1, sl] += jnp.sum(v * moved, axis=0, keepdims=True)
        dv_o[:, sl] = dv.astype(BF)

    dafb = jnp.where(off, daff, 0.0).astype(BF)
    db = db + dot(dafb, cm)
    dc = dc + dot_tn(dafb, bm)
    dbc = jnp.concatenate([db, dc], axis=1)
    pp = pspre_r[...]
    sp = sigmoid(pp)
    dpp = dbc * (sp * (1.0 + pp * (1.0 - sp)))
    ext = jnp.concatenate([dpp, edges_s[...] * last], axis=0)
    edges_s[...] = dpp[:8]
    ps = ps_r[...]
    dst = jnp.zeros((SPAN, 128), F32)
    for j in range(TAPS):
        moved = shifted(ext, j, SPAN)
        k = TAPS - 1 - j
        dst = dst + moved * cs[k : k + 1, :]
        csg_o[k : k + 1, :] += jnp.sum(ps * moved, axis=0, keepdims=True)
    dst_o[...] = dst.astype(BF)

    hi = red.astype(BF)
    lo = (red - hi.astype(F32)).astype(BF)
    summed = dot(tris[...], hi) + dot(tris[...], lo)
    parts = [summed[g * SPAN : (g + 1) * SPAN] for g in range(4)]
    picked = jnp.where(
        lane < 32, parts[0], jnp.where(lane < 64, parts[1], jnp.where(lane < 96, parts[2], parts[3]))
    )
    picked = picked + jnp.transpose(da_s[...])
    total = picked + pltpu.roll(picked, 64, 1)
    total = total + pltpu.roll(total, 32, 1)
    da = total + span_sum[0:1]
    dz = (ddt + da * nad[...]) * col
    dz = jnp.where((lane >= 96) & (lane < 96 + heads), dz, 0.0)
    dz_o[...] = dz.astype(BF)
    head_o[0:1, :] += jnp.sum(da * col * nad[...], axis=0, keepdims=True)
    head_o[1:2, :] += jnp.sum(dz, axis=0, keepdims=True)

    @pl.when(i == 0)
    def _():
        edge_o[...] = edge_s[...]
        edges_o[...] = edges_s[...]


def back(
    heads, sc, xpre, v, dy, bc, ps, pspre, col, row, sf, sb, gbl, pg, dff, gfd, gbd, skip, cv, cs, nad
):
    tokens, width = xpre.shape
    blocks = tokens // SPAN
    maps = expanders(width // HEAD_DIM)
    every = sum(maps)
    seg = np.stack([m.T for m in maps] + [every.T])
    at = np.arange(SPAN)
    row_at, col_at = at[:, None], at[None, :]
    tris = np.concatenate(
        [col_at >= row_at, col_at <= row_at, col_at < row_at, col_at > row_at], axis=0
    ).astype(np.float32)
    rect = np.concatenate([row_at >= col_at, row_at <= col_at], axis=1).astype(np.float32)

    def rev(shape):
        rank = len(shape)
        return pl.BlockSpec(shape, lambda i: (blocks - 1 - i,) + (0,) * (rank - 1))

    sds = jax.ShapeDtypeStruct
    state = (1, STATE, width)
    outs = [
        (sds((tokens, width), BF), rev((SPAN, width))),
        (sds((tokens, 128), BF), rev((SPAN, 128))),
        (sds((tokens, 128), BF), rev((SPAN, 128))),
        (sds((TAPS, width), F32), full((TAPS, width))),
        (sds((TAPS, 128), F32), full((TAPS, 128))),
        (sds((8, 128), F32), full((8, 128))),
        (sds((8, width), F32), full((8, width))),
        (sds((8, 128), F32), full((8, 128))),
    ]
    in_specs = [
        SMEM,
        rev((SPAN, width)),
        rev((SPAN, width)),
        rev((SPAN, width)),
        rev((SPAN, 128)),
        rev((SPAN, 128)),
        rev((SPAN, 128)),
        rev((SPAN, 128)),
        rev((SPAN, 128)),
        rev(state),
        rev(state),
        rev(state),
        rev((1, 8, width)),
        rev(state),
        full((STATE, width)),
        full((STATE, width)),
        full(skip.shape),
        full(cv.shape),
        full(cs.shape),
        full(nad.shape),
        full((128, width)),
        full((128, width)),
        full((128, width)),
        full(seg.shape),
        full(tris.shape),
        full(rect.shape),
    ]
    return pl.pallas_call(
        functools.partial(back_kernel, heads),
        grid=(blocks,),
        in_specs=in_specs,
        out_specs=[spec for _, spec in outs],
        out_shape=[shape for shape, _ in outs],
        scratch_shapes=[
            pltpu.VMEM((STATE, width), F32),
            pltpu.VMEM((8, width), F32),
            pltpu.VMEM((8, 128), F32),
            pltpu.VMEM((128, 128), F32),
        ],
        compiler_params=pltpu.CompilerParams(vmem_limit_bytes=58 * 1024 * 1024),
        name="back",
    )(
        sc, xpre, v, dy, bc, ps, pspre, col, row, sf, sb, gbl, pg, dff, gfd, gbd, skip, cv, cs, nad,
        jnp.asarray(maps[0], BF), jnp.asarray(maps[1], BF), jnp.asarray(maps[2], BF),
        jnp.asarray(seg, BF), jnp.asarray(tris, BF), jnp.asarray(rect, BF),
    )


def spread_heads(v):
    padded = jnp.zeros((GROUP,), F32).at[: v.shape[0]].set(v)
    return jnp.tile(padded, 4)[None]


def handed(total, passed, shards, up):
    pairs = [(k, k + 1) if up else (k + 1, k) for k in range(shards - 1)]
    entering = lax.ppermute(total.astype(BF), "chan", pairs)
    for _ in range(shards - 2):
        now = total + passed[0:1] * entering.astype(F32)
        entering = lax.ppermute(now.astype(BF), "chan", pairs)
    return entering


def on_device(
    hidden_in, norm_gain, gate_value_weight, state_weight, step_weight, value_conv, state_conv,
    step_bias, decay_log, skip_gain, gate_gain, out_weight, seq_length, seq_count, out_grad,
):
    tokens, width_in = hidden_in.shape
    channel = lax.axis_index("chan")
    shards = lax.axis_size("chan")
    length, count = seq_length[0], seq_count[0]
    sc = jnp.stack([channel * tokens, length, count, 0]).astype(jnp.int32)
    local_heads = gate_value_weight.shape[1]
    local = local_heads * HEAD_DIM

    def gather(v, axis):
        return lax.all_gather(v, "chan", axis=axis, tiled=True)

    wg = gather(gate_value_weight[:, :, :HEAD_DIM].reshape(width_in, local), 1)
    wv = gather(gate_value_weight[:, :, HEAD_DIM:].reshape(width_in, local), 1)
    ow = gather(out_weight, 0)
    heads = local_heads * shards
    width = heads * HEAD_DIM
    small = jnp.concatenate(
        [value_conv.reshape(-1), gate_gain, step_bias, decay_log, skip_gain]
    )
    small = gather(small[None], 0)
    cuts = np.cumsum([TAPS * local, local, local_heads, local_heads])
    cv = small[:, : cuts[0]].reshape(shards, TAPS, local).transpose(1, 0, 2).reshape(TAPS, width)
    ggain = small[:, cuts[0] : cuts[1]].reshape(1, width)
    bias_all = small[:, cuts[1] : cuts[2]].reshape(heads)
    dlog_all = small[:, cuts[2] : cuts[3]].reshape(heads)
    skip_all = small[:, cuts[3] :].reshape(heads)
    wstep = gather(step_weight, 1)
    wst = jnp.tile(jnp.pad(wstep, ((0, 0), (0, GROUP - heads))), (1, 4))
    skip = jnp.repeat(skip_all, HEAD_DIM)[None]
    nad = -jnp.exp(dlog_all)
    gain = norm_gain[None]

    ups = [(k, k + 1) for k in range(shards - 1)]
    downs = [(k + 1, k) for k in range(shards - 1)]
    edge = lax.ppermute(hidden_in[tokens - PAD :], "chan", ups)

    (
        normed, gate, v, xpre, ps, pspre, bc, col, row, ff, sbl, pb, sft, sbt, pft, pbt, vh, psh,
    ) = project(
        sc, hidden_in, edge, gain, wg, wv, state_weight, wst, cv, state_conv,
        spread_heads(bias_all), spread_heads(nad * LOG2E),
    )
    sfd = handed(sft, pft, shards, True)
    sbd = handed(sbt, pbt, shards, False)
    (
        output, gnorm, dy, dgate, sf, sb, gbl, pg, dff, gft, gbt, pgf, pgb, ggain_grad, skip_grad,
    ) = mix(
        sc, gate, xpre, bc, col, row, ff, sbl, pb, sfd, sbd, hidden_in, out_grad, ow, ow.T, ggain, skip
    )
    gfd = handed(gft, pgf, shards, False)
    gbd = handed(gbt, pgb, shards, True)
    dv, dst, dz, cvg, csg, head_sums, edge_g, edges_g = back(
        heads, sc, xpre, v, dy, bc, ps, pspre, col, row, sf, sb, gbl, pg, dff, gfd, gbd, skip, cv,
        state_conv, spread_heads(nad),
    )

    joined = jnp.concatenate([edge_g, edges_g], axis=1)
    kernel = jnp.concatenate([cv, state_conv], axis=1)
    past = jnp.concatenate([vh, psh], axis=1)
    reach = TAPS - 1
    after = lax.ppermute(joined, "chan", downs)[:reach]
    after = after * jnp.where(((channel + 1) * tokens) % length == 0, 0.0, 1.0)
    patch = jnp.zeros((reach, joined.shape[1]), F32)
    taps = []
    for j in range(TAPS):
        moved = jnp.zeros_like(patch).at[reach - j :].set(after[:j]) if j else jnp.zeros_like(patch)
        patch = patch + moved * kernel[TAPS - 1 - j][None]
        own = joined[:j] * past[PAD - j :]
        taps.append(jnp.sum(own, axis=0))
    cross_taps = jnp.stack(taps[::-1])
    tail = jnp.pad(patch, ((PAD - reach, 0), (0, 0)))
    dv = dv.at[tokens - PAD :].add(tail[:, :width].astype(BF))
    dst = dst.at[tokens - PAD :].add(tail[:, width:].astype(BF))
    cvg = cvg + cross_taps[:, :width]
    csg = csg + cross_taps[:, width:]

    gl_scale = jnp.where(
        (channel * tokens + jnp.arange(tokens, dtype=jnp.int32)) // length < count, 1.0, 0.0
    )[:, None]
    gl = (out_grad * gl_scale.astype(BF)).astype(BF)
    ow_grad = dot_tn(gnorm, gl)
    dwg = dot_tn(normed, dgate)
    dwv = dot_tn(normed, dv)
    dws = dot_tn(normed, dst)
    dwst = dot_tn(normed, dz)[:, 96 : 96 + heads]
    wst_tail = jnp.pad(wstep, ((0, 0), (96, GROUP - heads)))
    dn = dot_nt(dgate, wg) + dot_nt(dv, wv) + dot_nt(dst, state_weight) + dot_nt(dz, wst_tail)
    u = hidden_in.astype(F32)
    scale = lax.rsqrt(jnp.mean(u * u, axis=1, keepdims=True) + EPS)
    unit = u * scale
    norm_gain_grad = jnp.sum(dn * unit, axis=0)
    du = dn * gain
    inner = jnp.mean(du * unit, axis=1, keepdims=True)
    input_grad = (out_grad.astype(F32) + scale * (du - unit * inner)).astype(BF)

    gvw = jnp.stack(
        [dwg.reshape(width_in, heads, HEAD_DIM), dwv.reshape(width_in, heads, HEAD_DIM)], axis=2
    ).reshape(width_in, heads, 2 * HEAD_DIM)
    gvw = lax.psum(
        lax.psum_scatter(gvw.astype(BF), "chan", scatter_dimension=1, tiled=True), "dp"
    ).astype(F32)
    owg = lax.psum(
        lax.psum_scatter(ow_grad.astype(BF), "chan", scatter_dimension=0, tiled=True), "dp"
    ).astype(F32)
    smalls = (
        norm_gain_grad, dws, dwst, cvg, csg, head_sums[1, 96 : 96 + heads],
        head_sums[0, 64 : 64 + heads], skip_grad.reshape(heads, HEAD_DIM).sum(axis=1), ggain_grad[0],
    )
    sizes = [int(np.prod(s.shape)) for s in smalls]
    flat = lax.psum(jnp.concatenate([s.reshape(-1) for s in smalls]), ("dp", "chan"))
    pieces, offset = [], 0
    for s, size in zip(smalls, sizes):
        pieces.append(flat[offset : offset + size].reshape(s.shape))
        offset += size
    ngg, dws, dwst, cvg, csg, sbg, dlg, skg, ggg = pieces

    def mine(v, count_local, axis):
        return lax.dynamic_slice_in_dim(v, channel * count_local, count_local, axis)

    return (
        output,
        input_grad,
        ngg,
        gvw,
        dws,
        mine(dwst, local_heads, 1),
        mine(cvg, local, 1),
        csg,
        mine(sbg, local_heads, 0),
        mine(dlg, local_heads, 0),
        mine(skg, local_heads, 0),
        mine(ggg, local, 0),
        owg,
    )


def solution(mesh):
    in_specs = (
        P(("dp", "chan"), None),
        P(),
        P(None, "chan", None),
        P(),
        P(None, "chan"),
        P(None, "chan"),
        P(),
        P("chan"),
        P("chan"),
        P("chan"),
        P("chan"),
        P("chan", None),
        P("dp"),
        P("dp"),
        P(("dp", "chan"), None),
    )
    out_specs = (
        P(("dp", "chan"), None),
        P(("dp", "chan"), None),
        P(),
        P(None, "chan", None),
        P(),
        P(None, "chan"),
        P(None, "chan"),
        P(),
        P("chan"),
        P("chan"),
        P("chan"),
        P("chan"),
        P("chan", None),
    )
    return jax.shard_map(
        on_device, mesh=mesh, in_specs=in_specs, out_specs=out_specs, check_vma=False
    )
```

```python
import functools

import jax
import jax.numpy as jnp
import numpy as np
from jax import lax
from jax.experimental import pallas as pl
from jax.experimental.pallas import tpu as pltpu
from jax.sharding import PartitionSpec as P

HEAD_DIM = 64
STATE = 64
SPAN = 128
PAD = 16
GROUP = 32
TAPS = 4
EPS = 1e-05
LOG2E = float(np.log2(np.e))
BF = jnp.bfloat16
F32 = jnp.float32


def dot(a, b):
    return jnp.dot(a, b, preferred_element_type=F32)


def dot_nt(a, b):
    return lax.dot_general(a, b, (((1,), (1,)), ((), ())), preferred_element_type=F32)


def dot_tn(a, b):
    return lax.dot_general(a, b, (((0,), (0,)), ((), ())), preferred_element_type=F32)


def fine_nt(a, b):
    return lax.dot_general(
        a, b, (((1,), (1,)), ((), ())), precision=lax.Precision.HIGHEST, preferred_element_type=F32
    )


def sigmoid(v):
    return 0.5 + 0.5 * jnp.tanh(0.5 * v)


def lanes_of(rows):
    return lax.broadcasted_iota(jnp.int32, (rows, 128), 1)


def shifted(ext, offset, rows):
    return ext[offset : offset + rows]


def full(shape):
    rank = len(shape)
    return pl.BlockSpec(shape, lambda i: (0,) * rank)


SMEM = pl.BlockSpec(memory_space=pltpu.SMEM)


def expanders(heads):
    channel = np.arange(heads * HEAD_DIM) // HEAD_DIM
    lane = np.arange(128)[:, None]
    return [np.asarray(lane == GROUP * g + channel[None], np.float32) for g in range(4)]


def project_kernel(fresh, final, tile, chunk, *refs):
    refs = list(refs)

    def take(count):
        return [refs.pop(0) for _ in range(count)]

    sc, tokens_r, halo, edge, wg, wv, wst, cv, bias, nal, tri, e0, e1 = take(13)
    if fresh:
        gain, ws, cs = take(3)
    else:
        (bc_r,) = take(1)
    gate_o, v_o, xpre_o, ff_o, sb_o, pb_o, sft_o, sbt_o, pft_o, pbt_o, hand_o, vh_o = take(12)
    if fresh:
        normed_o, nedge_o, ps_o, pspre_o, bc_o, psh_o = take(6)
    if final:
        col_o, row_o = take(2)
    sb_s, pb_s, sf_s, pf_s = take(4)

    step = pl.program_id(0)
    tiles = pl.num_programs(0)
    at = tiles - 1 - step
    length = sc[1]
    start = sc[0] + at * tile
    width = e0.shape[1]
    blocks = tile // SPAN

    @pl.when(step == 0)
    def _():
        sb_s[...] = jnp.zeros_like(sb_s)
        sf_s[...] = jnp.zeros_like(sf_s)
        pb_s[...] = jnp.ones_like(pb_s)
        pf_s[...] = jnp.ones_like(pf_s)

    before = jnp.where(at == 0, edge[...].astype(F32), halo[...].astype(F32))
    rows = jnp.concatenate([before, tokens_r[...].astype(F32)], axis=0)
    keep = jnp.where(lax.rem(start, length) == 0, 0.0, 1.0)
    row_id = lax.broadcasted_iota(jnp.int32, (tile + PAD, 1), 0)
    keep_rows = jnp.where(row_id < PAD, keep, 1.0)
    if fresh:
        scale = lax.rsqrt(jnp.mean(rows * rows, axis=1, keepdims=True) + EPS)
        normed = (rows * scale * gain[...]).astype(BF)
        own = normed[PAD:]
        normed_o[...] = own

        ps = dot(normed, ws[...]) * keep_rows
        ps_o[...] = ps[PAD:]
        pspre = ps[PAD:] * cs[TAPS - 1 : TAPS]
        for j in range(1, TAPS):
            pspre = pspre + shifted(ps, PAD - j, tile) * cs[TAPS - 1 - j : TAPS - j]
        pspre_o[...] = pspre
        bc = pspre * sigmoid(pspre)
        bc_o[...] = bc

        @pl.when(at == 0)
        def _():
            nedge_o[...] = normed[:PAD]
            psh_o[...] = ps[:PAD]

    else:
        normed = rows.astype(BF)
        own = tokens_r[...]
        bc = bc_r[...]

    z = dot(own, wst[...]) + bias[...]
    dt = jnp.maximum(z, 0.0) + jnp.log1p(jnp.exp(-jnp.abs(z)))
    a2 = dt * nal[...]
    lane = lanes_of(SPAN)
    if final:
        sig = sigmoid(z)
    wmix, bts = [], []
    for b in range(blocks):
        sl = slice(b * SPAN, (b + 1) * SPAN)
        ab = a2[sl]
        ca = jnp.dot(tri[...], ab, precision=lax.Precision.HIGHEST, preferred_element_type=F32)
        ce = ca - ab
        if final:
            col = jnp.where(
                lane < 32, ca, jnp.where(lane < 64, ce, jnp.where(lane < 96, dt[sl], sig[sl]))
            )
            col_o[sl, :] = col
            row_o[sl, :] = jnp.transpose(col)
        end = ca[SPAN - 1 : SPAN]
        w = jnp.exp2(jnp.where(lane < 32, end - ca, ce)) * dt[sl]
        dec = jnp.broadcast_to(jnp.exp2(end), (8, 128))
        high = dec.astype(BF).astype(F32)
        wmix.append(jnp.concatenate([w, high, dec - high], axis=0).astype(BF))
        bts.append(jnp.transpose(bc[sl])[:STATE].astype(BF))

    for c in range(width // chunk):
        cl = slice(c * chunk, (c + 1) * chunk)
        gate_o[:, cl] = dot(own, wg[:, cl]).astype(BF)
        v = dot(normed, wv[:, cl]) * keep_rows
        v_o[:, cl] = v[PAD:].astype(BF)

        @pl.when(at == 0)
        def _():
            vh_o[:, cl] = v[:PAD]

        xpre = v[PAD:] * cv[TAPS - 1 : TAPS, cl]
        for j in range(1, TAPS):
            xpre = xpre + shifted(v, PAD - j, tile) * cv[TAPS - 1 - j : TAPS - j, cl]
        xpre_o[:, cl] = xpre.astype(BF)
        x = xpre * sigmoid(xpre)
        for b in reversed(range(blocks)):
            sl = slice(b * SPAN, (b + 1) * SPAN)
            we = dot(wmix[b], e0[:, cl])
            wbe = dot(wmix[b][:SPAN], e1[:, cl])
            dec = we[SPAN : SPAN + 1] + we[SPAN + 8 : SPAN + 9]
            xb = x[sl]
            fresh_f = dot(bts[b], (xb * we[:SPAN]).astype(BF))
            fresh_b = dot(bts[b], (xb * wbe).astype(BF))
            place = start + b * SPAN
            first = jnp.where(lax.rem(place, length) == 0, 0.0, 1.0)
            last = jnp.where(lax.rem(place + SPAN, length) == 0, 0.0, 1.0)
            ff_o[b, :, cl] = fresh_f.astype(BF)
            pf = pf_s[0:1, cl]
            sf_s[:, cl] = sf_s[:, cl] + pf * fresh_f
            pf_s[:, cl] = jnp.broadcast_to(pf * dec * first, (8, chunk))
            held = sb_s[:, cl] * last
            pb = pb_s[0:1, cl] * last
            sb_o[b, :, cl] = held.astype(BF)
            pb_o[b, :, cl] = jnp.broadcast_to(pb, (8, chunk))
            sb_s[:, cl] = held * dec + fresh_b
            pb_s[:, cl] = jnp.broadcast_to(pb * dec, (8, chunk))

    @pl.when(at == 0)
    def _():
        sft_o[...] = sf_s[...]
        sbt_o[...] = sb_s[...]
        pft_o[...] = pf_s[...]
        pbt_o[...] = pb_s[...]
        hand_o[...] = jnp.where(sc[0] == 0, sf_s[...], sb_s[...]).astype(BF)


def project(sc, source, edge, wg, wv, wst, cv, bias, nal, e0, e1, maps=None, bc=None, final=True):
    fresh = maps is not None
    tokens, width_in = source.shape
    width = wg.shape[1]
    tile = min(256, tokens)
    tiles = tokens // tile
    per = tile // SPAN
    blocks = tokens // SPAN
    chunk = 256 if width % 256 == 0 else 128
    tri = np.tril(np.ones((SPAN, SPAN), np.float32))

    def back(shape):
        rank = len(shape)
        return pl.BlockSpec(shape, lambda i: (tiles - 1 - i,) + (0,) * (rank - 1))

    sds = jax.ShapeDtypeStruct
    wide = (sds((tokens, width), BF), back((tile, width)))
    narrow = (sds((tokens, 128), F32), back((tile, 128)))
    held = (sds((blocks, STATE, width), BF), back((per, STATE, width)))
    total = (sds((STATE, width), F32), full((STATE, width)))
    passed = (sds((8, width), F32), full((8, width)))
    outs = [wide, wide, wide, held, held, (sds((blocks, 8, width), F32), back((per, 8, width)))]
    outs += [total, total, passed, passed, (sds((STATE, width), BF), full((STATE, width)))]
    outs += [(sds((PAD, width), F32), full((PAD, width)))]
    if fresh:
        outs += [
            (sds((tokens, width_in), BF), back((tile, width_in))),
            (sds((PAD, width_in), BF), full((PAD, width_in))),
            narrow,
            narrow,
            narrow,
            (sds((PAD, 128), F32), full((PAD, 128))),
        ]
    if final:
        outs += [narrow, narrow]
    steps = tile // PAD
    args = [sc, source, source, edge, wg, wv, wst, cv, bias, nal, tri, e0, e1]
    in_specs = [
        SMEM,
        back((tile, width_in)),
        pl.BlockSpec((PAD, width_in), lambda i: (jnp.maximum((tiles - 1 - i) * steps - 1, 0), 0)),
    ] + [full(a.shape) for a in args[3:]]
    if fresh:
        args += list(maps)
        in_specs += [full(a.shape) for a in maps]
    else:
        args += [bc]
        in_specs += [back((tile, 128))]
    return pl.pallas_call(
        functools.partial(project_kernel, fresh, final, tile, chunk),
        grid=(tiles,),
        in_specs=in_specs,
        out_specs=[spec for _, spec in outs],
        out_shape=[shape for shape, _ in outs],
        scratch_shapes=[
            pltpu.VMEM((STATE, width), F32),
            pltpu.VMEM((8, width), F32),
            pltpu.VMEM((STATE, width), F32),
            pltpu.VMEM((8, width), F32),
        ],
        compiler_params=pltpu.CompilerParams(vmem_limit_bytes=58 * 1024 * 1024),
        name="project",
    )(*args)


def split_refs(refs, groups, kinds):
    taken = [[refs.pop(0) for _ in range(groups)] for _ in range(kinds)]
    return [functools.partial(pick, refs_of) for refs_of in taken]


def pick(refs_of, p):
    per = refs_of[0].shape[-1] // 128
    return refs_of[p // per], slice((p % per) * 128, (p % per + 1) * 128)


def mix_kernel(groups, *refs):
    refs = list(refs)
    sc = refs.pop(0)
    gates, xpres, ffs, sbls, pbs, sfds, sbds = split_refs(refs, groups, 7)
    mix_body(sc, gates, xpres, ffs, sbls, pbs, sfds, sbds, *refs)


def mix_body(
    sc, gates, xpres, ffs, sbls, pbs, sfds, sbds,
    bc_r, col_r, row_r, hid, gout, ow, owt, ggain, skip, e0, e1, e2,
    out_o, gnorm_o, dy_o, dgate_o, sf_o, sb_o, gbl_o, pg_o, dff_o,
    gft_o, gbt_o, pgf_o, pgb_o, hand_o, ggain_o, skip_o,
    sf_s, gb_s, gf_s, pg_s, q_s, y_s, dgn_s, exp_s,
):
    i = pl.program_id(0)
    length = sc[1]
    place = sc[0] + i * SPAN
    first = jnp.where(lax.rem(place, length) == 0, 0.0, 1.0)
    last = jnp.where(lax.rem(place + SPAN, length) == 0, 0.0, 1.0)
    live = jnp.where(lax.div(place, length) < sc[2], 1.0, 0.0)
    width = e0.shape[1]
    pairs = width // 128

    @pl.when(i == 0)
    def _():
        enters_f = jnp.where(sc[3] == 1, 1.0, 0.0)
        for p in range(pairs):
            ref, at = sfds(p)
            sf_s[:, p * 128 : (p + 1) * 128] = ref[:, at].astype(F32) * enters_f
        gb_s[...] = jnp.zeros_like(gb_s)
        gf_s[...] = jnp.zeros_like(gf_s)
        pg_s[...] = jnp.ones_like(pg_s)
        q_s[...] = jnp.ones_like(q_s)
        ggain_o[...] = jnp.zeros_like(ggain_o)
        skip_o[...] = jnp.zeros_like(skip_o)

    enters_b = jnp.where(sc[4] == 1, 1.0, 0.0)
    glow = gout[...].astype(F32) * live
    gl = glow.astype(BF)
    dgn_s[...] = dot(gl, owt[...])

    lane = lanes_of(SPAN)
    low_half = lane < HEAD_DIM
    col = col_r[...]
    row = row_r[...]
    end = jnp.broadcast_to(col[SPAN - 1 : SPAN], (8, 128))
    end1 = pltpu.roll(end, GROUP, 1)
    w = jnp.where(lane < 64, jnp.exp2(jnp.where(lane < 32, col, end1[0:1] - col)), col)
    dec = jnp.exp2(end)
    high = dec.astype(BF).astype(F32)
    wmix = jnp.concatenate([w, high, dec - high], axis=0).astype(BF)
    wtok = wmix[:SPAN]
    bc = bc_r[...]
    bmf, cmf = bc[:, :STATE], bc[:, STATE:]
    cm = cmf.astype(BF)
    ct = jnp.transpose(bc)[STATE:].astype(BF)
    square_r = lax.broadcasted_iota(jnp.int32, (SPAN, SPAN), 0)
    aff = jnp.where(square_r == lane, 0.0, fine_nt(cmf, bmf))

    squares = jnp.zeros((SPAN, 128), F32)
    for p in range(pairs):
        sl = slice(p * 128, (p + 1) * 128)
        efd = dot(wmix, e0[:, sl])
        ef = efd[:SPAN]
        eb = dot(wtok, e1[:, sl])
        dte = dot(wtok, e2[:, sl])
        exp_s[0, :, sl] = ef
        exp_s[1, :, sl] = eb
        decay = efd[SPAN : SPAN + 1] + efd[SPAN + 8 : SPAN + 9]
        exp_s[2, 0:8, sl] = jnp.broadcast_to(decay, (8, 128))
        sf = sf_s[:, sl] * first
        sfb = sf.astype(BF)
        sf_o[0, :, sl] = sfb
        sbl, at = sbls(p)
        pb, sbd, ff, xpre, gate = (r(p)[0] for r in (pbs, sbds, ffs, xpres, gates))
        arrived = sbd[:, at].astype(F32) * enters_b
        sb = (sbl[0, :, at].astype(F32) + pb[0, 0:1, at] * arrived) * last
        sbb = sb.astype(BF)
        sb_o[0, :, sl] = sbb
        sf_s[:, sl] = sf * decay + ff[0, :, at].astype(F32)
        xp = xpre[:, at].astype(F32)
        x = xp * sigmoid(xp)
        xd = x * dte
        bd = jnp.concatenate(
            [jnp.where(low_half, xd, 0.0), jnp.where(low_half, 0.0, xd)], axis=0
        ).astype(BF)
        ms = []
        for h in (2 * p, 2 * p + 1):
            spread = jnp.minimum(
                col[:, h : h + 1] - row[h : h + 1, :],
                row[GROUP + h : GROUP + h + 1, :] - col[:, GROUP + h : GROUP + h + 1],
            )
            ms.append((aff * jnp.exp2(spread)).astype(BF))
        y = dot(jnp.concatenate(ms, axis=1), bd)
        y = y + ef * dot(cm, sfb) + eb * dot(cm, sbb) + skip[:, sl] * x
        y_s[:, sl] = y
        g = gate[:, at].astype(F32)
        gated = y * (g * sigmoid(g))
        squares = squares + gated * gated

    gsc = lax.rsqrt(jnp.sum(squares, axis=1, keepdims=True) * (1.0 / width) + EPS)
    inner = jnp.zeros((SPAN, 128), F32)
    for p in range(pairs):
        sl = slice(p * 128, (p + 1) * 128)
        gate, at = gates(p)
        g = gate[:, at].astype(F32)
        gunit = y_s[:, sl] * (g * sigmoid(g)) * gsc
        gnorm_o[:, sl] = (gunit * ggain[:, sl]).astype(BF)
        dgn = dgn_s[:, sl]
        dgu = dgn * gunit
        ggain_o[:, sl] += jnp.sum(dgu, axis=0, keepdims=True)
        inner = inner + dgu * ggain[:, sl]
    mean = jnp.sum(inner, axis=1, keepdims=True) * (1.0 / width)
    out_o[...] = (hid[...].astype(F32) + live * dot(gnorm_o[...], ow[...])).astype(BF)

    for p in range(pairs):
        sl = slice(p * 128, (p + 1) * 128)
        gate, at = gates(p)
        g = gate[:, at].astype(F32)
        sg = sigmoid(g)
        act = g * sg
        y = y_s[:, sl]
        gunit = y * act * gsc
        dgated = gsc * (dgn_s[:, sl] * ggain[:, sl] - gunit * mean)
        dy = dgated * act
        dy_o[:, sl] = dy.astype(BF)
        dgate_o[:, sl] = (dgated * y * (sg * (1.0 + g * (1.0 - sg)))).astype(BF)
        xp = xpres(p)[0][:, at].astype(F32)
        skip_o[:, sl] += jnp.sum(dy * (xp * sigmoid(xp)), axis=0, keepdims=True)
        decay = exp_s[2, 0:1, sl]
        dff = dot(ct, (exp_s[0, :, sl] * dy).astype(BF))
        dfb = dot(ct, (exp_s[1, :, sl] * dy).astype(BF))
        dff_o[0, :, sl] = dff.astype(BF)
        q = q_s[0:1, sl]
        gf_s[:, sl] = gf_s[:, sl] + q * dff
        q_s[:, sl] = jnp.broadcast_to(q * decay * last, (8, 128))
        gb = gb_s[:, sl] * first
        pg = pg_s[0:1, sl] * first
        gbl_o[0, :, sl] = gb.astype(BF)
        pg_o[0, :, sl] = jnp.broadcast_to(pg, (8, 128))
        gb_s[:, sl] = gb * decay + dfb
        pg_s[:, sl] = jnp.broadcast_to(pg * decay, (8, 128))

    @pl.when(i == pl.num_programs(0) - 1)
    def _():
        gft_o[...] = gf_s[...]
        gbt_o[...] = gb_s[...]
        pgf_o[...] = q_s[...]
        pgb_o[...] = pg_s[...]
        hand_o[...] = jnp.where(sc[0] == 0, gb_s[...], gf_s[...]).astype(BF)


def mix(sc, split, bc, col, row, hidden, out_grad, ow, owt, ggain, skip, e0, e1, e2):
    tokens, width_in = hidden.shape
    groups = len(split[0])
    width = e0.shape[1]
    part = width // groups
    blocks = tokens // SPAN

    def ahead(shape):
        rank = len(shape)
        return pl.BlockSpec(shape, lambda i: (i,) + (0,) * (rank - 1))

    sds = jax.ShapeDtypeStruct
    state = (1, STATE, width)
    outs = [
        (sds((tokens, width_in), BF), ahead((SPAN, width_in))),
        (sds((tokens, width), BF), ahead((SPAN, width))),
        (sds((tokens, width), BF), ahead((SPAN, width))),
        (sds((tokens, width), BF), ahead((SPAN, width))),
        (sds((blocks, STATE, width), BF), ahead(state)),
        (sds((blocks, STATE, width), BF), ahead(state)),
        (sds((blocks, STATE, width), BF), ahead(state)),
        (sds((blocks, 8, width), F32), ahead((1, 8, width))),
        (sds((blocks, STATE, width), BF), ahead(state)),
        (sds((STATE, width), F32), full((STATE, width))),
        (sds((STATE, width), F32), full((STATE, width))),
        (sds((8, width), F32), full((8, width))),
        (sds((8, width), F32), full((8, width))),
        (sds((STATE, width), BF), full((STATE, width))),
        (sds((1, width), F32), full((1, width))),
        (sds((1, width), F32), full((1, width))),
    ]
    shared = [ow, owt, ggain, skip, e0, e1, e2]
    in_specs = [SMEM]
    for shape in (
        (SPAN, part), (SPAN, part), (1, STATE, part), (1, STATE, part), (1, 8, part),
    ):
        in_specs += [ahead(shape)] * groups
    in_specs += [full((STATE, part))] * (2 * groups)
    in_specs += [ahead((SPAN, 128))] * 3 + [ahead((SPAN, width_in))] * 2
    in_specs += [full(a.shape) for a in shared]
    return pl.pallas_call(
        functools.partial(mix_kernel, groups),
        grid=(blocks,),
        in_specs=in_specs,
        out_specs=[spec for _, spec in outs],
        out_shape=[shape for shape, _ in outs],
        scratch_shapes=[
            pltpu.VMEM((STATE, width), F32),
            pltpu.VMEM((STATE, width), F32),
            pltpu.VMEM((STATE, width), F32),
            pltpu.VMEM((8, width), F32),
            pltpu.VMEM((8, width), F32),
            pltpu.VMEM((SPAN, width), F32),
            pltpu.VMEM((SPAN, width), F32),
            pltpu.VMEM((3, SPAN, width), F32),
        ],
        compiler_params=pltpu.CompilerParams(vmem_limit_bytes=58 * 1024 * 1024),
        name="mix",
    )(sc, *[a for kind in split for a in kind], bc, col, row, hidden, out_grad, *shared)


def back_kernel(heads, groups, *refs):
    refs = list(refs)
    sc = refs.pop(0)
    xpres, vs, gfds, gbds = split_refs(refs, groups, 4)
    back_body(heads, sc, xpres, vs, gfds, gbds, *refs)


def back_body(
    heads, sc, xpres, vs, gfds, gbds,
    dy_r, bc_r, ps_r, pspre_r, col_r, row_r, sf_r, sb_r, gbl, pg, dff,
    skip, cv, cs, nad, e0, e1, e2, seg, tris, rect,
    dv_o, dst_o, dz_o, cvg_o, csg_o, head_o, edge_o, edges_o,
    gf_s, edge_s, edges_s, da_s,
):
    step = pl.program_id(0)
    blocks = pl.num_programs(0)
    i = blocks - 1 - step
    length = sc[1]
    place = sc[0] + i * SPAN
    last = jnp.where(lax.rem(place + SPAN, length) == 0, 0.0, 1.0)
    width = e0.shape[1]
    pairs = width // 128

    @pl.when(step == 0)
    def _():
        enters_f = jnp.where(sc[5] == 1, 1.0, 0.0)
        for p in range(pairs):
            ref, at = gfds(p)
            gf_s[:, p * 128 : (p + 1) * 128] = ref[:, at].astype(F32) * enters_f
        edge_s[...] = jnp.zeros_like(edge_s)
        edges_s[...] = jnp.zeros_like(edges_s)
        da_s[...] = jnp.zeros_like(da_s)
        cvg_o[...] = jnp.zeros_like(cvg_o)
        csg_o[...] = jnp.zeros_like(csg_o)
        head_o[...] = jnp.zeros_like(head_o)

    lane = lanes_of(SPAN)
    low_half = lane < HEAD_DIM
    col = col_r[...]
    row = row_r[...]
    end = jnp.broadcast_to(col[SPAN - 1 : SPAN], (8, 128))
    end1 = pltpu.roll(end, GROUP, 1)
    w = jnp.where(lane < 64, jnp.exp2(jnp.where(lane < 32, col, end1[0:1] - col)), col)
    dec = jnp.exp2(end)
    high = dec.astype(BF).astype(F32)
    wmix = jnp.concatenate([w, high, dec - high], axis=0).astype(BF)
    wtok = wmix[:SPAN]
    winn = jnp.exp2(jnp.where(lane < 32, end[0:1] - col, col)).astype(BF)
    bc = bc_r[...]
    bmf, cmf = bc[:, :STATE], bc[:, STATE:]
    bm, cm = bmf.astype(BF), cmf.astype(BF)
    enters_b = jnp.where(sc[6] == 1, 1.0, 0.0)
    square_r = lax.broadcasted_iota(jnp.int32, (SPAN, SPAN), 0)
    off = square_r != lane
    aff = jnp.where(off, fine_nt(bmf, cmf), 0.0)

    daff = jnp.zeros((SPAN, SPAN), F32)
    red = jnp.zeros((SPAN, 128), F32)
    ddt = jnp.zeros((SPAN, 128), F32)
    span_sum = jnp.zeros((8, 128), F32)
    dc = jnp.zeros((SPAN, STATE), F32)
    db = jnp.zeros((SPAN, STATE), F32)
    for p in range(pairs):
        sl = slice(p * 128, (p + 1) * 128)
        efd = dot(wmix, e0[:, sl])
        ef = efd[:SPAN]
        decay = efd[SPAN : SPAN + 1] + efd[SPAN + 8 : SPAN + 9]
        eb = dot(wtok, e1[:, sl])
        dte = dot(wtok, e2[:, sl])
        wf = dot(winn, e0[:, sl])
        wb = dot(winn, e1[:, sl])
        sf, sb = sf_r[0, :, sl], sb_r[0, :, sl]
        gf32 = gf_s[:, sl] * last
        gbd, at = gbds(p)
        arrived = gbd[:, at].astype(F32) * enters_b
        gb32 = gbl[0, :, sl].astype(F32) + pg[0, 0:1, sl] * arrived
        gf, gb = gf32.astype(BF), gb32.astype(BF)
        gf_s[:, sl] = gf32 * decay + dff[0, :, sl].astype(F32)
        cross = (sf.astype(F32) * gf32 + sb.astype(F32) * gb32) * decay
        crossed = jnp.broadcast_to(jnp.sum(cross, axis=0, keepdims=True), (8, 128))
        span_sum = span_sum + dot(crossed.astype(BF), seg[4, sl, :])
        xp = xpres(p)[0][:, at].astype(F32)
        sg = sigmoid(xp)
        x = xp * sg
        xd = x * dte
        dy = dy_r[:, sl].astype(F32)
        efdy, ebdy = ef * dy, eb * dy
        wfxd, wbxd = wf * xd, wb * xd
        cf = wf * dot(bm, gf)
        cb = wb * dot(bm, gb)
        dc = dc + dot_nt(efdy.astype(BF), sf) + dot_nt(ebdy.astype(BF), sb)
        db = db + dot_nt(wfxd.astype(BF), gf) + dot_nt(wbxd.astype(BF), gb)
        red = red + dot((efdy * dot(cm, sf)).astype(BF), seg[0, sl, :])
        red = red + dot((ebdy * dot(cm, sb)).astype(BF), seg[1, sl, :])
        red = red + dot((xd * cf).astype(BF), seg[2, sl, :])
        red = red + dot((xd * cb).astype(BF), seg[3, sl, :])
        bd = jnp.concatenate(
            [jnp.where(low_half, dy, 0.0), jnp.where(low_half, 0.0, dy)], axis=0
        ).astype(BF)
        dm = dot_nt(xd.astype(BF), bd)
        ms = []
        for k in range(2):
            h = 2 * p + k
            spread = jnp.minimum(
                row[h : h + 1, :] - col[:, h : h + 1],
                col[:, GROUP + h : GROUP + h + 1] - row[GROUP + h : GROUP + h + 1, :],
            )
            f = jnp.exp2(spread)
            m = aff * f
            ms.append(m.astype(BF))
            dmh = dm[:, k * 128 : (k + 1) * 128]
            daff = daff + f * dmh
            sums = dot((m * dmh).astype(BF), rect[...])
            inside = jnp.where(
                square_r < lane, sums[:, :SPAN], jnp.where(off, sums[:, SPAN:], 0.0)
            )
            da_s[h : h + 1, :] = jnp.sum(inside, axis=0, keepdims=True)
        dxd = dot(jnp.concatenate(ms, axis=1), bd) + cf + cb
        ddt = ddt + dot((x * dxd).astype(BF), seg[4, sl, :])
        dx = dte * dxd + skip[:, sl] * dy
        dxp = dx * (sg * (1.0 + xp * (1.0 - sg)))
        ext = jnp.concatenate([dxp, edge_s[:, sl] * last], axis=0)
        edge_s[:, sl] = dxp[:8]
        v = vs(p)[0][:, at].astype(F32)
        dv = jnp.zeros((SPAN, 128), F32)
        for j in range(TAPS):
            moved = shifted(ext, j, SPAN)
            k = TAPS - 1 - j
            dv = dv + moved * cv[k : k + 1, sl]
            cvg_o[k : k + 1, sl] += jnp.sum(v * moved, axis=0, keepdims=True)
        dv_o[:, sl] = dv.astype(BF)

    dafb = jnp.where(off, daff, 0.0).astype(BF)
    db = db + dot(dafb, cm)
    dc = dc + dot_tn(dafb, bm)
    dbc = jnp.concatenate([db, dc], axis=1)
    pp = pspre_r[...]
    sp = sigmoid(pp)
    dpp = dbc * (sp * (1.0 + pp * (1.0 - sp)))
    ext = jnp.concatenate([dpp, edges_s[...] * last], axis=0)
    edges_s[...] = dpp[:8]
    ps = ps_r[...]
    dst = jnp.zeros((SPAN, 128), F32)
    for j in range(TAPS):
        moved = shifted(ext, j, SPAN)
        k = TAPS - 1 - j
        dst = dst + moved * cs[k : k + 1, :]
        csg_o[k : k + 1, :] += jnp.sum(ps * moved, axis=0, keepdims=True)
    dst_o[...] = dst.astype(BF)

    hi = red.astype(BF)
    lo = (red - hi.astype(F32)).astype(BF)
    summed = dot(tris[...], hi) + dot(tris[...], lo)
    parts = [summed[g * SPAN : (g + 1) * SPAN] for g in range(4)]
    picked = jnp.where(
        lane < 32, parts[0], jnp.where(lane < 64, parts[1], jnp.where(lane < 96, parts[2], parts[3]))
    )
    picked = picked + jnp.transpose(da_s[...])
    total = picked + pltpu.roll(picked, 64, 1)
    total = total + pltpu.roll(total, 32, 1)
    da = total + span_sum[0:1]
    dz = (ddt + da * nad[...]) * col
    dz = jnp.where((lane >= 96) & (lane < 96 + heads), dz, 0.0)
    dz_o[...] = dz.astype(BF)
    head_o[0:1, :] += jnp.sum(da * col * nad[...], axis=0, keepdims=True)
    head_o[1:2, :] += jnp.sum(dz, axis=0, keepdims=True)

    @pl.when(i == 0)
    def _():
        edge_o[...] = edge_s[...]
        edges_o[...] = edges_s[...]


def back(heads, sc, split, dy, bc, ps, pspre, col, row, sf, sb, gbl, pg, dff, skip, cv, cs, nad):
    tokens, width = dy.shape
    groups = len(split[0])
    part = width // groups
    blocks = tokens // SPAN
    maps = expanders(heads)
    every = sum(maps)
    seg = np.stack([m.T for m in maps] + [every.T])
    at = np.arange(SPAN)
    row_at, col_at = at[:, None], at[None, :]
    tris = np.concatenate(
        [col_at >= row_at, col_at <= row_at, col_at < row_at, col_at > row_at], axis=0
    ).astype(np.float32)
    rect = np.concatenate([row_at >= col_at, row_at <= col_at], axis=1).astype(np.float32)

    def rev(shape):
        rank = len(shape)
        return pl.BlockSpec(shape, lambda i: (blocks - 1 - i,) + (0,) * (rank - 1))

    sds = jax.ShapeDtypeStruct
    state = (1, STATE, width)
    outs = [
        (sds((tokens, width), BF), rev((SPAN, width))),
        (sds((tokens, 128), BF), rev((SPAN, 128))),
        (sds((tokens, 128), BF), rev((SPAN, 128))),
        (sds((TAPS, width), F32), full((TAPS, width))),
        (sds((TAPS, 128), F32), full((TAPS, 128))),
        (sds((8, 128), F32), full((8, 128))),
        (sds((8, width), F32), full((8, width))),
        (sds((8, 128), F32), full((8, 128))),
    ]
    shared = [skip, cv, cs, nad]
    shared += [jnp.asarray(m, BF) for m in (*maps[:3], seg, tris, rect)]
    in_specs = [SMEM] + [rev((SPAN, part))] * (2 * groups)
    in_specs += [full((STATE, part))] * (2 * groups)
    in_specs += [rev((SPAN, width))] + [rev((SPAN, 128))] * 5
    in_specs += [rev(state)] * 3 + [rev((1, 8, width)), rev(state)]
    in_specs += [full(a.shape) for a in shared]
    return pl.pallas_call(
        functools.partial(back_kernel, heads, groups),
        grid=(blocks,),
        in_specs=in_specs,
        out_specs=[spec for _, spec in outs],
        out_shape=[shape for shape, _ in outs],
        scratch_shapes=[
            pltpu.VMEM((STATE, width), F32),
            pltpu.VMEM((8, width), F32),
            pltpu.VMEM((8, 128), F32),
            pltpu.VMEM((128, 128), F32),
        ],
        compiler_params=pltpu.CompilerParams(vmem_limit_bytes=58 * 1024 * 1024),
        name="back",
    )(
        sc, *[a for kind in split for a in kind],
        dy, bc, ps, pspre, col, row, sf, sb, gbl, pg, dff, *shared,
    )


def reduce_kernel(bits, lanes, mats, *refs):
    n_mats = len(mats)
    srcs, both, tiny = refs[:n_mats], refs[n_mats], refs[n_mats + 1]
    outs = refs[n_mats + 2 : 2 * n_mats + 2]
    both_o, tiny_o = refs[2 * n_mats + 2], refs[2 * n_mats + 3]
    scratch = refs[2 * n_mats + 4 :]
    own_r, sent = scratch[0], scratch[1]
    halves, parts = scratch[2 : 2 + bits], scratch[2 + bits : 1 + 2 * bits]
    tiny_r, tiny_s, send_s, recv_s, tsend_s, trecv_s = scratch[1 + 2 * bits :]
    rows = srcs[0].shape[0] if mats[0] == "cols" else srcs[0].shape[0] // 2
    width = outs[0].shape[1]
    me = lax.axis_index("dp")
    chan = lax.axis_index("chan")
    bit = [lax.rem(lax.div(me, 2**k), 2) for k in range(bits)]
    partner = [{"dp": me + (1 - 2 * bit[k]) * 2**k} for k in range(bits)]
    across = {"chan": 1 - chan}
    stages = [partner[0], across] + partner[1:]

    barrier = pltpu.get_barrier_semaphore()
    for device in stages:
        pl.semaphore_signal(barrier, inc=1, device_id=device, device_id_type=pl.DeviceIdType.MESH)
    pl.semaphore_wait(barrier, bits + 1)

    chunks = [(m, s) for m in range(n_mats) for s in range(0, width, lanes)]
    extra = len(chunks)
    n = extra + 1
    half = rows // 2

    def mult(v):
        return pl.multiple_of(v, 16)

    def source(c, which, part):
        if c == extra:
            return both.at[pl.ds(mult(part * half), half), :]
        m, s = chunks[c]
        if mats[m] == "cols":
            return srcs[m].at[pl.ds(mult(part * half), half), pl.ds(which * width + s, lanes)]
        return srcs[m].at[pl.ds(mult(which * rows + part * half), half), pl.ds(s, lanes)]

    def target(c, start, size):
        if c == extra:
            return both_o.at[pl.ds(mult(start), size), :]
        m, s = chunks[c]
        return outs[m].at[pl.ds(mult(start), size), pl.ds(s, lanes)]

    def copy(src, dst, c, k, device):
        return pltpu.make_async_remote_copy(
            src_ref=src,
            dst_ref=dst,
            send_sem=send_s.at[c, k],
            recv_sem=recv_s.at[c, k],
            device_id=device,
            device_id_type=pl.DeviceIdType.MESH,
        )

    offset = [bit[0] * half]
    for k in range(1, bits):
        offset.append(offset[-1] + bit[k] * (half >> k))

    def first(c, which):
        if c == extra and which == 0:
            return None
        slot = own_r.at[c, which]
        return copy(source(c, which, 1 - bit[0]), slot, c, which, partner[0])

    def second(c):
        return copy(sent.at[c], halves[0].at[c], c, 2, across)

    def halving(c, k):
        size = half >> k
        src = parts[k - 1].at[c, pl.ds(mult((1 - bit[k]) * size), size), :]
        return copy(src, halves[k].at[c], c, 2 + k, partner[k])

    def doubling(c, k):
        size = half >> k
        place = target(c, offset[k], size)
        return copy(place, place, c, 2 + bits + k, partner[k])

    def f32(ref):
        return ref[...].astype(F32)

    def stage(c, s):
        if s == 0:
            for which in (0, 1):
                rdma = first(c, which)
                if rdma is not None:
                    rdma.start()
        elif s == 1:
            first(c, 1).wait_recv()
            sent[c] = (f32(source(c, 1, bit[0])) + f32(own_r.at[c, 1])).astype(BF)
            second(c).start()
        elif s == 2:
            second(c).wait_recv()
            if c == extra:
                total = f32(sent.at[c]) + f32(halves[0].at[c])
            else:
                first(c, 0).wait_recv()
                total = f32(source(c, 0, bit[0])) + f32(own_r.at[c, 0]) + f32(halves[0].at[c])
            parts[0][c] = total.astype(BF)
            halving(c, 1).start()
        elif s < bits + 2:
            k = s - 2
            size = half >> k
            halving(c, k).wait_recv()
            kept = parts[k - 1].at[c, pl.ds(mult(bit[k] * size), size), :]
            total = (f32(kept) + f32(halves[k].at[c])).astype(BF)
            if k < bits - 1:
                parts[k][c] = total
                halving(c, k + 1).start()
            else:
                target(c, offset[k], size)[...] = total
                doubling(c, k).start()
        else:
            k = 2 * bits + 1 - s
            doubling(c, k).wait_recv()
            if k > 0:
                doubling(c, k - 1).start()

    def tiny_copy(k):
        return pltpu.make_async_remote_copy(
            src_ref=tiny if k == 0 else tiny_s.at[k - 1],
            dst_ref=tiny_r.at[k],
            send_sem=tsend_s.at[k],
            recv_sem=trecv_s.at[k],
            device_id=stages[k],
            device_id_type=pl.DeviceIdType.MESH,
        )

    tiny_copy(0).start()
    last = 2 * bits + 1
    for tick in range(n + last):
        for s in range(last, -1, -1):
            c = tick - s
            if 0 <= c < n:
                stage(c, s)
        if 1 <= tick <= bits + 1:
            k = tick - 1
            tiny_copy(k).wait_recv()
            before = tiny[...] if k == 0 else tiny_s[k - 1]
            total = before + tiny_r[k]
            if k < bits:
                tiny_s[k] = total
                tiny_copy(k + 1).start()
            else:
                tiny_o[...] = total

    for c in range(n):
        for which in (0, 1):
            rdma = first(c, which)
            if rdma is not None:
                rdma.wait_send()
        second(c).wait_send()
        for k in range(1, bits):
            halving(c, k).wait_send()
        for k in range(bits):
            doubling(c, k).wait_send()
    for k in range(bits + 1):
        tiny_copy(k).wait_send()


def reduce_all(bits, mats, both, tiny, lanes):
    kinds = [kind for _, kind in mats]
    arrays = [a for a, _ in mats]
    rows = arrays[0].shape[0] if kinds[0] == "cols" else arrays[0].shape[0] // 2
    width = arrays[0].shape[1] // 2 if kinds[0] == "cols" else arrays[0].shape[1]
    half = rows // 2
    n = len(arrays) * (width // lanes) + 1
    vmem = pl.BlockSpec(memory_space=pltpu.VMEM)
    sds = jax.ShapeDtypeStruct
    scratch = [pltpu.VMEM((n, 2, half, lanes), BF), pltpu.VMEM((n, half, lanes), BF)]
    scratch += [pltpu.VMEM((n, half >> k, lanes), BF) for k in range(bits)]
    scratch += [pltpu.VMEM((n, half >> k, lanes), BF) for k in range(bits - 1)]
    scratch += [
        pltpu.VMEM((bits + 1,) + tiny.shape, F32),
        pltpu.VMEM((bits,) + tiny.shape, F32),
        pltpu.SemaphoreType.DMA((n, 2 + 2 * bits)),
        pltpu.SemaphoreType.DMA((n, 2 + 2 * bits)),
        pltpu.SemaphoreType.DMA((bits + 1,)),
        pltpu.SemaphoreType.DMA((bits + 1,)),
    ]
    return pl.pallas_call(
        functools.partial(reduce_kernel, bits, lanes, kinds),
        out_shape=[sds((rows, width), BF)] * len(arrays)
        + [sds(both.shape, BF), sds(tiny.shape, F32)],
        in_specs=[vmem] * (len(arrays) + 2),
        out_specs=[vmem] * (len(arrays) + 2),
        scratch_shapes=scratch,
        compiler_params=pltpu.CompilerParams(
            collective_id=0, has_side_effects=True, vmem_limit_bytes=58 * 1024 * 1024
        ),
        name="reduce_all",
    )(*arrays, both, tiny)


def spread_heads(v):
    padded = jnp.zeros((GROUP,), F32).at[: v.shape[0]].set(v)
    return jnp.tile(padded, 4)[None]


def handed(total, passed, shards, up):
    pairs = [(k, k + 1) if up else (k + 1, k) for k in range(shards - 1)]
    entering = lax.ppermute(total.astype(BF), "chan", pairs)
    for _ in range(shards - 2):
        now = total + passed[0:1] * entering.astype(F32)
        entering = lax.ppermute(now.astype(BF), "chan", pairs)
    return entering


def swap(v):
    return lax.ppermute(v, "chan", [(0, 1), (1, 0)])


def core_swap(v):
    size = lax.axis_size("dp")
    return lax.ppermute(v, "dp", [(k, k ^ 1) for k in range(size)])


def on_device(
    hidden_in, norm_gain, gate_value_weight, state_weight, step_weight, value_conv, state_conv,
    step_bias, decay_log, skip_gain, gate_gain, out_weight, seq_length, seq_count, out_grad,
):
    tokens, width_in = hidden_in.shape
    channel = lax.axis_index("chan")
    shards = lax.axis_size("chan")
    groups_dp = lax.axis_size("dp")
    length, count = seq_length[0], seq_count[0]
    local_heads = gate_value_weight.shape[1]
    local = local_heads * HEAD_DIM
    heads = local_heads * shards
    width = heads * HEAD_DIM
    paired = shards == 2 and local % 128 == 0 and groups_dp % 2 == 0
    one = jnp.ones((), jnp.int32)
    flags = [channel, 1 - channel, 1 - channel, channel] if paired else [one] * 4
    sc = jnp.stack([channel * tokens, length, count] + flags).astype(jnp.int32)
    ups = [(k, k + 1) for k in range(shards - 1)]
    downs = [(k + 1, k) for k in range(shards - 1)]
    gain = norm_gain[None]

    wg = gate_value_weight[:, :, :HEAD_DIM].reshape(width_in, local)
    wv = gate_value_weight[:, :, HEAD_DIM:].reshape(width_in, local)
    edge = lax.ppermute(hidden_in[tokens - PAD :], "chan", ups)
    vec = jnp.concatenate([step_bias, decay_log, skip_gain])
    small = jnp.concatenate(
        [
            value_conv,
            gate_gain[None],
            jnp.pad(vec, (0, local - 3 * local_heads))[None],
        ]
    )

    def step_matrix(steps):
        return jnp.tile(jnp.pad(steps, ((0, 0), (0, GROUP - steps.shape[1]))), (1, 4))

    e0, e1, e2, _ = [jnp.asarray(e, BF) for e in expanders(heads)]
    maps = (gain, state_weight, state_conv)
    if paired:
        first_core = lax.axis_index("dp") % 2 == 0
        come = swap(jnp.where(first_core, wg, wv))
        small_b = swap(small)
        wstep = jnp.concatenate([step_weight, swap(step_weight)], axis=1)
        ow_b = swap(out_weight)
        also = core_swap(come)
        wgs = [wg, jnp.where(first_core, come, also)]
        wvs = [wv, jnp.where(first_core, also, come)]
        smalls = [small, small_b]
        ow = jnp.concatenate([out_weight, ow_b], axis=0)
    else:
        wgs = [lax.all_gather(wg, "chan", axis=1, tiled=True)]
        wvs = [lax.all_gather(wv, "chan", axis=1, tiled=True)]
        gathered = lax.all_gather(small, "chan", axis=0)
        wstep = lax.all_gather(step_weight, "chan", axis=1, tiled=True)
        smalls = [gathered[k] for k in range(shards)]
        ow = lax.all_gather(out_weight, "chan", axis=0, tiled=True)

    def heads_row(k, parts):
        lo, hi = k * local_heads, (k + 1) * local_heads
        return jnp.concatenate([p[TAPS + 1, lo:hi] for p in parts])

    bias_all, dlog_all, skip_all = (heads_row(k, smalls) for k in range(3))
    cv = jnp.concatenate([p[:TAPS] for p in smalls], axis=1)
    ggain = jnp.concatenate([p[TAPS : TAPS + 1] for p in smalls], axis=1)
    skip = jnp.repeat(skip_all, HEAD_DIM)[None]
    nad = -jnp.exp(dlog_all)

    if paired:
        gate, v, xpre, ff, sbl, pb, _, _, _, _, hand, vh, normed, nedge, ps, pspre, bc, psh = project(
            sc, hidden_in, edge, wg, wv, step_matrix(step_weight), value_conv,
            spread_heads(step_bias), spread_heads(-jnp.exp(decay_log) * LOG2E),
            e0[:, :local], e1[:, :local], maps=maps, final=False,
        )
        enter_b = swap(hand)
        gate2, v2, xpre2, ff2, sbl2, pb2, _, _, _, _, hand2, vh2, col, row = project(
            sc, normed, nedge, wgs[1], wvs[1], step_matrix(wstep), smalls[1][:TAPS],
            spread_heads(bias_all), spread_heads(nad * LOG2E),
            e0[:, local:], e1[:, local:], bc=bc, final=True,
        )
        enter = [swap(hand2), enter_b]
        split = [[gate, gate2], [xpre, xpre2], [ff, ff2], [sbl, sbl2], [pb, pb2], enter, enter]
        vs, xs = [v, v2], [xpre, xpre2]
        vh = jnp.concatenate([vh, vh2], axis=1)
    else:
        (
            gate, v, xpre, ff, sbl, pb, sft, sbt, pft, pbt, _, vh, normed, nedge, ps, pspre, bc, psh,
            col, row,
        ) = project(
            sc, hidden_in, edge, wgs[0], wvs[0], step_matrix(wstep), cv, spread_heads(bias_all),
            spread_heads(nad * LOG2E), e0, e1, maps=maps,
        )
        sfd = handed(sft, pft, shards, True)
        sbd = handed(sbt, pbt, shards, False)
        split = [[gate], [xpre], [ff], [sbl], [pb], [sfd], [sbd]]
        vs, xs = [v], [xpre]
    (
        output, gnorm, dy, dgate, sf, sb, gbl, pg, dff, gft, gbt, pgf, pgb, hand, ggain_grad, skip_grad,
    ) = mix(sc, split, bc, col, row, hidden_in, out_grad, ow, ow.T, ggain, skip, e0, e1, e2)
    if paired:
        enter = swap(hand)
        enter = [enter[:, local:], enter[:, :local]]
        gfds = gbds = enter
    else:
        gfds = [handed(gft, pgf, shards, False)]
        gbds = [handed(gbt, pgb, shards, True)]

    own_ids = channel * tokens + jnp.arange(tokens, dtype=jnp.int32)
    live = jnp.where(own_ids // length < count, 1.0, 0.0)[:, None].astype(BF)
    ow_grad = dot_tn(gnorm, out_grad * live).astype(BF)
    dwg = dot_tn(normed, dgate).astype(BF)

    dv, dst, dz, cvg, csg, head_sums, edge_g, edges_g = back(
        heads, sc, [xs, vs, gfds, gbds], dy, bc, ps, pspre, col, row, sf, sb, gbl, pg, dff, skip, cv,
        state_conv, spread_heads(nad),
    )

    if paired:
        turned = jnp.concatenate([edge_g[:, local:], edge_g[:, :local]], axis=1)
    else:
        turned = edge_g
    kernel = jnp.concatenate([cv, state_conv], axis=1)
    past = jnp.concatenate([vh, psh], axis=1)
    reach = TAPS - 1
    after = lax.ppermute(jnp.concatenate([turned, edges_g], axis=1), "chan", downs)[:reach]
    joined = jnp.concatenate([edge_g, edges_g], axis=1)
    after = after * jnp.where(((channel + 1) * tokens) % length == 0, 0.0, 1.0)
    patch = jnp.zeros((reach, joined.shape[1]), F32)
    taps = []
    for j in range(TAPS):
        if j:
            moved = jnp.pad(after[:j], ((reach - j, 0), (0, 0)))
            patch = patch + moved * kernel[TAPS - 1 - j][None]
        taps.append(jnp.sum(joined[:j] * past[PAD - j :], axis=0))
    cross_taps = jnp.stack(taps[::-1])
    tail = jnp.pad(patch, ((PAD - reach, 0), (0, 0))).astype(BF)
    dv = dv.at[tokens - PAD :].add(tail[:, :width])
    dst = dst.at[tokens - PAD :].add(tail[:, width:])
    cvg = cvg + cross_taps[:, :width]
    csg = csg + cross_taps[:, width:]

    dwv = dot_tn(normed, dv).astype(BF)
    dws = dot_tn(normed, dst)
    dwst = dot_tn(normed, dz)[:, 96 : 96 + heads]
    wst_tail = jnp.pad(wstep, ((0, 0), (96, GROUP - heads)))
    dn = dot_nt(dst, state_weight) + dot_nt(dz, wst_tail)
    for k, (a, b) in enumerate(zip(wgs, wvs)):
        cut = slice(k * a.shape[1], (k + 1) * a.shape[1])
        dn = dn + dot_nt(dgate[:, cut], a) + dot_nt(dv[:, cut], b)
    u = hidden_in.astype(F32)
    scale = lax.rsqrt(jnp.mean(u * u, axis=1, keepdims=True) + EPS)
    unit = u * scale
    norm_gain_grad = jnp.sum(dn * unit, axis=0)
    du = dn * gain
    inner = jnp.mean(du * unit, axis=1, keepdims=True)
    input_grad = (out_grad.astype(F32) + scale * (du - unit * inner)).astype(BF)

    bias_sum = head_sums[1, 96 : 96 + heads]
    dlog_sum = head_sums[0, 64 : 64 + heads]
    skip_sum = skip_grad.reshape(heads, HEAD_DIM).sum(axis=1)

    def by_shard(k):
        cut, hcut = slice(k * local, (k + 1) * local), slice(k * local_heads, (k + 1) * local_heads)
        return jnp.concatenate(
            [cvg[:, cut].reshape(-1), ggain_grad[0, cut], bias_sum[hcut], dlog_sum[hcut], skip_sum[hcut]]
        )

    def absolute(parts, axis):
        if not paired:
            return jnp.concatenate(parts, axis=axis)
        a = jnp.concatenate(parts, axis=axis)
        b = jnp.concatenate(parts[::-1], axis=axis)
        return jnp.where(channel == 0, a, b)

    each = (TAPS + 1) * local + 3 * local_heads
    pad_each = -each % 128
    tiny = absolute([jnp.pad(by_shard(k), (0, pad_each)) for k in range(shards)], 0)
    tiny = jnp.concatenate([tiny, norm_gain_grad, csg.reshape(-1)])
    tiny = jnp.pad(tiny, (0, -tiny.shape[0] % 1024)).reshape(-1, 128)
    dwst = absolute([dwst[:, k * local_heads : (k + 1) * local_heads] for k in range(shards)], 1)
    both = jnp.concatenate([dws, jnp.pad(dwst, ((0, 0), (0, 128 - heads)))], axis=1).astype(BF)

    bits = groups_dp.bit_length() - 1
    if paired and groups_dp == 2**bits and bits >= 2 and width_in % (16 * groups_dp) == 0:
        dwg, dwv, owg, both, tiny = reduce_all(
            bits, [(dwg, "cols"), (dwv, "cols"), (ow_grad, "rows")], both, tiny, 256
        )
        dwg, dwv, owg = dwg.astype(F32), dwv.astype(F32), owg.astype(F32)
    else:

        def shared(v, axis):
            if paired:
                parts = jnp.split(v, 2, axis=axis)
                v = absolute(parts, axis)
            v = lax.psum_scatter(v, "chan", scatter_dimension=axis, tiled=True)
            return lax.psum(v, "dp").astype(F32)

        dwg, dwv, owg = shared(dwg, 1), shared(dwv, 1), shared(ow_grad, 0)
        both, tiny = lax.psum((both, tiny), ("dp", "chan"))

    gvw = jnp.stack(
        [dwg.reshape(width_in, local_heads, HEAD_DIM), dwv.reshape(width_in, local_heads, HEAD_DIM)],
        axis=2,
    ).reshape(width_in, local_heads, 2 * HEAD_DIM)
    both = both.astype(F32)
    flat = tiny.reshape(-1)
    base = (each + pad_each) * shards
    mine = lax.dynamic_slice_in_dim(flat, channel * (each + pad_each), each, 0)
    cuts = np.cumsum([TAPS * local, local, local_heads, local_heads])
    dwst = lax.dynamic_slice_in_dim(both[:, 128:], channel * local_heads, local_heads, 1)
    return (
        output,
        input_grad,
        flat[base : base + width_in],
        gvw,
        both[:, :128],
        dwst,
        mine[: cuts[0]].reshape(TAPS, local),
        flat[base + width_in : base + width_in + TAPS * 128].reshape(TAPS, 128),
        mine[cuts[1] : cuts[2]],
        mine[cuts[2] : cuts[3]],
        mine[cuts[3] :],
        mine[cuts[0] : cuts[1]],
        owg,
    )


def solution(mesh):
    in_specs = (
        P(("dp", "chan"), None),
        P(),
        P(None, "chan", None),
        P(),
        P(None, "chan"),
        P(None, "chan"),
        P(),
        P("chan"),
        P("chan"),
        P("chan"),
        P("chan"),
        P("chan", None),
        P("dp"),
        P("dp"),
        P(("dp", "chan"), None),
    )
    out_specs = (
        P(("dp", "chan"), None),
        P(("dp", "chan"), None),
        P(),
        P(None, "chan", None),
        P(),
        P(None, "chan"),
        P(None, "chan"),
        P(),
        P("chan"),
        P("chan"),
        P("chan"),
        P("chan"),
        P("chan", None),
    )
    return jax.shard_map(
        on_device, mesh=mesh, in_specs=in_specs, out_specs=out_specs, check_vma=False
    )
```

```python
import functools

import jax
import jax.numpy as jnp
import numpy as np
from jax import lax
from jax.experimental import pallas as pl
from jax.experimental.pallas import tpu as pltpu
from jax.sharding import PartitionSpec as P

HEAD_DIM = 64
STATE = 64
SPAN = 128
PAD = 16
GROUP = 32
TAPS = 4
LANES = 128
SLACK = 2
EPS = 1e-05
LOG2E = float(np.log2(np.e))
BF = jnp.bfloat16
F32 = jnp.float32


def dot(a, b):
    return jnp.dot(a, b, preferred_element_type=F32)


def dot_nt(a, b):
    return lax.dot_general(a, b, (((1,), (1,)), ((), ())), preferred_element_type=F32)


def dot_tn(a, b):
    return lax.dot_general(a, b, (((0,), (0,)), ((), ())), preferred_element_type=F32)


def fine_nt(a, b):
    return lax.dot_general(
        a, b, (((1,), (1,)), ((), ())), precision=lax.Precision.HIGHEST, preferred_element_type=F32
    )


def sigmoid(v):
    return 0.5 + 0.5 * jnp.tanh(0.5 * v)


def lanes_of(rows):
    return lax.broadcasted_iota(jnp.int32, (rows, 128), 1)


def shifted(ext, offset, rows):
    return ext[offset : offset + rows]


def full(shape):
    rank = len(shape)
    return pl.BlockSpec(shape, lambda i: (0,) * rank)


SMEM = pl.BlockSpec(memory_space=pltpu.SMEM)


def cost(micros):
    return pl.CostEstimate(flops=int(micros * 1e9), bytes_accessed=1024, transcendentals=0)


def side(a, b):
    return jnp.concatenate([a, b], axis=1)


def high_low(v):
    hi = v.astype(BF)
    return side(hi, (v - hi.astype(F32)).astype(BF))


def by_pairs(maps, axis):
    pairs = maps[0].shape[axis] // 128
    pieces = [np.split(m, pairs, axis=axis) for m in maps]
    return np.concatenate([piece[p] for p in range(pairs) for piece in pieces], axis=axis)


def expanders(heads):
    channel = np.arange(heads * HEAD_DIM) // HEAD_DIM
    lane = np.arange(128)[:, None]
    return [np.asarray(lane == GROUP * g + channel[None], np.float32) for g in range(4)]


def project_kernel(fresh, final, tile, chunk, *refs):
    refs = list(refs)

    def take(count):
        return [refs.pop(0) for _ in range(count)]

    sc, tokens_r, halo, edge, wg, wv, wst, cv, bias, nal, tri, e0, e1 = take(13)
    if fresh:
        gain, ws, cs = take(3)
    else:
        (bc_r,) = take(1)
    gate_o, v_o, xpre_o, ff_o, sb_o, pb_o, sft_o, sbt_o, pft_o, pbt_o, hand_o, vh_o = take(12)
    if fresh:
        normed_o, nedge_o, ps_o, pspre_o, bc_o, psh_o = take(6)
    if final:
        col_o, row_o = take(2)
    sb_s, pb_s, sf_s, pf_s = take(4)

    step = pl.program_id(0)
    tiles = pl.num_programs(0)
    at = tiles - 1 - step
    length = sc[1]
    start = sc[0] + at * tile
    width = e0.shape[1]
    blocks = tile // SPAN

    @pl.when(step == 0)
    def _():
        sb_s[...] = jnp.zeros_like(sb_s)
        sf_s[...] = jnp.zeros_like(sf_s)
        pb_s[...] = jnp.ones_like(pb_s)
        pf_s[...] = jnp.ones_like(pf_s)

    before = jnp.where(at == 0, edge[...].astype(F32), halo[...].astype(F32))
    rows = jnp.concatenate([before, tokens_r[...].astype(F32)], axis=0)
    keep = jnp.where(lax.rem(start, length) == 0, 0.0, 1.0)
    row_id = lax.broadcasted_iota(jnp.int32, (tile + PAD, 1), 0)
    keep_rows = jnp.where(row_id < PAD, keep, 1.0)
    if fresh:
        scale = lax.rsqrt(jnp.mean(rows * rows, axis=1, keepdims=True) + EPS)
        normed = (rows * scale * gain[...]).astype(BF)
        own = normed[PAD:]
        normed_o[...] = own

        ps = dot(normed, ws[...]) * keep_rows
        ps_o[...] = ps[PAD:]
        pspre = ps[PAD:] * cs[TAPS - 1 : TAPS]
        for j in range(1, TAPS):
            pspre = pspre + shifted(ps, PAD - j, tile) * cs[TAPS - 1 - j : TAPS - j]
        pspre_o[...] = pspre
        bc = pspre * sigmoid(pspre)
        bc_o[...] = bc

        @pl.when(at == 0)
        def _():
            nedge_o[...] = normed[:PAD]
            psh_o[...] = ps[:PAD]

    else:
        normed = rows.astype(BF)
        own = tokens_r[...]
        bc = bc_r[...]

    z = dot(own, wst[...]) + bias[...]
    dt = jnp.maximum(z, 0.0) + jnp.log1p(jnp.exp(-jnp.abs(z)))
    a2 = dt * nal[...]
    lane = lanes_of(SPAN)
    if final:
        sig = sigmoid(z)
    wmix, bts = [], []
    for b in range(blocks):
        sl = slice(b * SPAN, (b + 1) * SPAN)
        ab = a2[sl]
        ca = jnp.dot(tri[...], ab, precision=lax.Precision.HIGHEST, preferred_element_type=F32)
        ce = ca - ab
        if final:
            col = jnp.where(
                lane < 32, ca, jnp.where(lane < 64, ce, jnp.where(lane < 96, dt[sl], sig[sl]))
            )
            col_o[sl, :] = col
            row_o[sl, :] = jnp.transpose(col)
        end = ca[SPAN - 1 : SPAN]
        w = jnp.exp2(jnp.where(lane < 32, end - ca, ce)) * dt[sl]
        dec = jnp.broadcast_to(jnp.exp2(end), (8, 128))
        high = dec.astype(BF).astype(F32)
        wmix.append(jnp.concatenate([w, high, dec - high], axis=0).astype(BF))
        bts.append(jnp.transpose(bc[sl])[:STATE].astype(BF))

    for c in range(width // chunk):
        cl = slice(c * chunk, (c + 1) * chunk)
        gate_o[:, cl] = dot(own, wg[:, cl]).astype(BF)
        v = dot(normed, wv[:, cl]) * keep_rows
        v_o[:, cl] = v[PAD:].astype(BF)

        @pl.when(at == 0)
        def _():
            vh_o[:, cl] = v[:PAD]

        xpre = v[PAD:] * cv[TAPS - 1 : TAPS, cl]
        for j in range(1, TAPS):
            xpre = xpre + shifted(v, PAD - j, tile) * cv[TAPS - 1 - j : TAPS - j, cl]
        xpre_o[:, cl] = xpre.astype(BF)
        x = xpre * sigmoid(xpre)
        for b in reversed(range(blocks)):
            sl = slice(b * SPAN, (b + 1) * SPAN)
            we = dot(wmix[b], e0[:, cl])
            wbe = dot(wmix[b][:SPAN], e1[:, cl])
            dec = we[SPAN : SPAN + 1] + we[SPAN + 8 : SPAN + 9]
            xb = x[sl]
            fresh_f = dot(bts[b], (xb * we[:SPAN]).astype(BF))
            fresh_b = dot(bts[b], (xb * wbe).astype(BF))
            place = start + b * SPAN
            first = jnp.where(lax.rem(place, length) == 0, 0.0, 1.0)
            last = jnp.where(lax.rem(place + SPAN, length) == 0, 0.0, 1.0)
            ff_o[b, :, cl] = fresh_f.astype(BF)
            pf = pf_s[0:1, cl]
            sf_s[:, cl] = sf_s[:, cl] + pf * fresh_f
            pf_s[:, cl] = jnp.broadcast_to(pf * dec * first, (8, chunk))
            held = sb_s[:, cl] * last
            pb = pb_s[0:1, cl] * last
            sb_o[b, :, cl] = held.astype(BF)
            pb_o[b, :, cl] = jnp.broadcast_to(pb, (8, chunk))
            sb_s[:, cl] = held * dec + fresh_b
            pb_s[:, cl] = jnp.broadcast_to(pb * dec, (8, chunk))

    @pl.when(at == 0)
    def _():
        sft_o[...] = sf_s[...]
        sbt_o[...] = sb_s[...]
        pft_o[...] = pf_s[...]
        pbt_o[...] = pb_s[...]
        hand_o[...] = jnp.where(sc[0] == 0, sf_s[...], sb_s[...]).astype(BF)


def project(sc, source, edge, wg, wv, wst, cv, bias, nal, e0, e1, maps=None, bc=None, final=True):
    fresh = maps is not None
    tokens, width_in = source.shape
    width = wg.shape[1]
    tile = min(256, tokens)
    tiles = tokens // tile
    per = tile // SPAN
    blocks = tokens // SPAN
    chunk = 256 if width % 256 == 0 else 128
    tri = np.tril(np.ones((SPAN, SPAN), np.float32))

    def back(shape):
        rank = len(shape)
        return pl.BlockSpec(shape, lambda i: (tiles - 1 - i,) + (0,) * (rank - 1))

    sds = jax.ShapeDtypeStruct
    wide = (sds((tokens, width), BF), back((tile, width)))
    narrow = (sds((tokens, 128), F32), back((tile, 128)))
    held = (sds((blocks, STATE, width), BF), back((per, STATE, width)))
    total = (sds((STATE, width), F32), full((STATE, width)))
    passed = (sds((8, width), F32), full((8, width)))
    outs = [wide, wide, wide, held, held, (sds((blocks, 8, width), F32), back((per, 8, width)))]
    outs += [total, total, passed, passed, (sds((STATE, width), BF), full((STATE, width)))]
    outs += [(sds((PAD, width), F32), full((PAD, width)))]
    if fresh:
        outs += [
            (sds((tokens, width_in), BF), back((tile, width_in))),
            (sds((PAD, width_in), BF), full((PAD, width_in))),
            narrow,
            narrow,
            narrow,
            (sds((PAD, 128), F32), full((PAD, 128))),
        ]
    if final:
        outs += [narrow, narrow]
    steps = tile // PAD
    args = [sc, source, source, edge, wg, wv, wst, cv, bias, nal, tri, e0, e1]
    in_specs = [
        SMEM,
        back((tile, width_in)),
        pl.BlockSpec((PAD, width_in), lambda i: (jnp.maximum((tiles - 1 - i) * steps - 1, 0), 0)),
    ] + [full(a.shape) for a in args[3:]]
    if fresh:
        args += list(maps)
        in_specs += [full(a.shape) for a in maps]
    else:
        args += [bc]
        in_specs += [back((tile, 128))]
    return pl.pallas_call(
        functools.partial(project_kernel, fresh, final, tile, chunk),
        grid=(tiles,),
        in_specs=in_specs,
        out_specs=[spec for _, spec in outs],
        out_shape=[shape for shape, _ in outs],
        scratch_shapes=[
            pltpu.VMEM((STATE, width), F32),
            pltpu.VMEM((8, width), F32),
            pltpu.VMEM((STATE, width), F32),
            pltpu.VMEM((8, width), F32),
        ],
        compiler_params=pltpu.CompilerParams(vmem_limit_bytes=58 * 1024 * 1024),
        cost_estimate=cost(28),
        name="project",
    )(*args)


def split_refs(refs, groups, kinds):
    taken = [[refs.pop(0) for _ in range(groups)] for _ in range(kinds)]
    return [functools.partial(pick, refs_of) for refs_of in taken]


def pick(refs_of, p):
    per = refs_of[0].shape[-1] // 128
    return refs_of[p // per], slice((p % per) * 128, (p % per + 1) * 128)


def mix_kernel(groups, *refs):
    refs = list(refs)
    sc = refs.pop(0)
    gates, xpres, ffs, sbls, pbs, sfds, sbds = split_refs(refs, groups, 7)
    mix_body(sc, gates, xpres, ffs, sbls, pbs, sfds, sbds, *refs)


def mix_body(
    sc, gates, xpres, ffs, sbls, pbs, sfds, sbds,
    bc_r, col_r, row_r, hid, gout, ow, owt, ggain, skip, e01, e2,
    out_o, gnorm_o, dy_o, dgate_o, sf_o, sb_o, gbl_o, pg_o, dff_o,
    gft_o, gbt_o, pgf_o, pgb_o, hand_o, ggain_o, skip_o,
    sf_s, gb_s, gf_s, pg_s, q_s, y_s, dgn_s, exp_s,
):
    i = pl.program_id(0)
    length = sc[1]
    place = sc[0] + i * SPAN
    first = jnp.where(lax.rem(place, length) == 0, 0.0, 1.0)
    last = jnp.where(lax.rem(place + SPAN, length) == 0, 0.0, 1.0)
    live = jnp.where(lax.div(place, length) < sc[2], 1.0, 0.0)
    width = e2.shape[1]
    pairs = width // 128

    @pl.when(i == 0)
    def _():
        enters_f = jnp.where(sc[3] == 1, 1.0, 0.0)
        for p in range(pairs):
            ref, at = sfds(p)
            sf_s[:, p * 128 : (p + 1) * 128] = ref[:, at].astype(F32) * enters_f
        gb_s[...] = jnp.zeros_like(gb_s)
        gf_s[...] = jnp.zeros_like(gf_s)
        pg_s[...] = jnp.ones_like(pg_s)
        q_s[...] = jnp.ones_like(q_s)
        ggain_o[...] = jnp.zeros_like(ggain_o)
        skip_o[...] = jnp.zeros_like(skip_o)

    enters_b = jnp.where(sc[4] == 1, 1.0, 0.0)
    glow = gout[...].astype(F32) * live
    gl = glow.astype(BF)
    dgn_s[...] = dot(gl, owt[...])

    lane = lanes_of(SPAN)
    low_half = lane < HEAD_DIM
    col = col_r[...]
    row = row_r[...]
    end = jnp.broadcast_to(col[SPAN - 1 : SPAN], (8, 128))
    end1 = pltpu.roll(end, GROUP, 1)
    w = jnp.where(lane < 64, jnp.exp2(jnp.where(lane < 32, col, end1[0:1] - col)), col)
    dec = jnp.exp2(end)
    high = dec.astype(BF).astype(F32)
    wmix = jnp.concatenate([w, high, dec - high], axis=0).astype(BF)
    wtok = wmix[:SPAN]
    bc = bc_r[...]
    bmf, cmf = bc[:, :STATE], bc[:, STATE:]
    cm = cmf.astype(BF)
    ct = jnp.transpose(bc)[STATE:].astype(BF)
    square_r = lax.broadcasted_iota(jnp.int32, (SPAN, SPAN), 0)
    aff = jnp.where(square_r == lane, 0.0, fine_nt(cmf, bmf))

    squares = jnp.zeros((SPAN, 128), F32)
    for p in range(pairs):
        sl = slice(p * 128, (p + 1) * 128)
        efd = dot(wmix, e01[:, p * 256 : (p + 1) * 256])
        ef, eb = efd[:SPAN, :128], efd[:SPAN, 128:]
        dte = dot(wtok, e2[:, sl])
        exp_s[0, :, sl] = ef
        exp_s[1, :, sl] = eb
        decay = efd[SPAN : SPAN + 1, :128] + efd[SPAN + 8 : SPAN + 9, :128]
        exp_s[2, 0:8, sl] = jnp.broadcast_to(decay, (8, 128))
        sf = sf_s[:, sl] * first
        sfb = sf.astype(BF)
        sf_o[0, :, sl] = sfb
        sbl, at = sbls(p)
        pb, sbd, ff, xpre, gate = (r(p)[0] for r in (pbs, sbds, ffs, xpres, gates))
        arrived = sbd[:, at].astype(F32) * enters_b
        sb = (sbl[0, :, at].astype(F32) + pb[0, 0:1, at] * arrived) * last
        sbb = sb.astype(BF)
        sb_o[0, :, sl] = sbb
        sf_s[:, sl] = sf * decay + ff[0, :, at].astype(F32)
        xp = xpre[:, at].astype(F32)
        x = xp * sigmoid(xp)
        xd = x * dte
        bd = jnp.concatenate(
            [jnp.where(low_half, xd, 0.0), jnp.where(low_half, 0.0, xd)], axis=0
        ).astype(BF)
        ms = []
        for h in (2 * p, 2 * p + 1):
            spread = jnp.minimum(
                col[:, h : h + 1] - row[h : h + 1, :],
                row[GROUP + h : GROUP + h + 1, :] - col[:, GROUP + h : GROUP + h + 1],
            )
            ms.append((aff * jnp.exp2(spread)).astype(BF))
        y = dot(jnp.concatenate(ms, axis=1), bd)
        carried = dot(cm, side(sfb, sbb))
        y = y + ef * carried[:, :128] + eb * carried[:, 128:] + skip[:, sl] * x
        y_s[:, sl] = y
        g = gate[:, at].astype(F32)
        gated = y * (g * sigmoid(g))
        squares = squares + gated * gated

    gsc = lax.rsqrt(jnp.sum(squares, axis=1, keepdims=True) * (1.0 / width) + EPS)
    inner = jnp.zeros((SPAN, 128), F32)
    for p in range(pairs):
        sl = slice(p * 128, (p + 1) * 128)
        gate, at = gates(p)
        g = gate[:, at].astype(F32)
        gunit = y_s[:, sl] * (g * sigmoid(g)) * gsc
        gnorm_o[:, sl] = (gunit * ggain[:, sl]).astype(BF)
        dgn = dgn_s[:, sl]
        dgu = dgn * gunit
        ggain_o[:, sl] += jnp.sum(dgu, axis=0, keepdims=True)
        inner = inner + dgu * ggain[:, sl]
    mean = jnp.sum(inner, axis=1, keepdims=True) * (1.0 / width)
    out_o[...] = (hid[...].astype(F32) + live * dot(gnorm_o[...], ow[...])).astype(BF)

    for p in range(pairs):
        sl = slice(p * 128, (p + 1) * 128)
        gate, at = gates(p)
        g = gate[:, at].astype(F32)
        sg = sigmoid(g)
        act = g * sg
        y = y_s[:, sl]
        gunit = y * act * gsc
        dgated = gsc * (dgn_s[:, sl] * ggain[:, sl] - gunit * mean)
        dy = dgated * act
        dy_o[:, sl] = dy.astype(BF)
        dgate_o[:, sl] = (dgated * y * (sg * (1.0 + g * (1.0 - sg)))).astype(BF)
        xp = xpres(p)[0][:, at].astype(F32)
        skip_o[:, sl] += jnp.sum(dy * (xp * sigmoid(xp)), axis=0, keepdims=True)
        decay = exp_s[2, 0:1, sl]
        states = dot(ct, side(exp_s[0, :, sl] * dy, exp_s[1, :, sl] * dy).astype(BF))
        dff, dfb = states[:, :128], states[:, 128:]
        dff_o[0, :, sl] = dff.astype(BF)
        q = q_s[0:1, sl]
        gf_s[:, sl] = gf_s[:, sl] + q * dff
        q_s[:, sl] = jnp.broadcast_to(q * decay * last, (8, 128))
        gb = gb_s[:, sl] * first
        pg = pg_s[0:1, sl] * first
        gbl_o[0, :, sl] = gb.astype(BF)
        pg_o[0, :, sl] = jnp.broadcast_to(pg, (8, 128))
        gb_s[:, sl] = gb * decay + dfb
        pg_s[:, sl] = jnp.broadcast_to(pg * decay, (8, 128))

    @pl.when(i == pl.num_programs(0) - 1)
    def _():
        gft_o[...] = gf_s[...]
        gbt_o[...] = gb_s[...]
        pgf_o[...] = q_s[...]
        pgb_o[...] = pg_s[...]
        hand_o[...] = jnp.where(sc[0] == 0, gb_s[...], gf_s[...]).astype(BF)


def mix(sc, split, bc, col, row, hidden, out_grad, ow, owt, ggain, skip, e01, e2):
    tokens, width_in = hidden.shape
    groups = len(split[0])
    width = e2.shape[1]
    part = width // groups
    blocks = tokens // SPAN

    def ahead(shape):
        rank = len(shape)
        return pl.BlockSpec(shape, lambda i: (i,) + (0,) * (rank - 1))

    sds = jax.ShapeDtypeStruct
    state = (1, STATE, width)
    outs = [
        (sds((tokens, width_in), BF), ahead((SPAN, width_in))),
        (sds((tokens, width), BF), ahead((SPAN, width))),
        (sds((tokens, width), BF), ahead((SPAN, width))),
        (sds((tokens, width), BF), ahead((SPAN, width))),
        (sds((blocks, STATE, width), BF), ahead(state)),
        (sds((blocks, STATE, width), BF), ahead(state)),
        (sds((blocks, STATE, width), BF), ahead(state)),
        (sds((blocks, 8, width), F32), ahead((1, 8, width))),
        (sds((blocks, STATE, width), BF), ahead(state)),
        (sds((STATE, width), F32), full((STATE, width))),
        (sds((STATE, width), F32), full((STATE, width))),
        (sds((8, width), F32), full((8, width))),
        (sds((8, width), F32), full((8, width))),
        (sds((STATE, width), BF), full((STATE, width))),
        (sds((1, width), F32), full((1, width))),
        (sds((1, width), F32), full((1, width))),
    ]
    shared = [ow, owt, ggain, skip, e01, e2]
    in_specs = [SMEM]
    for shape in (
        (SPAN, part), (SPAN, part), (1, STATE, part), (1, STATE, part), (1, 8, part),
    ):
        in_specs += [ahead(shape)] * groups
    in_specs += [full((STATE, part))] * (2 * groups)
    in_specs += [ahead((SPAN, 128))] * 3 + [ahead((SPAN, width_in))] * 2
    in_specs += [full(a.shape) for a in shared]
    return pl.pallas_call(
        functools.partial(mix_kernel, groups),
        grid=(blocks,),
        in_specs=in_specs,
        out_specs=[spec for _, spec in outs],
        out_shape=[shape for shape, _ in outs],
        scratch_shapes=[
            pltpu.VMEM((STATE, width), F32),
            pltpu.VMEM((STATE, width), F32),
            pltpu.VMEM((STATE, width), F32),
            pltpu.VMEM((8, width), F32),
            pltpu.VMEM((8, width), F32),
            pltpu.VMEM((SPAN, width), F32),
            pltpu.VMEM((SPAN, width), F32),
            pltpu.VMEM((3, SPAN, width), F32),
        ],
        compiler_params=pltpu.CompilerParams(vmem_limit_bytes=58 * 1024 * 1024),
        cost_estimate=cost(60),
        name="mix",
    )(sc, *[a for kind in split for a in kind], bc, col, row, hidden, out_grad, *shared)


def back_kernel(heads, groups, *refs):
    refs = list(refs)
    sc = refs.pop(0)
    xpres, vs, gfds, gbds = split_refs(refs, groups, 4)
    back_body(heads, sc, xpres, vs, gfds, gbds, *refs)


def back_body(
    heads, sc, xpres, vs, gfds, gbds,
    dy_r, bc_r, ps_r, pspre_r, col_r, row_r, sf_r, sb_r, gbl, pg, dff,
    skip, cv, cs, nad, e01, seg4, seg2, segs, tris,
    dv_o, dst_o, dz_o, cvg_o, csg_o, head_o, edge_o, edges_o,
    gf_s, edge_s, edges_s, da_s, cross_s,
):
    step = pl.program_id(0)
    blocks = pl.num_programs(0)
    i = blocks - 1 - step
    length = sc[1]
    place = sc[0] + i * SPAN
    last = jnp.where(lax.rem(place + SPAN, length) == 0, 0.0, 1.0)
    width = e01.shape[1] // 2
    pairs = width // 128

    @pl.when(step == 0)
    def _():
        enters_f = jnp.where(sc[5] == 1, 1.0, 0.0)
        for p in range(pairs):
            ref, at = gfds(p)
            gf_s[:, p * 128 : (p + 1) * 128] = ref[:, at].astype(F32) * enters_f
        edge_s[...] = jnp.zeros_like(edge_s)
        edges_s[...] = jnp.zeros_like(edges_s)
        da_s[...] = jnp.zeros_like(da_s)
        cvg_o[...] = jnp.zeros_like(cvg_o)
        csg_o[...] = jnp.zeros_like(csg_o)
        head_o[...] = jnp.zeros_like(head_o)

    lane = lanes_of(SPAN)
    low_half = lane < HEAD_DIM
    col = col_r[...]
    row = row_r[...]
    end = jnp.broadcast_to(col[SPAN - 1 : SPAN], (8, 128))
    end1 = pltpu.roll(end, GROUP, 1)
    w = jnp.where(lane < 64, jnp.exp2(jnp.where(lane < 32, col, end1[0:1] - col)), col)
    dec = jnp.exp2(end)
    high = dec.astype(BF).astype(F32)
    inner = jnp.exp2(jnp.where(lane < 32, end[0:1] - col, col))
    steps = pltpu.roll(col, 64, 1)
    wall = jnp.concatenate([w, inner, steps, high, dec - high], axis=0).astype(BF)
    bc = bc_r[...]
    bmf, cmf = bc[:, :STATE], bc[:, STATE:]
    bm, cm = bmf.astype(BF), cmf.astype(BF)
    enters_b = jnp.where(sc[6] == 1, 1.0, 0.0)
    square_r = lax.broadcasted_iota(jnp.int32, (SPAN, SPAN), 0)
    off = square_r != lane
    aff = jnp.where(off, fine_nt(bmf, cmf), 0.0)

    daff = jnp.zeros((SPAN, SPAN), F32)
    red = jnp.zeros((SPAN, 128), F32)
    whole = jnp.zeros((SPAN, 128), F32)
    ddt = jnp.zeros((SPAN, 128), F32)
    dc = jnp.zeros((SPAN, STATE), F32)
    db = jnp.zeros((SPAN, STATE), F32)
    for p in range(pairs):
        sl = slice(p * 128, (p + 1) * 128)
        two = slice(p * 256, (p + 1) * 256)
        efd = dot(wall, e01[:, two])
        ef, eb = efd[:SPAN, :128], efd[:SPAN, 128:]
        wf, wb = efd[SPAN : 2 * SPAN, :128], efd[SPAN : 2 * SPAN, 128:]
        dte = efd[2 * SPAN : 3 * SPAN, :128]
        decay = efd[3 * SPAN : 3 * SPAN + 1, :128] + efd[3 * SPAN + 8 : 3 * SPAN + 9, :128]
        sf, sb = sf_r[0, :, sl], sb_r[0, :, sl]
        gf32 = gf_s[:, sl] * last
        gbd, at = gbds(p)
        arrived = gbd[:, at].astype(F32) * enters_b
        gb32 = gbl[0, :, sl].astype(F32) + pg[0, 0:1, sl] * arrived
        gf, gb = gf32.astype(BF), gb32.astype(BF)
        gf_s[:, sl] = gf32 * decay + dff[0, :, sl].astype(F32)
        cross = (sf.astype(F32) * gf32 + sb.astype(F32) * gb32) * decay
        cross_s[:, sl] = jnp.broadcast_to(jnp.sum(cross, axis=0, keepdims=True), (8, 128))
        xp = xpres(p)[0][:, at].astype(F32)
        sg = sigmoid(xp)
        x = xp * sg
        xd = x * dte
        dy = dy_r[:, sl].astype(F32)
        efdy, ebdy = ef * dy, eb * dy
        wfxd, wbxd = wf * xd, wb * xd
        s_both, g_both = side(sf, sb), side(gf, gb)
        fed = dot(bm, g_both)
        cf, cb = wf * fed[:, :128], wb * fed[:, 128:]
        carried = dot(cm, s_both)
        edy = side(efdy, ebdy)
        dc = dc + dot_nt(edy.astype(BF), s_both)
        db = db + dot_nt(side(wfxd, wbxd).astype(BF), g_both)
        products = side((edy * carried).astype(BF), side(xd * cf, xd * cb).astype(BF))
        red = red + dot(products, seg4[p * 512 : (p + 1) * 512, :])
        bd = jnp.concatenate(
            [jnp.where(low_half, dy, 0.0), jnp.where(low_half, 0.0, dy)], axis=0
        ).astype(BF)
        dm = dot_nt(xd.astype(BF), bd)
        ms = []
        for k in range(2):
            h = 2 * p + k
            spread = jnp.minimum(
                row[h : h + 1, :] - col[:, h : h + 1],
                col[:, GROUP + h : GROUP + h + 1] - row[GROUP + h : GROUP + h + 1, :],
            )
            f = jnp.exp2(spread)
            m = aff * f
            ms.append(m.astype(BF))
            dmh = dm[:, k * 128 : (k + 1) * 128]
            daff = daff + f * dmh
            q = m * dmh
            ql = jnp.where(square_r < lane, q, 0.0)
            qu = q - ql
            da_s[h : h + 1, :] = jnp.sum(ql, axis=0, keepdims=True)
            da_s[GROUP + h : GROUP + h + 1, :] = jnp.sum(qu, axis=0, keepdims=True)
            whole = jnp.where(lane == h, jnp.sum(ql, axis=1, keepdims=True), whole)
            whole = jnp.where(lane == GROUP + h, jnp.sum(qu, axis=1, keepdims=True), whole)
        dxd = dot(jnp.concatenate(ms, axis=1), bd) + cf + cb
        ddt = ddt + dot(high_low(x * dxd), seg2[two, :])
        dx = dte * dxd + skip[:, sl] * dy
        dxp = dx * (sg * (1.0 + xp * (1.0 - sg)))
        ext = jnp.concatenate([dxp, edge_s[:, sl] * last], axis=0)
        edge_s[:, sl] = dxp[:8]
        v = vs(p)[0][:, at].astype(F32)
        dv = jnp.zeros((SPAN, 128), F32)
        for j in range(TAPS):
            moved = shifted(ext, j, SPAN)
            k = TAPS - 1 - j
            dv = dv + moved * cv[k : k + 1, sl]
            cvg_o[k : k + 1, sl] += jnp.sum(v * moved, axis=0, keepdims=True)
        dv_o[:, sl] = dv.astype(BF)

    dafb = jnp.where(off, daff, 0.0).astype(BF)
    db = db + dot(dafb, cm)
    dc = dc + dot_tn(dafb, bm)
    dbc = jnp.concatenate([db, dc], axis=1)
    pp = pspre_r[...]
    sp = sigmoid(pp)
    dpp = dbc * (sp * (1.0 + pp * (1.0 - sp)))
    ext = jnp.concatenate([dpp, edges_s[...] * last], axis=0)
    edges_s[...] = dpp[:8]
    ps = ps_r[...]
    dst = jnp.zeros((SPAN, 128), F32)
    for j in range(TAPS):
        moved = shifted(ext, j, SPAN)
        k = TAPS - 1 - j
        dst = dst + moved * cs[k : k + 1, :]
        csg_o[k : k + 1, :] += jnp.sum(ps * moved, axis=0, keepdims=True)
    dst_o[...] = dst.astype(BF)

    red = red - whole + jnp.transpose(da_s[...])
    hi = red.astype(BF)
    lo = (red - hi.astype(F32)).astype(BF)
    summed = dot(tris[...], hi) + dot(tris[...], lo)
    parts = [summed[g * SPAN : (g + 1) * SPAN] for g in range(4)]
    picked = jnp.where(
        lane < 32, parts[0], jnp.where(lane < 64, parts[1], jnp.where(lane < 96, parts[2], parts[3]))
    )
    total = picked + pltpu.roll(picked, 64, 1)
    total = total + pltpu.roll(total, 32, 1)
    crossed = cross_s[...]
    crossed_hi = crossed.astype(BF)
    crossed_lo = (crossed - crossed_hi.astype(F32)).astype(BF)
    da = total + (dot(crossed_hi, segs[...]) + dot(crossed_lo, segs[...]))[0:1]
    dz = (ddt + da * nad[...]) * col
    dz = jnp.where((lane >= 96) & (lane < 96 + heads), dz, 0.0)
    dz_o[...] = dz.astype(BF)
    head_o[0:1, :] += jnp.sum(da * col * nad[...], axis=0, keepdims=True)
    head_o[1:2, :] += jnp.sum(dz, axis=0, keepdims=True)

    @pl.when(i == 0)
    def _():
        edge_o[...] = edge_s[...]
        edges_o[...] = edges_s[...]


def back(heads, sc, split, dy, bc, ps, pspre, col, row, sf, sb, gbl, pg, dff, skip, cv, cs, nad):
    tokens, width = dy.shape
    groups = len(split[0])
    part = width // groups
    blocks = tokens // SPAN
    maps = expanders(heads)
    every = sum(maps)
    seg4 = by_pairs([m.T for m in maps], 0)
    seg2 = by_pairs([every.T, every.T], 0)
    segs = every.T
    at = np.arange(SPAN)
    row_at, col_at = at[:, None], at[None, :]
    tris = np.concatenate(
        [col_at >= row_at, col_at <= row_at, col_at < row_at, col_at > row_at], axis=0
    ).astype(np.float32)
    e01 = by_pairs(maps[:2], 1)

    def rev(shape):
        rank = len(shape)
        return pl.BlockSpec(shape, lambda i: (blocks - 1 - i,) + (0,) * (rank - 1))

    sds = jax.ShapeDtypeStruct
    state = (1, STATE, width)
    outs = [
        (sds((tokens, width), BF), rev((SPAN, width))),
        (sds((tokens, 128), BF), rev((SPAN, 128))),
        (sds((tokens, 128), BF), rev((SPAN, 128))),
        (sds((TAPS, width), F32), full((TAPS, width))),
        (sds((TAPS, 128), F32), full((TAPS, 128))),
        (sds((8, 128), F32), full((8, 128))),
        (sds((8, width), F32), full((8, width))),
        (sds((8, 128), F32), full((8, 128))),
    ]
    shared = [skip, cv, cs, nad]
    shared += [jnp.asarray(m, BF) for m in (e01, seg4, seg2, segs, tris)]
    in_specs = [SMEM] + [rev((SPAN, part))] * (2 * groups)
    in_specs += [full((STATE, part))] * (2 * groups)
    in_specs += [rev((SPAN, width))] + [rev((SPAN, 128))] * 5
    in_specs += [rev(state)] * 3 + [rev((1, 8, width)), rev(state)]
    in_specs += [full(a.shape) for a in shared]
    return pl.pallas_call(
        functools.partial(back_kernel, heads, groups),
        grid=(blocks,),
        in_specs=in_specs,
        out_specs=[spec for _, spec in outs],
        out_shape=[shape for shape, _ in outs],
        scratch_shapes=[
            pltpu.VMEM((STATE, width), F32),
            pltpu.VMEM((8, width), F32),
            pltpu.VMEM((8, 128), F32),
            pltpu.VMEM((128, 128), F32),
            pltpu.VMEM((8, width), F32),
        ],
        compiler_params=pltpu.CompilerParams(vmem_limit_bytes=58 * 1024 * 1024),
        cost_estimate=cost(100),
        name="back",
    )(
        sc, *[a for kind in split for a in kind],
        dy, bc, ps, pspre, col, row, sf, sb, gbl, pg, dff, *shared,
    )


def input_kernel(groups, *refs):
    refs = list(refs)
    wgs, wvs = (refs[:groups], refs[groups : 2 * groups])
    dgate, dv, dst, dz, ws, wst, gain, hid, gout, grad_o, gain_o = refs[2 * groups :]

    @pl.when(pl.program_id(0) == 0)
    def _():
        gain_o[...] = jnp.zeros_like(gain_o)

    dn = dot_nt(dst[...], ws[...]) + dot_nt(dz[...], wst[...])
    for k in range(groups):
        part = wgs[k].shape[1]
        cut = slice(k * part, (k + 1) * part)
        dn = dn + dot_nt(dgate[:, cut], wgs[k][...]) + dot_nt(dv[:, cut], wvs[k][...])
    u = hid[...].astype(F32)
    scale = lax.rsqrt(jnp.mean(u * u, axis=1, keepdims=True) + EPS)
    unit = u * scale
    gain_o[...] += jnp.sum(dn * unit, axis=0, keepdims=True)
    du = dn * gain[...]
    inner = jnp.mean(du * unit, axis=1, keepdims=True)
    grad_o[...] = (gout[...].astype(F32) + scale * (du - unit * inner)).astype(BF)


def input_side(wgs, wvs, dgate, dv, dst, dz, ws, wst, gain, hidden, out_grad):
    tokens, width_in = hidden.shape
    tile = min(512, tokens)

    def rows(a):
        return pl.BlockSpec((tile, a.shape[1]), lambda i: (i, 0))

    sds = jax.ShapeDtypeStruct
    fixed = [*wgs, *wvs]
    streams = [dgate, dv, dst, dz]
    specs = [full(a.shape) for a in fixed] + [rows(a) for a in streams]
    specs += [full(a.shape) for a in (ws, wst, gain)] + [rows(hidden), rows(out_grad)]
    return pl.pallas_call(
        functools.partial(input_kernel, len(wgs)),
        grid=(tokens // tile,),
        in_specs=specs,
        out_specs=[rows(hidden), full((1, width_in))],
        out_shape=[sds((tokens, width_in), BF), sds((1, width_in), F32)],
        compiler_params=pltpu.CompilerParams(vmem_limit_bytes=58 * 1024 * 1024),
        cost_estimate=cost(15),
        name="input_side",
    )(*fixed, *streams, ws, wst, gain, hidden, out_grad)


def reduce_kernel(bits, lanes, mats, *refs):
    n_mats = len(mats)
    srcs, both, tiny = refs[:n_mats], refs[n_mats], refs[n_mats + 1]
    paired_o, last_o, both_o, tiny_o = refs[n_mats + 2 : n_mats + 6]
    outs = (*refs[n_mats + 6 : n_mats + 8], last_o)
    scratch = refs[n_mats + 8 :]
    own_r, sent = scratch[0], scratch[1]
    halves, parts = scratch[2 : 2 + bits], scratch[2 + bits : 1 + 2 * bits]
    tiny_r, tiny_s, send_s, recv_s, tsend_s, trecv_s = scratch[1 + 2 * bits :]
    rows = srcs[0].shape[0] if mats[0] == "cols" else srcs[0].shape[0] // 2
    width = outs[0].shape[1]
    me = lax.axis_index("dp")
    chan = lax.axis_index("chan")
    bit = [lax.rem(lax.div(me, 2**k), 2) for k in range(bits)]
    partner = [{"dp": me + (1 - 2 * bit[k]) * 2**k} for k in range(bits)]
    across = {"chan": 1 - chan}
    stages = [partner[0], across] + partner[1:]

    barrier = pltpu.get_barrier_semaphore()
    for device in stages:
        pl.semaphore_signal(barrier, inc=1, device_id=device, device_id_type=pl.DeviceIdType.MESH)
    pl.semaphore_wait(barrier, bits + 1)

    chunks = [(m, s) for m in range(n_mats) for s in range(0, width, lanes)]
    mains = len(chunks)
    n = mains + both.shape[1] // lanes
    half = rows // 2

    def mult(v):
        return pl.multiple_of(v, 16)

    def source(c, which, part):
        if c >= mains:
            return both.at[pl.ds(mult(part * half), half), pl.ds((c - mains) * lanes, lanes)]
        m, s = chunks[c]
        if mats[m] == "cols":
            return srcs[m].at[pl.ds(mult(part * half), half), pl.ds(which * width + s, lanes)]
        return srcs[m].at[pl.ds(mult(which * rows + part * half), half), pl.ds(s, lanes)]

    def target(c, start, size):
        if c >= mains:
            return both_o.at[pl.ds(mult(start), size), pl.ds((c - mains) * lanes, lanes)]
        m, s = chunks[c]
        return outs[m].at[pl.ds(mult(start), size), pl.ds(s, lanes)]

    def copy(src, dst, c, k, device):
        return pltpu.make_async_remote_copy(
            src_ref=src,
            dst_ref=dst,
            send_sem=send_s.at[c, k],
            recv_sem=recv_s.at[c, k],
            device_id=device,
            device_id_type=pl.DeviceIdType.MESH,
        )

    offset = [bit[0] * half]
    for k in range(1, bits):
        offset.append(offset[-1] + bit[k] * (half >> k))

    def first(c, which):
        if c >= mains and which == 0:
            return None
        slot = own_r.at[c, which]
        return copy(source(c, which, 1 - bit[0]), slot, c, which, partner[0])

    def second(c):
        return copy(sent.at[c], halves[0].at[c], c, 2, across)

    def halving(c, k):
        size = half >> k
        src = parts[k - 1].at[c, pl.ds(mult((1 - bit[k]) * size), size), :]
        return copy(src, halves[k].at[c], c, 2 + k, partner[k])

    def doubling(c, k):
        size = half >> k
        place = target(c, offset[k], size)
        return copy(place, place, c, 2 + bits + k, partner[k])

    def f32(ref):
        return ref[...].astype(F32)

    def stage(c, s):
        if s == 0:
            for which in (0, 1):
                rdma = first(c, which)
                if rdma is not None:
                    rdma.start()
        elif s == 1:
            first(c, 1).wait_recv()
            sent[c] = (f32(source(c, 1, bit[0])) + f32(own_r.at[c, 1])).astype(BF)
            second(c).start()
        elif s == 2:
            second(c).wait_recv()
            if c >= mains:
                total = f32(sent.at[c]) + f32(halves[0].at[c])
            else:
                first(c, 0).wait_recv()
                total = f32(source(c, 0, bit[0])) + f32(own_r.at[c, 0]) + f32(halves[0].at[c])
            parts[0][c] = total.astype(BF)
            halving(c, 1).start()
        elif s < bits + 2:
            k = s - 2
            size = half >> k
            halving(c, k).wait_recv()
            kept = parts[k - 1].at[c, pl.ds(mult(bit[k] * size), size), :]
            total = (f32(kept) + f32(halves[k].at[c])).astype(BF)
            if k < bits - 1:
                parts[k][c] = total
                halving(c, k + 1).start()
            else:
                target(c, offset[k], size)[...] = total
                doubling(c, k).start()
        else:
            k = 2 * bits + 1 - s
            doubling(c, k).wait_recv()
            if k > 0:
                doubling(c, k - 1).start()

    def tiny_copy(k):
        return pltpu.make_async_remote_copy(
            src_ref=tiny if k == 0 else tiny_s.at[k - 1],
            dst_ref=tiny_r.at[k],
            send_sem=tsend_s.at[k],
            recv_sem=trecv_s.at[k],
            device_id=stages[k],
            device_id_type=pl.DeviceIdType.MESH,
        )

    tiny_copy(0).start()
    last = 2 * bits + 1
    for tick in range(n + SLACK * last):
        for s in range(last, -1, -1):
            c = tick - SLACK * s
            if 0 <= c < n:
                stage(c, s)
        if 1 <= tick <= bits + 1:
            k = tick - 1
            tiny_copy(k).wait_recv()
            before = tiny[...] if k == 0 else tiny_s[k - 1]
            total = before + tiny_r[k]
            if k < bits:
                tiny_s[k] = total
                tiny_copy(k + 1).start()
            else:
                tiny_o[...] = total

    low_half = lanes_of(rows) < HEAD_DIM
    for p in range(width // 128):
        sl = slice(p * 128, (p + 1) * 128)
        g, v = f32(outs[0].at[:, sl]), f32(outs[1].at[:, sl])
        paired_o[:, 2 * p * 128 : (2 * p + 1) * 128] = jnp.where(low_half, g, pltpu.roll(v, 64, 1))
        paired_o[:, (2 * p + 1) * 128 : (2 * p + 2) * 128] = jnp.where(
            low_half, pltpu.roll(g, 64, 1), v
        )

    for c in range(n):
        for which in (0, 1):
            rdma = first(c, which)
            if rdma is not None:
                rdma.wait_send()
        second(c).wait_send()
        for k in range(1, bits):
            halving(c, k).wait_send()
        for k in range(bits):
            doubling(c, k).wait_send()
    for k in range(bits + 1):
        tiny_copy(k).wait_send()


def reduce_all(bits, mats, both, tiny, lanes):
    kinds = [kind for _, kind in mats]
    arrays = [a for a, _ in mats]
    rows = arrays[0].shape[0] if kinds[0] == "cols" else arrays[0].shape[0] // 2
    width = arrays[0].shape[1] // 2 if kinds[0] == "cols" else arrays[0].shape[1]
    half = rows // 2
    n = len(arrays) * (width // lanes) + both.shape[1] // lanes
    vmem = pl.BlockSpec(memory_space=pltpu.VMEM)
    sds = jax.ShapeDtypeStruct
    scratch = [pltpu.VMEM((rows, width), BF)] * 2
    scratch += [pltpu.VMEM((n, 2, half, lanes), BF), pltpu.VMEM((n, half, lanes), BF)]
    scratch += [pltpu.VMEM((n, half >> k, lanes), BF) for k in range(bits)]
    scratch += [pltpu.VMEM((n, half >> k, lanes), BF) for k in range(bits - 1)]
    scratch += [
        pltpu.VMEM((bits + 1,) + tiny.shape, F32),
        pltpu.VMEM((bits,) + tiny.shape, F32),
        pltpu.SemaphoreType.DMA((n, 2 + 2 * bits)),
        pltpu.SemaphoreType.DMA((n, 2 + 2 * bits)),
        pltpu.SemaphoreType.DMA((bits + 1,)),
        pltpu.SemaphoreType.DMA((bits + 1,)),
    ]
    return pl.pallas_call(
        functools.partial(reduce_kernel, bits, lanes, kinds),
        out_shape=[
            sds((rows, 2 * width), F32), sds((rows, width), BF), sds(both.shape, BF), sds(tiny.shape, F32)
        ],
        in_specs=[vmem] * (len(arrays) + 2),
        out_specs=[vmem] * 4,
        scratch_shapes=scratch,
        compiler_params=pltpu.CompilerParams(
            collective_id=0, has_side_effects=True, vmem_limit_bytes=58 * 1024 * 1024
        ),
        name="reduce_all",
    )(*arrays, both, tiny)


def spread_heads(v):
    padded = jnp.zeros((GROUP,), F32).at[: v.shape[0]].set(v)
    return jnp.tile(padded, 4)[None]


def handed(total, passed, shards, up):
    pairs = [(k, k + 1) if up else (k + 1, k) for k in range(shards - 1)]
    entering = lax.ppermute(total.astype(BF), "chan", pairs)
    for _ in range(shards - 2):
        now = total + passed[0:1] * entering.astype(F32)
        entering = lax.ppermute(now.astype(BF), "chan", pairs)
    return entering


def swap(v):
    return lax.ppermute(v, "chan", [(0, 1), (1, 0)])


def core_swap(v):
    size = lax.axis_size("dp")
    return lax.ppermute(v, "dp", [(k, k ^ 1) for k in range(size)])


def on_device(
    hidden_in, norm_gain, gate_value_weight, state_weight, step_weight, value_conv, state_conv,
    step_bias, decay_log, skip_gain, gate_gain, out_weight, seq_length, seq_count, out_grad,
):
    tokens, width_in = hidden_in.shape
    channel = lax.axis_index("chan")
    shards = lax.axis_size("chan")
    groups_dp = lax.axis_size("dp")
    length, count = seq_length[0], seq_count[0]
    local_heads = gate_value_weight.shape[1]
    local = local_heads * HEAD_DIM
    heads = local_heads * shards
    width = heads * HEAD_DIM
    paired = shards == 2 and local % 128 == 0 and groups_dp % 2 == 0
    one = jnp.ones((), jnp.int32)
    flags = [channel, 1 - channel, 1 - channel, channel] if paired else [one] * 4
    sc = jnp.stack([channel * tokens, length, count] + flags).astype(jnp.int32)
    ups = [(k, k + 1) for k in range(shards - 1)]
    downs = [(k + 1, k) for k in range(shards - 1)]
    gain = norm_gain[None]

    wg = gate_value_weight[:, :, :HEAD_DIM].reshape(width_in, local)
    wv = gate_value_weight[:, :, HEAD_DIM:].reshape(width_in, local)
    edge = lax.ppermute(hidden_in[tokens - PAD :], "chan", ups)
    vec = jnp.concatenate([step_bias, decay_log, skip_gain])
    small = jnp.concatenate(
        [
            value_conv,
            gate_gain[None],
            jnp.pad(vec, (0, local - 3 * local_heads))[None],
        ]
    )

    def step_matrix(steps):
        return jnp.tile(jnp.pad(steps, ((0, 0), (0, GROUP - steps.shape[1]))), (1, 4))

    each_map = expanders(heads)
    e0, e1, e2, _ = [jnp.asarray(e, BF) for e in each_map]
    e01 = jnp.asarray(by_pairs(each_map[:2], 1), BF)
    maps = (gain, state_weight, state_conv)
    if paired:
        first_core = lax.axis_index("dp") % 2 == 0
        payload, edge = lax.optimization_barrier((jnp.where(first_core, wg, wv), edge))
        come = swap(payload)
        small_b, wstep_b, ow_b = swap(small), swap(step_weight), swap(out_weight)
        gate, v, xpre, ff, sbl, pb, _, _, _, _, hand, vh, normed, nedge, ps, pspre, bc, psh = project(
            sc, hidden_in, edge, wg, wv, step_matrix(step_weight), value_conv,
            spread_heads(step_bias), spread_heads(-jnp.exp(decay_log) * LOG2E),
            e0[:, :local], e1[:, :local], maps=maps, final=False,
        )
        come, small_b, wstep_b, ow_b, nedge, hand = lax.optimization_barrier(
            (come, small_b, wstep_b, ow_b, nedge, hand)
        )
        also = core_swap(come)
        enter_b = swap(hand)
        wgs = [wg, jnp.where(first_core, come, also)]
        wvs = [wv, jnp.where(first_core, also, come)]
        smalls = [small, small_b]
        wstep = jnp.concatenate([step_weight, wstep_b], axis=1)
        ow = jnp.concatenate([out_weight, ow_b], axis=0)
    else:
        wgs = [lax.all_gather(wg, "chan", axis=1, tiled=True)]
        wvs = [lax.all_gather(wv, "chan", axis=1, tiled=True)]
        gathered = lax.all_gather(small, "chan", axis=0)
        smalls = [gathered[k] for k in range(shards)]
        wstep = lax.all_gather(step_weight, "chan", axis=1, tiled=True)
        ow = lax.all_gather(out_weight, "chan", axis=0, tiled=True)

    def heads_row(k, parts):
        lo, hi = k * local_heads, (k + 1) * local_heads
        return jnp.concatenate([p[TAPS + 1, lo:hi] for p in parts])

    bias_all, dlog_all, skip_all = (heads_row(k, smalls) for k in range(3))
    cv = jnp.concatenate([p[:TAPS] for p in smalls], axis=1)
    ggain = jnp.concatenate([p[TAPS : TAPS + 1] for p in smalls], axis=1)
    skip = jnp.repeat(skip_all, HEAD_DIM)[None]
    nad = -jnp.exp(dlog_all)

    if paired:
        gate2, v2, xpre2, ff2, sbl2, pb2, _, _, _, _, hand2, vh2, col, row = project(
            sc, normed, nedge, wgs[1], wvs[1], step_matrix(wstep), smalls[1][:TAPS],
            spread_heads(bias_all), spread_heads(nad * LOG2E),
            e0[:, local:], e1[:, local:], bc=bc, final=True,
        )
        enter = [swap(hand2), enter_b]
        split = [[gate, gate2], [xpre, xpre2], [ff, ff2], [sbl, sbl2], [pb, pb2], enter, enter]
        vs, xs = [v, v2], [xpre, xpre2]
        vh = jnp.concatenate([vh, vh2], axis=1)
    else:
        (
            gate, v, xpre, ff, sbl, pb, sft, sbt, pft, pbt, _, vh, normed, nedge, ps, pspre, bc, psh,
            col, row,
        ) = project(
            sc, hidden_in, edge, wgs[0], wvs[0], step_matrix(wstep), cv, spread_heads(bias_all),
            spread_heads(nad * LOG2E), e0, e1, maps=maps,
        )
        sfd = handed(sft, pft, shards, True)
        sbd = handed(sbt, pbt, shards, False)
        split = [[gate], [xpre], [ff], [sbl], [pb], [sfd], [sbd]]
        vs, xs = [v], [xpre]
    (
        output, gnorm, dy, dgate, sf, sb, gbl, pg, dff, gft, gbt, pgf, pgb, hand, ggain_grad, skip_grad,
    ) = mix(sc, split, bc, col, row, hidden_in, out_grad, ow, ow.T, ggain, skip, e01, e2)
    if paired:
        enter = swap(hand)
        enter = [enter[:, local:], enter[:, :local]]
        gfds = gbds = enter
    else:
        gfds = [handed(gft, pgf, shards, False)]
        gbds = [handed(gbt, pgb, shards, True)]

    own_ids = channel * tokens + jnp.arange(tokens, dtype=jnp.int32)
    live = jnp.where(own_ids // length < count, 1.0, 0.0)[:, None].astype(BF)
    ow_grad = dot_tn(gnorm, out_grad * live).astype(BF)
    dwg = dot_tn(normed, dgate).astype(BF)

    def absolute(parts, axis):
        if not paired:
            return jnp.concatenate(parts, axis=axis)
        a = jnp.concatenate(parts, axis=axis)
        b = jnp.concatenate(parts[::-1], axis=axis)
        return jnp.where(channel == 0, a, b)

    def shared(v, axis):
        if paired:
            a, b = jnp.split(v, 2, axis=axis)
            v = (a.astype(F32) + swap(b).astype(F32)).astype(BF)
        else:
            v = lax.psum_scatter(v, "chan", scatter_dimension=axis, tiled=True)
        return lax.psum(v, "dp")

    dv, dst, dz, cvg, csg, head_sums, edge_g, edges_g = back(
        heads, sc, [xs, vs, gfds, gbds], dy, bc, ps, pspre, col, row, sf, sb, gbl, pg, dff, skip, cv,
        state_conv, spread_heads(nad),
    )

    if paired:
        turned = jnp.concatenate([edge_g[:, local:], edge_g[:, :local]], axis=1)
    else:
        turned = edge_g
    kernel = jnp.concatenate([cv, state_conv], axis=1)
    past = jnp.concatenate([vh, psh], axis=1)
    reach = TAPS - 1
    after = lax.ppermute(jnp.concatenate([turned, edges_g], axis=1), "chan", downs)[:reach]
    joined = jnp.concatenate([edge_g, edges_g], axis=1)
    after = after * jnp.where(((channel + 1) * tokens) % length == 0, 0.0, 1.0)
    patch = jnp.zeros((reach, joined.shape[1]), F32)
    taps = []
    for j in range(TAPS):
        if j:
            moved = jnp.pad(after[:j], ((reach - j, 0), (0, 0)))
            patch = patch + moved * kernel[TAPS - 1 - j][None]
        taps.append(jnp.sum(joined[:j] * past[PAD - j :], axis=0))
    cross_taps = jnp.stack(taps[::-1])
    tail = jnp.pad(patch, ((PAD - reach, 0), (0, 0))).astype(BF)
    dv = dv.at[tokens - PAD :].add(tail[:, :width])
    dst = dst.at[tokens - PAD :].add(tail[:, width:])
    cvg = cvg + cross_taps[:, :width]
    csg = csg + cross_taps[:, width:]

    dwv = dot_tn(normed, dv).astype(BF)
    dws = dot_tn(normed, dst)
    dwst = dot_tn(normed, dz)[:, 96 : 96 + heads]
    wst_tail = jnp.pad(wstep, ((0, 0), (96, GROUP - heads)))
    input_grad, norm_gain_grad = input_side(
        wgs, wvs, dgate, dv, dst, dz, state_weight, wst_tail, gain, hidden_in, out_grad
    )

    bias_sum = head_sums[1, 96 : 96 + heads]
    dlog_sum = head_sums[0, 64 : 64 + heads]
    skip_sum = skip_grad.reshape(heads, HEAD_DIM).sum(axis=1)

    def by_shard(k):
        cut, hcut = slice(k * local, (k + 1) * local), slice(k * local_heads, (k + 1) * local_heads)
        return jnp.concatenate(
            [cvg[:, cut].reshape(-1), ggain_grad[0, cut], bias_sum[hcut], dlog_sum[hcut], skip_sum[hcut]]
        )

    each = (TAPS + 1) * local + 3 * local_heads
    pad_each = -each % 128
    tiny = absolute([jnp.pad(by_shard(k), (0, pad_each)) for k in range(shards)], 0)
    tiny = jnp.concatenate([tiny, norm_gain_grad[0], csg.reshape(-1)])
    tiny = jnp.pad(tiny, (0, -tiny.shape[0] % 1024)).reshape(-1, 128)
    dwst = absolute([dwst[:, k * local_heads : (k + 1) * local_heads] for k in range(shards)], 1)
    both = jnp.concatenate([dws, jnp.pad(dwst, ((0, 0), (0, 128 - heads)))], axis=1).astype(BF)

    bits = groups_dp.bit_length() - 1
    if paired and groups_dp == 2**bits and bits >= 2 and width_in % (16 * groups_dp) == 0:
        gvw, owg, both, tiny = reduce_all(
            bits, [(dwg, "cols"), (dwv, "cols"), (ow_grad, "rows")], both, tiny, LANES
        )
        gvw = gvw.reshape(width_in, local_heads, 2 * HEAD_DIM)
        owg = owg.astype(F32)
    else:
        dwg, dwv, owg = shared(dwg, 1), shared(dwv, 1), shared(ow_grad, 0).astype(F32)
        both, tiny = lax.psum((both, tiny), ("dp", "chan"))
        pieces = [a.reshape(width_in, local_heads, HEAD_DIM) for a in (dwg, dwv)]
        gvw = jnp.concatenate(pieces, axis=2).astype(F32)
    both = both.astype(F32)
    flat = tiny.reshape(-1)
    base = (each + pad_each) * shards
    mine = lax.dynamic_slice_in_dim(flat, channel * (each + pad_each), each, 0)
    cuts = np.cumsum([TAPS * local, local, local_heads, local_heads])
    dwst = lax.dynamic_slice_in_dim(both[:, 128:], channel * local_heads, local_heads, 1)
    return (
        output,
        input_grad,
        flat[base : base + width_in],
        gvw,
        both[:, :128],
        dwst,
        mine[: cuts[0]].reshape(TAPS, local),
        flat[base + width_in : base + width_in + TAPS * 128].reshape(TAPS, 128),
        mine[cuts[1] : cuts[2]],
        mine[cuts[2] : cuts[3]],
        mine[cuts[3] :],
        mine[cuts[0] : cuts[1]],
        owg,
    )


def solution(mesh):
    in_specs = (
        P(("dp", "chan"), None),
        P(),
        P(None, "chan", None),
        P(),
        P(None, "chan"),
        P(None, "chan"),
        P(),
        P("chan"),
        P("chan"),
        P("chan"),
        P("chan"),
        P("chan", None),
        P("dp"),
        P("dp"),
        P(("dp", "chan"), None),
    )
    out_specs = (
        P(("dp", "chan"), None),
        P(("dp", "chan"), None),
        P(),
        P(None, "chan", None),
        P(),
        P(None, "chan"),
        P(None, "chan"),
        P(),
        P("chan"),
        P("chan"),
        P("chan"),
        P("chan"),
        P("chan", None),
    )
    return jax.shard_map(
        on_device, mesh=mesh, in_specs=in_specs, out_specs=out_specs, check_vma=False
    )
```

```python
import functools

import jax
import jax.numpy as jnp
import numpy as np
from jax import lax
from jax.experimental import pallas as pl
from jax.experimental.pallas import tpu as pltpu
from jax.sharding import PartitionSpec as P

HEAD_DIM = 64
STATE = 64
SPAN = 128
PAD = 16
GROUP = 32
TAPS = 4
LANES = 128
SLACK = 2
EPS = 1e-05
LOG2E = float(np.log2(np.e))
BF = jnp.bfloat16
F32 = jnp.float32


def dot(a, b):
    return jnp.dot(a, b, preferred_element_type=F32)


def dot_nt(a, b):
    return lax.dot_general(a, b, (((1,), (1,)), ((), ())), preferred_element_type=F32)


def dot_tn(a, b):
    return lax.dot_general(a, b, (((0,), (0,)), ((), ())), preferred_element_type=F32)


def fine_nt(a, b):
    return lax.dot_general(
        a, b, (((1,), (1,)), ((), ())), precision=lax.Precision.HIGHEST, preferred_element_type=F32
    )


def sigmoid(v):
    return 0.5 + 0.5 * jnp.tanh(0.5 * v)


def lanes_of(rows):
    return lax.broadcasted_iota(jnp.int32, (rows, 128), 1)


def shifted(ext, offset, rows):
    return ext[offset : offset + rows]


def full(shape):
    rank = len(shape)
    return pl.BlockSpec(shape, lambda i: (0,) * rank)


SMEM = pl.BlockSpec(memory_space=pltpu.SMEM)


def cost(micros):
    return pl.CostEstimate(flops=int(micros * 1e9), bytes_accessed=1024, transcendentals=0)


def side(a, b):
    return jnp.concatenate([a, b], axis=1)


def high_low(v):
    hi = v.astype(BF)
    return side(hi, (v - hi.astype(F32)).astype(BF))


def by_pairs(maps, axis):
    pairs = maps[0].shape[axis] // 128
    pieces = [np.split(m, pairs, axis=axis) for m in maps]
    return np.concatenate([piece[p] for p in range(pairs) for piece in pieces], axis=axis)


def unpaired(a, b):
    low = lanes_of(a.shape[0]) < HEAD_DIM
    return jnp.where(low, a, pltpu.roll(b, 64, 1)), jnp.where(low, pltpu.roll(a, 64, 1), b)


def expanders(heads):
    channel = np.arange(heads * HEAD_DIM) // HEAD_DIM
    lane = np.arange(128)[:, None]
    return [np.asarray(lane == GROUP * g + channel[None], np.float32) for g in range(4)]


def project_kernel(fresh, final, tile, chunk, *refs):
    refs = list(refs)

    def take(count):
        return [refs.pop(0) for _ in range(count)]

    sc, tokens_r, halo, edge, slabs, wst, cv, bias, nal, tri, e0, e1 = take(12)
    if fresh:
        gain, ws, cs = take(3)
    else:
        (bc_r,) = take(1)
    gate_o, v_o, xpre_o, ff_o, sb_o, pb_o, sft_o, sbt_o, pft_o, pbt_o, hand_o, vh_o = take(12)
    if fresh:
        normed_o, nedge_o, ps_o, pspre_o, bc_o, psh_o = take(6)
    if final:
        col_o, row_o = take(2)
    sb_s, pb_s, sf_s, pf_s = take(4)

    step = pl.program_id(0)
    tiles = pl.num_programs(0)
    at = tiles - 1 - step
    length = sc[1]
    start = sc[0] + at * tile
    width = e0.shape[1]
    blocks = tile // SPAN

    @pl.when(step == 0)
    def _():
        sb_s[...] = jnp.zeros_like(sb_s)
        sf_s[...] = jnp.zeros_like(sf_s)
        pb_s[...] = jnp.ones_like(pb_s)
        pf_s[...] = jnp.ones_like(pf_s)

    before = jnp.where(at == 0, edge[...].astype(F32), halo[...].astype(F32))
    rows = jnp.concatenate([before, tokens_r[...].astype(F32)], axis=0)
    keep = jnp.where(lax.rem(start, length) == 0, 0.0, 1.0)
    row_id = lax.broadcasted_iota(jnp.int32, (tile + PAD, 1), 0)
    keep_rows = jnp.where(row_id < PAD, keep, 1.0)
    if fresh:
        scale = lax.rsqrt(jnp.mean(rows * rows, axis=1, keepdims=True) + EPS)
        normed = (rows * scale * gain[...]).astype(BF)
        own = normed[PAD:]
        normed_o[...] = own

        ps = dot(normed, ws[...]) * keep_rows
        ps_o[...] = ps[PAD:]
        pspre = ps[PAD:] * cs[TAPS - 1 : TAPS]
        for j in range(1, TAPS):
            pspre = pspre + shifted(ps, PAD - j, tile) * cs[TAPS - 1 - j : TAPS - j]
        pspre_o[...] = pspre
        bc = pspre * sigmoid(pspre)
        bc_o[...] = bc

        @pl.when(at == 0)
        def _():
            nedge_o[...] = normed[:PAD]
            psh_o[...] = ps[:PAD]

    else:
        normed = rows.astype(BF)
        own = tokens_r[...]
        bc = bc_r[...]

    z = dot(own, wst[...]) + bias[...]
    dt = jnp.maximum(z, 0.0) + jnp.log1p(jnp.exp(-jnp.abs(z)))
    a2 = dt * nal[...]
    lane = lanes_of(SPAN)
    if final:
        sig = sigmoid(z)
    wmix, bts = [], []
    for b in range(blocks):
        sl = slice(b * SPAN, (b + 1) * SPAN)
        ab = a2[sl]
        ca = jnp.dot(tri[...], ab, precision=lax.Precision.HIGHEST, preferred_element_type=F32)
        ce = ca - ab
        if final:
            col = jnp.where(
                lane < 32, ca, jnp.where(lane < 64, ce, jnp.where(lane < 96, dt[sl], sig[sl]))
            )
            col_o[sl, :] = col
            row_o[sl, :] = jnp.transpose(col)
        end = ca[SPAN - 1 : SPAN]
        w = jnp.exp2(jnp.where(lane < 32, end - ca, ce)) * dt[sl]
        dec = jnp.broadcast_to(jnp.exp2(end), (8, 128))
        high = dec.astype(BF).astype(F32)
        wmix.append(jnp.concatenate([w, high, dec - high], axis=0).astype(BF))
        bts.append(jnp.transpose(bc[sl])[:STATE].astype(BF))

    for c in range(width // chunk):
        cl = slice(c * chunk, (c + 1) * chunk)
        parts = []
        for h in range(c * chunk // HEAD_DIM, (c + 1) * chunk // HEAD_DIM, 2):
            both = dot(normed, side(slabs[h], slabs[h + 1]))
            parts.append(unpaired(both[:, :128], both[:, 128:]))
        gates = jnp.concatenate([part[0][PAD:] for part in parts], axis=1)
        gate_o[:, cl] = gates.astype(BF)
        v = jnp.concatenate([part[1] for part in parts], axis=1) * keep_rows
        v_o[:, cl] = v[PAD:].astype(BF)

        @pl.when(at == 0)
        def _():
            vh_o[:, cl] = v[:PAD]

        xpre = v[PAD:] * cv[TAPS - 1 : TAPS, cl]
        for j in range(1, TAPS):
            xpre = xpre + shifted(v, PAD - j, tile) * cv[TAPS - 1 - j : TAPS - j, cl]
        xpre_o[:, cl] = xpre.astype(BF)
        x = xpre * sigmoid(xpre)
        for b in reversed(range(blocks)):
            sl = slice(b * SPAN, (b + 1) * SPAN)
            we = dot(wmix[b], e0[:, cl])
            wbe = dot(wmix[b][:SPAN], e1[:, cl])
            dec = we[SPAN : SPAN + 1] + we[SPAN + 8 : SPAN + 9]
            xb = x[sl]
            fresh_f = dot(bts[b], (xb * we[:SPAN]).astype(BF))
            fresh_b = dot(bts[b], (xb * wbe).astype(BF))
            place = start + b * SPAN
            first = jnp.where(lax.rem(place, length) == 0, 0.0, 1.0)
            last = jnp.where(lax.rem(place + SPAN, length) == 0, 0.0, 1.0)
            ff_o[b, :, cl] = fresh_f.astype(BF)
            pf = pf_s[0:1, cl]
            sf_s[:, cl] = sf_s[:, cl] + pf * fresh_f
            pf_s[:, cl] = jnp.broadcast_to(pf * dec * first, (8, chunk))
            held = sb_s[:, cl] * last
            pb = pb_s[0:1, cl] * last
            sb_o[b, :, cl] = held.astype(BF)
            pb_o[b, :, cl] = jnp.broadcast_to(pb, (8, chunk))
            sb_s[:, cl] = held * dec + fresh_b
            pb_s[:, cl] = jnp.broadcast_to(pb * dec, (8, chunk))

    @pl.when(at == 0)
    def _():
        sft_o[...] = sf_s[...]
        sbt_o[...] = sb_s[...]
        pft_o[...] = pf_s[...]
        pbt_o[...] = pb_s[...]
        hand_o[...] = jnp.where(sc[0] == 0, sf_s[...], sb_s[...]).astype(BF)


def project(sc, source, edge, slabs, wst, cv, bias, nal, e0, e1, maps=None, bc=None, final=True):
    fresh = maps is not None
    tokens, width_in = source.shape
    width = slabs.shape[0] * HEAD_DIM
    tile = min(256, tokens)
    tiles = tokens // tile
    per = tile // SPAN
    blocks = tokens // SPAN
    chunk = 256 if width % 256 == 0 else 128
    tri = np.tril(np.ones((SPAN, SPAN), np.float32))

    def back(shape):
        rank = len(shape)
        return pl.BlockSpec(shape, lambda i: (tiles - 1 - i,) + (0,) * (rank - 1))

    sds = jax.ShapeDtypeStruct
    wide = (sds((tokens, width), BF), back((tile, width)))
    narrow = (sds((tokens, 128), F32), back((tile, 128)))
    held = (sds((blocks, STATE, width), BF), back((per, STATE, width)))
    total = (sds((STATE, width), F32), full((STATE, width)))
    passed = (sds((8, width), F32), full((8, width)))
    outs = [wide, wide, wide, held, held, (sds((blocks, 8, width), F32), back((per, 8, width)))]
    outs += [total, total, passed, passed, (sds((STATE, width), BF), full((STATE, width)))]
    outs += [(sds((PAD, width), F32), full((PAD, width)))]
    if fresh:
        outs += [
            (sds((tokens, width_in), BF), back((tile, width_in))),
            (sds((PAD, width_in), BF), full((PAD, width_in))),
            narrow,
            narrow,
            narrow,
            (sds((PAD, 128), F32), full((PAD, 128))),
        ]
    if final:
        outs += [narrow, narrow]
    steps = tile // PAD
    args = [sc, source, source, edge, slabs, wst, cv, bias, nal, tri, e0, e1]
    in_specs = [
        SMEM,
        back((tile, width_in)),
        pl.BlockSpec((PAD, width_in), lambda i: (jnp.maximum((tiles - 1 - i) * steps - 1, 0), 0)),
    ] + [full(a.shape) for a in args[3:]]
    if fresh:
        args += list(maps)
        in_specs += [full(a.shape) for a in maps]
    else:
        args += [bc]
        in_specs += [back((tile, 128))]
    return pl.pallas_call(
        functools.partial(project_kernel, fresh, final, tile, chunk),
        grid=(tiles,),
        in_specs=in_specs,
        out_specs=[spec for _, spec in outs],
        out_shape=[shape for shape, _ in outs],
        scratch_shapes=[
            pltpu.VMEM((STATE, width), F32),
            pltpu.VMEM((8, width), F32),
            pltpu.VMEM((STATE, width), F32),
            pltpu.VMEM((8, width), F32),
        ],
        compiler_params=pltpu.CompilerParams(vmem_limit_bytes=58 * 1024 * 1024),
        cost_estimate=cost(28),
        name="project",
    )(*args)


def split_refs(refs, groups, kinds):
    taken = [[refs.pop(0) for _ in range(groups)] for _ in range(kinds)]
    return [functools.partial(pick, refs_of) for refs_of in taken]


def pick(refs_of, p):
    per = refs_of[0].shape[-1] // 128
    return refs_of[p // per], slice((p % per) * 128, (p % per + 1) * 128)


def mix_kernel(groups, *refs):
    refs = list(refs)
    sc = refs.pop(0)
    gates, xpres, ffs, sbls, pbs, sfds, sbds = split_refs(refs, groups, 7)
    mix_body(sc, gates, xpres, ffs, sbls, pbs, sfds, sbds, *refs)


def mix_body(
    sc, gates, xpres, ffs, sbls, pbs, sfds, sbds,
    bc_r, col_r, row_r, hid, gout, ow, owt, ggain, skip, e01,
    out_o, gnorm_o, dy_o, dgate_o, sf_o, sb_o, gbl_o, pg_o, dff_o,
    gft_o, gbt_o, pgf_o, pgb_o, hand_o, ggain_o, skip_o,
    sf_s, gb_s, gf_s, pg_s, q_s, y_s, dgn_s, exp_s,
):
    i = pl.program_id(0)
    length = sc[1]
    place = sc[0] + i * SPAN
    first = jnp.where(lax.rem(place, length) == 0, 0.0, 1.0)
    last = jnp.where(lax.rem(place + SPAN, length) == 0, 0.0, 1.0)
    live = jnp.where(lax.div(place, length) < sc[2], 1.0, 0.0)
    width = e01.shape[1] // 2
    pairs = width // 128

    @pl.when(i == 0)
    def _():
        enters_f = jnp.where(sc[3] == 1, 1.0, 0.0)
        for p in range(pairs):
            ref, at = sfds(p)
            sf_s[:, p * 128 : (p + 1) * 128] = ref[:, at].astype(F32) * enters_f
        gb_s[...] = jnp.zeros_like(gb_s)
        gf_s[...] = jnp.zeros_like(gf_s)
        pg_s[...] = jnp.ones_like(pg_s)
        q_s[...] = jnp.ones_like(q_s)
        ggain_o[...] = jnp.zeros_like(ggain_o)
        skip_o[...] = jnp.zeros_like(skip_o)

    enters_b = jnp.where(sc[4] == 1, 1.0, 0.0)
    glow = gout[...].astype(F32) * live
    gl = glow.astype(BF)
    dgn_s[...] = dot(gl, owt[...])

    lane = lanes_of(SPAN)
    low_half = lane < HEAD_DIM
    col = col_r[...]
    row = row_r[...]
    end = jnp.broadcast_to(col[SPAN - 1 : SPAN], (8, 128))
    end1 = pltpu.roll(end, GROUP, 1)
    w = jnp.exp2(jnp.where(lane < 32, col, end1[0:1] - col))
    dec = jnp.exp2(end)
    high = dec.astype(BF).astype(F32)
    wmix = jnp.concatenate([w, pltpu.roll(col, 64, 1), high, dec - high], axis=0).astype(BF)
    bc = bc_r[...]
    bmf, cmf = bc[:, :STATE], bc[:, STATE:]
    cm = cmf.astype(BF)
    ct = jnp.transpose(bc)[STATE:].astype(BF)
    square_r = lax.broadcasted_iota(jnp.int32, (SPAN, SPAN), 0)
    aff = jnp.where(square_r == lane, 0.0, fine_nt(cmf, bmf))

    squares = jnp.zeros((SPAN, 128), F32)
    for p in range(pairs):
        sl = slice(p * 128, (p + 1) * 128)
        efd = dot(wmix, e01[:, p * 256 : (p + 1) * 256])
        ef, eb = efd[:SPAN, :128], efd[:SPAN, 128:]
        dte = efd[SPAN : 2 * SPAN, :128]
        exp_s[0, :, sl] = ef
        exp_s[1, :, sl] = eb
        decay = efd[2 * SPAN : 2 * SPAN + 1, :128] + efd[2 * SPAN + 8 : 2 * SPAN + 9, :128]
        exp_s[2, 0:8, sl] = jnp.broadcast_to(decay, (8, 128))
        sf = sf_s[:, sl] * first
        sfb = sf.astype(BF)
        sf_o[0, :, sl] = sfb
        sbl, at = sbls(p)
        pb, sbd, ff, xpre, gate = (r(p)[0] for r in (pbs, sbds, ffs, xpres, gates))
        arrived = sbd[:, at].astype(F32) * enters_b
        sb = (sbl[0, :, at].astype(F32) + pb[0, 0:1, at] * arrived) * last
        sbb = sb.astype(BF)
        sb_o[0, :, sl] = sbb
        sf_s[:, sl] = sf * decay + ff[0, :, at].astype(F32)
        xp = xpre[:, at].astype(F32)
        x = xp * sigmoid(xp)
        xd = x * dte
        bd = jnp.concatenate(
            [jnp.where(low_half, xd, 0.0), jnp.where(low_half, 0.0, xd)], axis=0
        ).astype(BF)
        ms = []
        for h in (2 * p, 2 * p + 1):
            spread = jnp.minimum(
                col[:, h : h + 1] - row[h : h + 1, :],
                row[GROUP + h : GROUP + h + 1, :] - col[:, GROUP + h : GROUP + h + 1],
            )
            ms.append((aff * jnp.exp2(spread)).astype(BF))
        y = dot(jnp.concatenate(ms, axis=1), bd)
        carried = dot(cm, side(sfb, sbb))
        y = y + ef * carried[:, :128] + eb * carried[:, 128:] + skip[:, sl] * x
        y_s[:, sl] = y
        g = gate[:, at].astype(F32)
        gated = y * (g * sigmoid(g))
        squares = squares + gated * gated

    gsc = lax.rsqrt(jnp.sum(squares, axis=1, keepdims=True) * (1.0 / width) + EPS)
    inner = jnp.zeros((SPAN, 128), F32)
    for p in range(pairs):
        sl = slice(p * 128, (p + 1) * 128)
        gate, at = gates(p)
        g = gate[:, at].astype(F32)
        gunit = y_s[:, sl] * (g * sigmoid(g)) * gsc
        gnorm_o[:, sl] = (gunit * ggain[:, sl]).astype(BF)
        dgn = dgn_s[:, sl]
        dgu = dgn * gunit
        ggain_o[:, sl] += jnp.sum(dgu, axis=0, keepdims=True)
        inner = inner + dgu * ggain[:, sl]
    mean = jnp.sum(inner, axis=1, keepdims=True) * (1.0 / width)
    out_o[...] = (hid[...].astype(F32) + live * dot(gnorm_o[...], ow[...])).astype(BF)

    for p in range(pairs):
        sl = slice(p * 128, (p + 1) * 128)
        gate, at = gates(p)
        g = gate[:, at].astype(F32)
        sg = sigmoid(g)
        act = g * sg
        y = y_s[:, sl]
        gunit = y * act * gsc
        dgated = gsc * (dgn_s[:, sl] * ggain[:, sl] - gunit * mean)
        dy = dgated * act
        dy_o[:, sl] = dy.astype(BF)
        dgate_o[:, sl] = (dgated * y * (sg * (1.0 + g * (1.0 - sg)))).astype(BF)
        xp = xpres(p)[0][:, at].astype(F32)
        skip_o[:, sl] += jnp.sum(dy * (xp * sigmoid(xp)), axis=0, keepdims=True)
        decay = exp_s[2, 0:1, sl]
        states = dot(ct, side(exp_s[0, :, sl] * dy, exp_s[1, :, sl] * dy).astype(BF))
        dff, dfb = states[:, :128], states[:, 128:]
        dff_o[0, :, sl] = dff.astype(BF)
        q = q_s[0:1, sl]
        gf_s[:, sl] = gf_s[:, sl] + q * dff
        q_s[:, sl] = jnp.broadcast_to(q * decay * last, (8, 128))
        gb = gb_s[:, sl] * first
        pg = pg_s[0:1, sl] * first
        gbl_o[0, :, sl] = gb.astype(BF)
        pg_o[0, :, sl] = jnp.broadcast_to(pg, (8, 128))
        gb_s[:, sl] = gb * decay + dfb
        pg_s[:, sl] = jnp.broadcast_to(pg * decay, (8, 128))

    @pl.when(i == pl.num_programs(0) - 1)
    def _():
        gft_o[...] = gf_s[...]
        gbt_o[...] = gb_s[...]
        pgf_o[...] = q_s[...]
        pgb_o[...] = pg_s[...]
        hand_o[...] = jnp.where(sc[0] == 0, gb_s[...], gf_s[...]).astype(BF)


def mix(sc, split, bc, col, row, hidden, out_grad, ow, owt, ggain, skip, e01):
    tokens, width_in = hidden.shape
    groups = len(split[0])
    width = e01.shape[1] // 2
    part = width // groups
    blocks = tokens // SPAN

    def ahead(shape):
        rank = len(shape)
        return pl.BlockSpec(shape, lambda i: (i,) + (0,) * (rank - 1))

    sds = jax.ShapeDtypeStruct
    state = (1, STATE, width)
    outs = [
        (sds((tokens, width_in), BF), ahead((SPAN, width_in))),
        (sds((tokens, width), BF), ahead((SPAN, width))),
        (sds((tokens, width), BF), ahead((SPAN, width))),
        (sds((tokens, width), BF), ahead((SPAN, width))),
        (sds((blocks, STATE, width), BF), ahead(state)),
        (sds((blocks, STATE, width), BF), ahead(state)),
        (sds((blocks, STATE, width), BF), ahead(state)),
        (sds((blocks, 8, width), F32), ahead((1, 8, width))),
        (sds((blocks, STATE, width), BF), ahead(state)),
        (sds((STATE, width), F32), full((STATE, width))),
        (sds((STATE, width), F32), full((STATE, width))),
        (sds((8, width), F32), full((8, width))),
        (sds((8, width), F32), full((8, width))),
        (sds((STATE, width), BF), full((STATE, width))),
        (sds((1, width), F32), full((1, width))),
        (sds((1, width), F32), full((1, width))),
    ]
    shared = [ow, owt, ggain, skip, e01]
    in_specs = [SMEM]
    for shape in (
        (SPAN, part), (SPAN, part), (1, STATE, part), (1, STATE, part), (1, 8, part),
    ):
        in_specs += [ahead(shape)] * groups
    in_specs += [full((STATE, part))] * (2 * groups)
    in_specs += [ahead((SPAN, 128))] * 3 + [ahead((SPAN, width_in))] * 2
    in_specs += [full(a.shape) for a in shared]
    return pl.pallas_call(
        functools.partial(mix_kernel, groups),
        grid=(blocks,),
        in_specs=in_specs,
        out_specs=[spec for _, spec in outs],
        out_shape=[shape for shape, _ in outs],
        scratch_shapes=[
            pltpu.VMEM((STATE, width), F32),
            pltpu.VMEM((STATE, width), F32),
            pltpu.VMEM((STATE, width), F32),
            pltpu.VMEM((8, width), F32),
            pltpu.VMEM((8, width), F32),
            pltpu.VMEM((SPAN, width), F32),
            pltpu.VMEM((SPAN, width), F32),
            pltpu.VMEM((3, SPAN, width), F32),
        ],
        compiler_params=pltpu.CompilerParams(vmem_limit_bytes=58 * 1024 * 1024),
        cost_estimate=cost(60),
        name="mix",
    )(sc, *[a for kind in split for a in kind], bc, col, row, hidden, out_grad, *shared)


def back_kernel(heads, groups, *refs):
    refs = list(refs)
    sc = refs.pop(0)
    xpres, vs, gfds, gbds = split_refs(refs, groups, 4)
    back_body(heads, sc, xpres, vs, gfds, gbds, *refs)


def back_body(
    heads, sc, xpres, vs, gfds, gbds,
    dy_r, bc_r, ps_r, pspre_r, col_r, row_r, sf_r, sb_r, gbl, pg, dff,
    skip, cv, cs, nad, e01, seg4, seg2, segs, tris,
    dv_o, dst_o, dz_o, cvg_o, csg_o, head_o, edge_o, edges_o,
    gf_s, edge_s, edges_s, da_s, cross_s,
):
    step = pl.program_id(0)
    blocks = pl.num_programs(0)
    i = blocks - 1 - step
    length = sc[1]
    place = sc[0] + i * SPAN
    last = jnp.where(lax.rem(place + SPAN, length) == 0, 0.0, 1.0)
    width = e01.shape[1] // 2
    pairs = width // 128

    @pl.when(step == 0)
    def _():
        enters_f = jnp.where(sc[5] == 1, 1.0, 0.0)
        for p in range(pairs):
            ref, at = gfds(p)
            gf_s[:, p * 128 : (p + 1) * 128] = ref[:, at].astype(F32) * enters_f
        edge_s[...] = jnp.zeros_like(edge_s)
        edges_s[...] = jnp.zeros_like(edges_s)
        da_s[...] = jnp.zeros_like(da_s)
        cvg_o[...] = jnp.zeros_like(cvg_o)
        csg_o[...] = jnp.zeros_like(csg_o)
        head_o[...] = jnp.zeros_like(head_o)

    lane = lanes_of(SPAN)
    low_half = lane < HEAD_DIM
    col = col_r[...]
    row = row_r[...]
    end = jnp.broadcast_to(col[SPAN - 1 : SPAN], (8, 128))
    end1 = pltpu.roll(end, GROUP, 1)
    w = jnp.where(lane < 64, jnp.exp2(jnp.where(lane < 32, col, end1[0:1] - col)), col)
    dec = jnp.exp2(end)
    high = dec.astype(BF).astype(F32)
    inner = jnp.exp2(jnp.where(lane < 32, end[0:1] - col, col))
    steps = pltpu.roll(col, 64, 1)
    wall = jnp.concatenate([w, inner, steps, high, dec - high], axis=0).astype(BF)
    bc = bc_r[...]
    bmf, cmf = bc[:, :STATE], bc[:, STATE:]
    bm, cm = bmf.astype(BF), cmf.astype(BF)
    enters_b = jnp.where(sc[6] == 1, 1.0, 0.0)
    square_r = lax.broadcasted_iota(jnp.int32, (SPAN, SPAN), 0)
    off = square_r != lane
    aff = jnp.where(off, fine_nt(bmf, cmf), 0.0)

    daff = jnp.zeros((SPAN, SPAN), F32)
    red = jnp.zeros((SPAN, 128), F32)
    whole = jnp.zeros((SPAN, 128), F32)
    ddt = jnp.zeros((SPAN, 128), F32)
    dc = jnp.zeros((SPAN, STATE), F32)
    db = jnp.zeros((SPAN, STATE), F32)
    for p in range(pairs):
        sl = slice(p * 128, (p + 1) * 128)
        two = slice(p * 256, (p + 1) * 256)
        efd = dot(wall, e01[:, two])
        ef, eb = efd[:SPAN, :128], efd[:SPAN, 128:]
        wf, wb = efd[SPAN : 2 * SPAN, :128], efd[SPAN : 2 * SPAN, 128:]
        dte = efd[2 * SPAN : 3 * SPAN, :128]
        decay = efd[3 * SPAN : 3 * SPAN + 1, :128] + efd[3 * SPAN + 8 : 3 * SPAN + 9, :128]
        sf, sb = sf_r[0, :, sl], sb_r[0, :, sl]
        gf32 = gf_s[:, sl] * last
        gbd, at = gbds(p)
        arrived = gbd[:, at].astype(F32) * enters_b
        gb32 = gbl[0, :, sl].astype(F32) + pg[0, 0:1, sl] * arrived
        gf, gb = gf32.astype(BF), gb32.astype(BF)
        gf_s[:, sl] = gf32 * decay + dff[0, :, sl].astype(F32)
        cross = (sf.astype(F32) * gf32 + sb.astype(F32) * gb32) * decay
        cross_s[:, sl] = jnp.broadcast_to(jnp.sum(cross, axis=0, keepdims=True), (8, 128))
        xp = xpres(p)[0][:, at].astype(F32)
        sg = sigmoid(xp)
        x = xp * sg
        xd = x * dte
        dy = dy_r[:, sl].astype(F32)
        efdy, ebdy = ef * dy, eb * dy
        wfxd, wbxd = wf * xd, wb * xd
        s_both, g_both = side(sf, sb), side(gf, gb)
        fed = dot(bm, g_both)
        cf, cb = wf * fed[:, :128], wb * fed[:, 128:]
        carried = dot(cm, s_both)
        edy = side(efdy, ebdy)
        dc = dc + dot_nt(edy.astype(BF), s_both)
        db = db + dot_nt(side(wfxd, wbxd).astype(BF), g_both)
        products = side((edy * carried).astype(BF), side(xd * cf, xd * cb).astype(BF))
        red = red + dot(products, seg4[p * 512 : (p + 1) * 512, :])
        bd = jnp.concatenate(
            [jnp.where(low_half, dy, 0.0), jnp.where(low_half, 0.0, dy)], axis=0
        ).astype(BF)
        dm = dot_nt(xd.astype(BF), bd)
        ms = []
        for k in range(2):
            h = 2 * p + k
            spread = jnp.minimum(
                row[h : h + 1, :] - col[:, h : h + 1],
                col[:, GROUP + h : GROUP + h + 1] - row[GROUP + h : GROUP + h + 1, :],
            )
            f = jnp.exp2(spread)
            m = aff * f
            ms.append(m.astype(BF))
            dmh = dm[:, k * 128 : (k + 1) * 128]
            daff = daff + f * dmh
            q = m * dmh
            ql = jnp.where(square_r < lane, q, 0.0)
            qu = q - ql
            da_s[h : h + 1, :] = jnp.sum(ql, axis=0, keepdims=True)
            da_s[GROUP + h : GROUP + h + 1, :] = jnp.sum(qu, axis=0, keepdims=True)
            whole = jnp.where(lane == h, jnp.sum(ql, axis=1, keepdims=True), whole)
            whole = jnp.where(lane == GROUP + h, jnp.sum(qu, axis=1, keepdims=True), whole)
        dxd = dot(jnp.concatenate(ms, axis=1), bd) + cf + cb
        ddt = ddt + dot(high_low(x * dxd), seg2[two, :])
        dx = dte * dxd + skip[:, sl] * dy
        dxp = dx * (sg * (1.0 + xp * (1.0 - sg)))
        ext = jnp.concatenate([dxp, edge_s[:, sl] * last], axis=0)
        edge_s[:, sl] = dxp[:8]
        v = vs(p)[0][:, at].astype(F32)
        dv = jnp.zeros((SPAN, 128), F32)
        for j in range(TAPS):
            moved = shifted(ext, j, SPAN)
            k = TAPS - 1 - j
            dv = dv + moved * cv[k : k + 1, sl]
            cvg_o[k : k + 1, sl] += jnp.sum(v * moved, axis=0, keepdims=True)
        dv_o[:, sl] = dv.astype(BF)

    dafb = jnp.where(off, daff, 0.0).astype(BF)
    db = db + dot(dafb, cm)
    dc = dc + dot_tn(dafb, bm)
    dbc = jnp.concatenate([db, dc], axis=1)
    pp = pspre_r[...]
    sp = sigmoid(pp)
    dpp = dbc * (sp * (1.0 + pp * (1.0 - sp)))
    ext = jnp.concatenate([dpp, edges_s[...] * last], axis=0)
    edges_s[...] = dpp[:8]
    ps = ps_r[...]
    dst = jnp.zeros((SPAN, 128), F32)
    for j in range(TAPS):
        moved = shifted(ext, j, SPAN)
        k = TAPS - 1 - j
        dst = dst + moved * cs[k : k + 1, :]
        csg_o[k : k + 1, :] += jnp.sum(ps * moved, axis=0, keepdims=True)
    dst_o[...] = dst.astype(BF)

    red = red - whole + jnp.transpose(da_s[...])
    hi = red.astype(BF)
    lo = (red - hi.astype(F32)).astype(BF)
    summed = dot(tris[...], hi) + dot(tris[...], lo)
    parts = [summed[g * SPAN : (g + 1) * SPAN] for g in range(4)]
    picked = jnp.where(
        lane < 32, parts[0], jnp.where(lane < 64, parts[1], jnp.where(lane < 96, parts[2], parts[3]))
    )
    total = picked + pltpu.roll(picked, 64, 1)
    total = total + pltpu.roll(total, 32, 1)
    crossed = cross_s[...]
    crossed_hi = crossed.astype(BF)
    crossed_lo = (crossed - crossed_hi.astype(F32)).astype(BF)
    da = total + (dot(crossed_hi, segs[...]) + dot(crossed_lo, segs[...]))[0:1]
    dz = (ddt + da * nad[...]) * col
    dz = jnp.where((lane >= 96) & (lane < 96 + heads), dz, 0.0)
    dz_o[...] = dz.astype(BF)
    head_o[0:1, :] += jnp.sum(da * col * nad[...], axis=0, keepdims=True)
    head_o[1:2, :] += jnp.sum(dz, axis=0, keepdims=True)

    @pl.when(i == 0)
    def _():
        edge_o[...] = edge_s[...]
        edges_o[...] = edges_s[...]


def back(heads, sc, split, dy, bc, ps, pspre, col, row, sf, sb, gbl, pg, dff, skip, cv, cs, nad):
    tokens, width = dy.shape
    groups = len(split[0])
    part = width // groups
    blocks = tokens // SPAN
    maps = expanders(heads)
    every = sum(maps)
    seg4 = by_pairs([m.T for m in maps], 0)
    seg2 = by_pairs([every.T, every.T], 0)
    segs = every.T
    at = np.arange(SPAN)
    row_at, col_at = at[:, None], at[None, :]
    tris = np.concatenate(
        [col_at >= row_at, col_at <= row_at, col_at < row_at, col_at > row_at], axis=0
    ).astype(np.float32)
    e01 = by_pairs(maps[:2], 1)

    def rev(shape):
        rank = len(shape)
        return pl.BlockSpec(shape, lambda i: (blocks - 1 - i,) + (0,) * (rank - 1))

    sds = jax.ShapeDtypeStruct
    state = (1, STATE, width)
    outs = [
        (sds((tokens, width), BF), rev((SPAN, width))),
        (sds((tokens, 128), BF), rev((SPAN, 128))),
        (sds((tokens, 128), BF), rev((SPAN, 128))),
        (sds((TAPS, width), F32), full((TAPS, width))),
        (sds((TAPS, 128), F32), full((TAPS, 128))),
        (sds((8, 128), F32), full((8, 128))),
        (sds((8, width), F32), full((8, width))),
        (sds((8, 128), F32), full((8, 128))),
    ]
    shared = [skip, cv, cs, nad]
    shared += [jnp.asarray(m, BF) for m in (e01, seg4, seg2, segs, tris)]
    in_specs = [SMEM] + [rev((SPAN, part))] * (2 * groups)
    in_specs += [full((STATE, part))] * (2 * groups)
    in_specs += [rev((SPAN, width))] + [rev((SPAN, 128))] * 5
    in_specs += [rev(state)] * 3 + [rev((1, 8, width)), rev(state)]
    in_specs += [full(a.shape) for a in shared]
    return pl.pallas_call(
        functools.partial(back_kernel, heads, groups),
        grid=(blocks,),
        in_specs=in_specs,
        out_specs=[spec for _, spec in outs],
        out_shape=[shape for shape, _ in outs],
        scratch_shapes=[
            pltpu.VMEM((STATE, width), F32),
            pltpu.VMEM((8, width), F32),
            pltpu.VMEM((8, 128), F32),
            pltpu.VMEM((128, 128), F32),
            pltpu.VMEM((8, width), F32),
        ],
        compiler_params=pltpu.CompilerParams(vmem_limit_bytes=58 * 1024 * 1024),
        cost_estimate=cost(100),
        name="back",
    )(
        sc, *[a for kind in split for a in kind],
        dy, bc, ps, pspre, col, row, sf, sb, gbl, pg, dff, *shared,
    )


def input_kernel(groups, *refs):
    refs = list(refs)
    slabs = refs[:groups]
    dgate, dv, dst, dz, ws, wst, gain, hid, gout, grad_o, gain_o, wg, wv = refs[groups:]

    @pl.when(pl.program_id(0) == 0)
    def _():
        gain_o[...] = jnp.zeros_like(gain_o)
        pairs_in = slabs[0].shape[0] // 2
        for p in range(groups * pairs_in):
            slab, h = slabs[p // pairs_in], 2 * (p % pairs_in)
            g, v = unpaired(slab[h].astype(F32), slab[h + 1].astype(F32))
            wg[:, p * 128 : (p + 1) * 128] = g.astype(BF)
            wv[:, p * 128 : (p + 1) * 128] = v.astype(BF)

    dn = dot_nt(dst[...], ws[...]) + dot_nt(dz[...], wst[...])
    dn = dn + dot_nt(dgate[...], wg[...]) + dot_nt(dv[...], wv[...])
    u = hid[...].astype(F32)
    scale = lax.rsqrt(jnp.mean(u * u, axis=1, keepdims=True) + EPS)
    unit = u * scale
    gain_o[...] += jnp.sum(dn * unit, axis=0, keepdims=True)
    du = dn * gain[...]
    inner = jnp.mean(du * unit, axis=1, keepdims=True)
    grad_o[...] = (gout[...].astype(F32) + scale * (du - unit * inner)).astype(BF)


def input_side(slabs, dgate, dv, dst, dz, ws, wst, gain, hidden, out_grad):
    tokens, width_in = hidden.shape
    tile = min(512, tokens)

    def rows(a):
        return pl.BlockSpec((tile, a.shape[1]), lambda i: (i, 0))

    sds = jax.ShapeDtypeStruct
    fixed = list(slabs)
    width = dgate.shape[1]
    streams = [dgate, dv, dst, dz]
    specs = [full(a.shape) for a in fixed] + [rows(a) for a in streams]
    specs += [full(a.shape) for a in (ws, wst, gain)] + [rows(hidden), rows(out_grad)]
    return pl.pallas_call(
        functools.partial(input_kernel, len(slabs)),
        grid=(tokens // tile,),
        in_specs=specs,
        out_specs=[rows(hidden), full((1, width_in))],
        out_shape=[sds((tokens, width_in), BF), sds((1, width_in), F32)],
        scratch_shapes=[pltpu.VMEM((width_in, width), BF)] * 2,
        compiler_params=pltpu.CompilerParams(vmem_limit_bytes=58 * 1024 * 1024),
        cost_estimate=cost(15),
        name="input_side",
    )(*fixed, *streams, ws, wst, gain, hidden, out_grad)


def reduce_kernel(bits, lanes, mats, *refs):
    n_mats = len(mats)
    srcs, both, tiny = refs[:n_mats], refs[n_mats], refs[n_mats + 1]
    paired_o, last_o, both_o, tiny_o = refs[n_mats + 2 : n_mats + 6]
    outs = (*refs[n_mats + 6 : n_mats + 8], last_o)
    scratch = refs[n_mats + 8 :]
    own_r, sent = scratch[0], scratch[1]
    halves, parts = scratch[2 : 2 + bits], scratch[2 + bits : 1 + 2 * bits]
    tiny_r, tiny_s, send_s, recv_s, tsend_s, trecv_s = scratch[1 + 2 * bits :]
    rows = srcs[0].shape[0] if mats[0] == "cols" else srcs[0].shape[0] // 2
    width = outs[0].shape[1]
    me = lax.axis_index("dp")
    chan = lax.axis_index("chan")
    bit = [lax.rem(lax.div(me, 2**k), 2) for k in range(bits)]
    partner = [{"dp": me + (1 - 2 * bit[k]) * 2**k} for k in range(bits)]
    across = {"chan": 1 - chan}
    stages = [partner[0], across] + partner[1:]

    barrier = pltpu.get_barrier_semaphore()
    for device in stages:
        pl.semaphore_signal(barrier, inc=1, device_id=device, device_id_type=pl.DeviceIdType.MESH)
    pl.semaphore_wait(barrier, bits + 1)

    chunks = [(m, s) for m in range(n_mats) for s in range(0, width, lanes)]
    mains = len(chunks)
    n = mains + both.shape[1] // lanes
    half = rows // 2

    def mult(v):
        return pl.multiple_of(v, 16)

    def source(c, which, part):
        if c >= mains:
            return both.at[pl.ds(mult(part * half), half), pl.ds((c - mains) * lanes, lanes)]
        m, s = chunks[c]
        if mats[m] == "cols":
            return srcs[m].at[pl.ds(mult(part * half), half), pl.ds(which * width + s, lanes)]
        return srcs[m].at[pl.ds(mult(which * rows + part * half), half), pl.ds(s, lanes)]

    def target(c, start, size):
        if c >= mains:
            return both_o.at[pl.ds(mult(start), size), pl.ds((c - mains) * lanes, lanes)]
        m, s = chunks[c]
        return outs[m].at[pl.ds(mult(start), size), pl.ds(s, lanes)]

    def copy(src, dst, c, k, device):
        return pltpu.make_async_remote_copy(
            src_ref=src,
            dst_ref=dst,
            send_sem=send_s.at[c, k],
            recv_sem=recv_s.at[c, k],
            device_id=device,
            device_id_type=pl.DeviceIdType.MESH,
        )

    offset = [bit[0] * half]
    for k in range(1, bits):
        offset.append(offset[-1] + bit[k] * (half >> k))

    def first(c, which):
        if c >= mains and which == 0:
            return None
        slot = own_r.at[c, which]
        return copy(source(c, which, 1 - bit[0]), slot, c, which, partner[0])

    def second(c):
        return copy(sent.at[c], halves[0].at[c], c, 2, across)

    def halving(c, k):
        size = half >> k
        src = parts[k - 1].at[c, pl.ds(mult((1 - bit[k]) * size), size), :]
        return copy(src, halves[k].at[c], c, 2 + k, partner[k])

    def doubling(c, k):
        size = half >> k
        place = target(c, offset[k], size)
        return copy(place, place, c, 2 + bits + k, partner[k])

    def f32(ref):
        return ref[...].astype(F32)

    def stage(c, s):
        if s == 0:
            for which in (0, 1):
                rdma = first(c, which)
                if rdma is not None:
                    rdma.start()
        elif s == 1:
            first(c, 1).wait_recv()
            sent[c] = (f32(source(c, 1, bit[0])) + f32(own_r.at[c, 1])).astype(BF)
            second(c).start()
        elif s == 2:
            second(c).wait_recv()
            if c >= mains:
                total = f32(sent.at[c]) + f32(halves[0].at[c])
            else:
                first(c, 0).wait_recv()
                total = f32(source(c, 0, bit[0])) + f32(own_r.at[c, 0]) + f32(halves[0].at[c])
            parts[0][c] = total.astype(BF)
            halving(c, 1).start()
        elif s < bits + 2:
            k = s - 2
            size = half >> k
            halving(c, k).wait_recv()
            kept = parts[k - 1].at[c, pl.ds(mult(bit[k] * size), size), :]
            total = (f32(kept) + f32(halves[k].at[c])).astype(BF)
            if k < bits - 1:
                parts[k][c] = total
                halving(c, k + 1).start()
            else:
                target(c, offset[k], size)[...] = total
                doubling(c, k).start()
        else:
            k = 2 * bits + 1 - s
            doubling(c, k).wait_recv()
            if k > 0:
                doubling(c, k - 1).start()

    def tiny_copy(k):
        return pltpu.make_async_remote_copy(
            src_ref=tiny if k == 0 else tiny_s.at[k - 1],
            dst_ref=tiny_r.at[k],
            send_sem=tsend_s.at[k],
            recv_sem=trecv_s.at[k],
            device_id=stages[k],
            device_id_type=pl.DeviceIdType.MESH,
        )

    tiny_copy(0).start()
    last = 2 * bits + 1
    for tick in range(n + SLACK * last):
        for s in range(last, -1, -1):
            c = tick - SLACK * s
            if 0 <= c < n:
                stage(c, s)
        if 1 <= tick <= bits + 1:
            k = tick - 1
            tiny_copy(k).wait_recv()
            before = tiny[...] if k == 0 else tiny_s[k - 1]
            total = before + tiny_r[k]
            if k < bits:
                tiny_s[k] = total
                tiny_copy(k + 1).start()
            else:
                tiny_o[...] = total

    low_half = lanes_of(rows) < HEAD_DIM
    for p in range(width // 128):
        sl = slice(p * 128, (p + 1) * 128)
        g, v = f32(outs[0].at[:, sl]), f32(outs[1].at[:, sl])
        paired_o[2 * p] = jnp.where(low_half, g, pltpu.roll(v, 64, 1))
        paired_o[2 * p + 1] = jnp.where(low_half, pltpu.roll(g, 64, 1), v)

    for c in range(n):
        for which in (0, 1):
            rdma = first(c, which)
            if rdma is not None:
                rdma.wait_send()
        second(c).wait_send()
        for k in range(1, bits):
            halving(c, k).wait_send()
        for k in range(bits):
            doubling(c, k).wait_send()
    for k in range(bits + 1):
        tiny_copy(k).wait_send()


def reduce_all(bits, mats, both, tiny, lanes):
    kinds = [kind for _, kind in mats]
    arrays = [a for a, _ in mats]
    rows = arrays[0].shape[0] if kinds[0] == "cols" else arrays[0].shape[0] // 2
    width = arrays[0].shape[1] // 2 if kinds[0] == "cols" else arrays[0].shape[1]
    half = rows // 2
    n = len(arrays) * (width // lanes) + both.shape[1] // lanes
    vmem = pl.BlockSpec(memory_space=pltpu.VMEM)
    sds = jax.ShapeDtypeStruct
    scratch = [pltpu.VMEM((rows, width), BF)] * 2
    scratch += [pltpu.VMEM((n, 2, half, lanes), BF), pltpu.VMEM((n, half, lanes), BF)]
    scratch += [pltpu.VMEM((n, half >> k, lanes), BF) for k in range(bits)]
    scratch += [pltpu.VMEM((n, half >> k, lanes), BF) for k in range(bits - 1)]
    scratch += [
        pltpu.VMEM((bits + 1,) + tiny.shape, F32),
        pltpu.VMEM((bits,) + tiny.shape, F32),
        pltpu.SemaphoreType.DMA((n, 2 + 2 * bits)),
        pltpu.SemaphoreType.DMA((n, 2 + 2 * bits)),
        pltpu.SemaphoreType.DMA((bits + 1,)),
        pltpu.SemaphoreType.DMA((bits + 1,)),
    ]
    return pl.pallas_call(
        functools.partial(reduce_kernel, bits, lanes, kinds),
        out_shape=[
            sds((width // HEAD_DIM, rows, 128), F32), sds((rows, width), BF), sds(both.shape, BF), sds(tiny.shape, F32)
        ],
        in_specs=[vmem] * (len(arrays) + 2),
        out_specs=[vmem] * 4,
        scratch_shapes=scratch,
        compiler_params=pltpu.CompilerParams(
            collective_id=0, has_side_effects=True, vmem_limit_bytes=58 * 1024 * 1024
        ),
        name="reduce_all",
    )(*arrays, both, tiny)


def spread_heads(v):
    padded = jnp.zeros((GROUP,), F32).at[: v.shape[0]].set(v)
    return jnp.tile(padded, 4)[None]


def handed(total, passed, shards, up):
    pairs = [(k, k + 1) if up else (k + 1, k) for k in range(shards - 1)]
    entering = lax.ppermute(total.astype(BF), "chan", pairs)
    for _ in range(shards - 2):
        now = total + passed[0:1] * entering.astype(F32)
        entering = lax.ppermute(now.astype(BF), "chan", pairs)
    return entering


def swap(v):
    return lax.ppermute(v, "chan", [(0, 1), (1, 0)])


def core_swap(v):
    size = lax.axis_size("dp")
    return lax.ppermute(v, "dp", [(k, k ^ 1) for k in range(size)])


def on_device(
    hidden_in, norm_gain, gate_value_weight, state_weight, step_weight, value_conv, state_conv,
    step_bias, decay_log, skip_gain, gate_gain, out_weight, seq_length, seq_count, out_grad,
):
    tokens, width_in = hidden_in.shape
    channel = lax.axis_index("chan")
    shards = lax.axis_size("chan")
    groups_dp = lax.axis_size("dp")
    length, count = seq_length[0], seq_count[0]
    local_heads = gate_value_weight.shape[1]
    local = local_heads * HEAD_DIM
    heads = local_heads * shards
    width = heads * HEAD_DIM
    paired = shards == 2 and local_heads % 4 == 0 and groups_dp % 2 == 0
    one = jnp.ones((), jnp.int32)
    flags = [channel, 1 - channel, 1 - channel, channel] if paired else [one] * 4
    sc = jnp.stack([channel * tokens, length, count] + flags).astype(jnp.int32)
    ups = [(k, k + 1) for k in range(shards - 1)]
    downs = [(k + 1, k) for k in range(shards - 1)]
    gain = norm_gain[None]

    slab = gate_value_weight.transpose(1, 0, 2)
    edge = lax.ppermute(hidden_in[tokens - PAD :], "chan", ups)
    vec = jnp.concatenate([step_bias, decay_log, skip_gain])
    small = jnp.concatenate(
        [
            value_conv,
            gate_gain[None],
            jnp.pad(vec, (0, local - 3 * local_heads))[None],
        ]
    )

    def step_matrix(steps):
        return jnp.tile(jnp.pad(steps, ((0, 0), (0, GROUP - steps.shape[1]))), (1, 4))

    each_map = expanders(heads)
    e0, e1, _, _ = [jnp.asarray(e, BF) for e in each_map]
    e01 = jnp.asarray(by_pairs(each_map[:2], 1), BF)
    maps = (gain, state_weight, state_conv)
    if paired:
        core = lax.axis_index("dp") % 2
        half = lax.dynamic_slice_in_dim(slab, core * (local_heads // 2), local_heads // 2, 0)
        payload, edge = lax.optimization_barrier((half, edge))
        come = swap(payload)
        small_b, wstep_b, ow_b = swap(small), swap(step_weight), swap(out_weight)
        gate, v, xpre, ff, sbl, pb, _, _, _, _, hand, vh, normed, nedge, ps, pspre, bc, psh = project(
            sc, hidden_in, edge, slab, step_matrix(step_weight), value_conv,
            spread_heads(step_bias), spread_heads(-jnp.exp(decay_log) * LOG2E),
            e0[:, :local], e1[:, :local], maps=maps, final=False,
        )
        come, small_b, wstep_b, ow_b, nedge, hand = lax.optimization_barrier(
            (come, small_b, wstep_b, ow_b, nedge, hand)
        )
        also = core_swap(come)
        enter_b = swap(hand)
        halves = jnp.where(core == 0, jnp.stack([come, also]), jnp.stack([also, come]))
        slabs = [slab, halves.reshape(slab.shape)]
        smalls = [small, small_b]
        wstep = jnp.concatenate([step_weight, wstep_b], axis=1)
        ow = jnp.concatenate([out_weight, ow_b], axis=0)
    else:
        slabs = [lax.all_gather(slab, "chan", axis=0, tiled=True)]
        gathered = lax.all_gather(small, "chan", axis=0)
        smalls = [gathered[k] for k in range(shards)]
        wstep = lax.all_gather(step_weight, "chan", axis=1, tiled=True)
        ow = lax.all_gather(out_weight, "chan", axis=0, tiled=True)

    def heads_row(k, parts):
        lo, hi = k * local_heads, (k + 1) * local_heads
        return jnp.concatenate([p[TAPS + 1, lo:hi] for p in parts])

    bias_all, dlog_all, skip_all = (heads_row(k, smalls) for k in range(3))
    cv = jnp.concatenate([p[:TAPS] for p in smalls], axis=1)
    ggain = jnp.concatenate([p[TAPS : TAPS + 1] for p in smalls], axis=1)
    skip = jnp.repeat(skip_all, HEAD_DIM)[None]
    nad = -jnp.exp(dlog_all)

    if paired:
        gate2, v2, xpre2, ff2, sbl2, pb2, _, _, _, _, hand2, vh2, col, row = project(
            sc, normed, nedge, slabs[1], step_matrix(wstep), smalls[1][:TAPS],
            spread_heads(bias_all), spread_heads(nad * LOG2E),
            e0[:, local:], e1[:, local:], bc=bc, final=True,
        )
        enter = [swap(hand2), enter_b]
        split = [[gate, gate2], [xpre, xpre2], [ff, ff2], [sbl, sbl2], [pb, pb2], enter, enter]
        vs, xs = [v, v2], [xpre, xpre2]
        vh = jnp.concatenate([vh, vh2], axis=1)
    else:
        (
            gate, v, xpre, ff, sbl, pb, sft, sbt, pft, pbt, _, vh, normed, nedge, ps, pspre, bc, psh,
            col, row,
        ) = project(
            sc, hidden_in, edge, slabs[0], step_matrix(wstep), cv, spread_heads(bias_all),
            spread_heads(nad * LOG2E), e0, e1, maps=maps,
        )
        sfd = handed(sft, pft, shards, True)
        sbd = handed(sbt, pbt, shards, False)
        split = [[gate], [xpre], [ff], [sbl], [pb], [sfd], [sbd]]
        vs, xs = [v], [xpre]
    (
        output, gnorm, dy, dgate, sf, sb, gbl, pg, dff, gft, gbt, pgf, pgb, hand, ggain_grad, skip_grad,
    ) = mix(sc, split, bc, col, row, hidden_in, out_grad, ow, ow.T, ggain, skip, e01)
    if paired:
        enter = swap(hand)
        enter = [enter[:, local:], enter[:, :local]]
        gfds = gbds = enter
    else:
        gfds = [handed(gft, pgf, shards, False)]
        gbds = [handed(gbt, pgb, shards, True)]

    own_ids = channel * tokens + jnp.arange(tokens, dtype=jnp.int32)
    live = jnp.where(own_ids // length < count, 1.0, 0.0)[:, None].astype(BF)
    ow_grad = dot_tn(gnorm, out_grad * live).astype(BF)
    dwg = dot_tn(normed, dgate).astype(BF)

    def absolute(parts, axis):
        if not paired:
            return jnp.concatenate(parts, axis=axis)
        a = jnp.concatenate(parts, axis=axis)
        b = jnp.concatenate(parts[::-1], axis=axis)
        return jnp.where(channel == 0, a, b)

    def shared(v, axis):
        if paired:
            a, b = jnp.split(v, 2, axis=axis)
            v = (a.astype(F32) + swap(b).astype(F32)).astype(BF)
        else:
            v = lax.psum_scatter(v, "chan", scatter_dimension=axis, tiled=True)
        return lax.psum(v, "dp")

    dv, dst, dz, cvg, csg, head_sums, edge_g, edges_g = back(
        heads, sc, [xs, vs, gfds, gbds], dy, bc, ps, pspre, col, row, sf, sb, gbl, pg, dff, skip, cv,
        state_conv, spread_heads(nad),
    )

    if paired:
        turned = jnp.concatenate([edge_g[:, local:], edge_g[:, :local]], axis=1)
    else:
        turned = edge_g
    kernel = jnp.concatenate([cv, state_conv], axis=1)
    past = jnp.concatenate([vh, psh], axis=1)
    reach = TAPS - 1
    after = lax.ppermute(jnp.concatenate([turned, edges_g], axis=1), "chan", downs)[:reach]
    joined = jnp.concatenate([edge_g, edges_g], axis=1)
    after = after * jnp.where(((channel + 1) * tokens) % length == 0, 0.0, 1.0)
    patch = jnp.zeros((reach, joined.shape[1]), F32)
    taps = []
    for j in range(TAPS):
        if j:
            moved = jnp.pad(after[:j], ((reach - j, 0), (0, 0)))
            patch = patch + moved * kernel[TAPS - 1 - j][None]
        taps.append(jnp.sum(joined[:j] * past[PAD - j :], axis=0))
    cross_taps = jnp.stack(taps[::-1])
    tail = jnp.pad(patch, ((PAD - reach, 0), (0, 0))).astype(BF)
    dv = dv.at[tokens - PAD :].add(tail[:, :width])
    dst = dst.at[tokens - PAD :].add(tail[:, width:])
    cvg = cvg + cross_taps[:, :width]
    csg = csg + cross_taps[:, width:]

    dwv = dot_tn(normed, dv).astype(BF)
    dws = dot_tn(normed, dst)
    dwst = dot_tn(normed, dz)[:, 96 : 96 + heads]
    wst_tail = jnp.pad(wstep, ((0, 0), (96, GROUP - heads)))
    input_grad, norm_gain_grad = input_side(
        slabs, dgate, dv, dst, dz, state_weight, wst_tail, gain, hidden_in, out_grad
    )

    bias_sum = head_sums[1, 96 : 96 + heads]
    dlog_sum = head_sums[0, 64 : 64 + heads]
    skip_sum = skip_grad.reshape(heads, HEAD_DIM).sum(axis=1)

    def by_shard(k):
        cut, hcut = slice(k * local, (k + 1) * local), slice(k * local_heads, (k + 1) * local_heads)
        return jnp.concatenate(
            [cvg[:, cut].reshape(-1), ggain_grad[0, cut], bias_sum[hcut], dlog_sum[hcut], skip_sum[hcut]]
        )

    each = (TAPS + 1) * local + 3 * local_heads
    pad_each = -each % 128
    tiny = absolute([jnp.pad(by_shard(k), (0, pad_each)) for k in range(shards)], 0)
    tiny = jnp.concatenate([tiny, norm_gain_grad[0], csg.reshape(-1)])
    tiny = jnp.pad(tiny, (0, -tiny.shape[0] % 1024)).reshape(-1, 128)
    dwst = absolute([dwst[:, k * local_heads : (k + 1) * local_heads] for k in range(shards)], 1)
    both = jnp.concatenate([dws, jnp.pad(dwst, ((0, 0), (0, 128 - heads)))], axis=1).astype(BF)

    bits = groups_dp.bit_length() - 1
    if paired and groups_dp == 2**bits and bits >= 2 and width_in % (16 * groups_dp) == 0:
        gvw, owg, both, tiny = reduce_all(
            bits, [(dwg, "cols"), (dwv, "cols"), (ow_grad, "rows")], both, tiny, LANES
        )
        gvw = gvw.transpose(1, 0, 2)
        owg = owg.astype(F32)
    else:
        dwg, dwv, owg = shared(dwg, 1), shared(dwv, 1), shared(ow_grad, 0).astype(F32)
        both, tiny = lax.psum((both, tiny), ("dp", "chan"))
        pieces = [a.reshape(width_in, local_heads, HEAD_DIM) for a in (dwg, dwv)]
        gvw = jnp.concatenate(pieces, axis=2).astype(F32)
    both = both.astype(F32)
    flat = tiny.reshape(-1)
    base = (each + pad_each) * shards
    mine = lax.dynamic_slice_in_dim(flat, channel * (each + pad_each), each, 0)
    cuts = np.cumsum([TAPS * local, local, local_heads, local_heads])
    dwst = lax.dynamic_slice_in_dim(both[:, 128:], channel * local_heads, local_heads, 1)
    return (
        output,
        input_grad,
        flat[base : base + width_in],
        gvw,
        both[:, :128],
        dwst,
        mine[: cuts[0]].reshape(TAPS, local),
        flat[base + width_in : base + width_in + TAPS * 128].reshape(TAPS, 128),
        mine[cuts[1] : cuts[2]],
        mine[cuts[2] : cuts[3]],
        mine[cuts[3] :],
        mine[cuts[0] : cuts[1]],
        owg,
    )


def solution(mesh):
    in_specs = (
        P(("dp", "chan"), None),
        P(),
        P(None, "chan", None),
        P(),
        P(None, "chan"),
        P(None, "chan"),
        P(),
        P("chan"),
        P("chan"),
        P("chan"),
        P("chan"),
        P("chan", None),
        P("dp"),
        P("dp"),
        P(("dp", "chan"), None),
    )
    out_specs = (
        P(("dp", "chan"), None),
        P(("dp", "chan"), None),
        P(),
        P(None, "chan", None),
        P(),
        P(None, "chan"),
        P(None, "chan"),
        P(),
        P("chan"),
        P("chan"),
        P("chan"),
        P("chan"),
        P("chan", None),
    )
    return jax.shard_map(
        on_device, mesh=mesh, in_specs=in_specs, out_specs=out_specs, check_vma=False
    )
```

```python
import functools

import jax
import jax.numpy as jnp
import numpy as np
from jax import lax
from jax.experimental import pallas as pl
from jax.experimental.pallas import tpu as pltpu
from jax.sharding import PartitionSpec as P

HEAD_DIM = 64
STATE = 64
SPAN = 128
PAD = 16
GROUP = 32
TAPS = 4
LANES = 128
SLACK = 2
EPS = 1e-05
LOG2E = float(np.log2(np.e))
BF = jnp.bfloat16
F32 = jnp.float32


def dot(a, b):
    return jnp.dot(a, b, preferred_element_type=F32)


def dot_nt(a, b):
    return lax.dot_general(a, b, (((1,), (1,)), ((), ())), preferred_element_type=F32)


def dot_tn(a, b):
    return lax.dot_general(a, b, (((0,), (0,)), ((), ())), preferred_element_type=F32)


def fine_nt(a, b):
    return lax.dot_general(
        a, b, (((1,), (1,)), ((), ())), precision=lax.Precision.HIGHEST, preferred_element_type=F32
    )


def fine(a, b):
    return jnp.dot(a, b, precision=lax.Precision.HIGHEST, preferred_element_type=F32)


def sigmoid(v):
    return 0.5 + 0.5 * jnp.tanh(0.5 * v)


def lanes_of(rows):
    return lax.broadcasted_iota(jnp.int32, (rows, 128), 1)


def shifted(ext, offset, rows):
    return ext[offset : offset + rows]


def full(shape):
    rank = len(shape)
    return pl.BlockSpec(shape, lambda i: (0,) * rank)


SMEM = pl.BlockSpec(memory_space=pltpu.SMEM)


def placing(heads, groups=range(4)):
    lane, head = np.arange(128)[None], np.arange(heads)[:, None]
    hits = sum((lane == GROUP * g + head).astype(np.float32) for g in groups)
    return jnp.asarray(hits)


def cost(micros):
    return pl.CostEstimate(flops=int(micros * 1e9), bytes_accessed=1024, transcendentals=0)


def side(a, b):
    return jnp.concatenate([a, b], axis=1)


def high_low(v):
    hi = v.astype(BF)
    return side(hi, (v - hi.astype(F32)).astype(BF))


def by_pairs(maps, axis):
    pairs = maps[0].shape[axis] // 128
    pieces = [np.split(m, pairs, axis=axis) for m in maps]
    return np.concatenate([piece[p] for p in range(pairs) for piece in pieces], axis=axis)


def unpaired(a, b):
    low = lanes_of(a.shape[0]) < HEAD_DIM
    return jnp.where(low, a, pltpu.roll(b, 64, 1)), jnp.where(low, pltpu.roll(a, 64, 1), b)


def expanders(heads):
    channel = np.arange(heads * HEAD_DIM) // HEAD_DIM
    lane = np.arange(128)[:, None]
    return [np.asarray(lane == GROUP * g + channel[None], np.float32) for g in range(4)]


def project_kernel(fresh, final, tile, chunk, *refs):
    refs = list(refs)

    def take(count):
        return [refs.pop(0) for _ in range(count)]

    sc, tokens_r, halo, edge, slabs, steps_t, cv, hv, place_r, tri, e0, e1 = take(12)
    if fresh:
        gain, ws, cs = take(3)
    else:
        (bc_r,) = take(1)
    gate_o, v_o, xpre_o, ff_o, sb_o, pb_o, sft_o, sbt_o, pft_o, pbt_o, hand_o, vh_o = take(12)
    if fresh:
        normed_o, nedge_o, ps_o, pspre_o, bc_o, psh_o = take(6)
    if final:
        col_o, row_o = take(2)
    sb_s, pb_s, sf_s, pf_s, wst, hv_s = take(6)

    step = pl.program_id(0)
    tiles = pl.num_programs(0)
    at = tiles - 1 - step
    length = sc[1]
    start = sc[0] + at * tile
    width = e0.shape[1]
    blocks = tile // SPAN

    @pl.when(step == 0)
    def _():
        sb_s[...] = jnp.zeros_like(sb_s)
        sf_s[...] = jnp.zeros_like(sf_s)
        pb_s[...] = jnp.ones_like(pb_s)
        pf_s[...] = jnp.ones_like(pf_s)
        wst[...] = dot_tn(steps_t[...], place_r[...].astype(BF)).astype(BF)
        rows_hv = fine(hv[...], place_r[...])
        hv_s[0:1] = rows_hv[0:1]
        hv_s[1:2] = -LOG2E * jnp.exp(rows_hv[1:2])

    before = jnp.where(at == 0, edge[...].astype(F32), halo[...].astype(F32))
    rows = jnp.concatenate([before, tokens_r[...].astype(F32)], axis=0)
    keep = jnp.where(lax.rem(start, length) == 0, 0.0, 1.0)
    row_id = lax.broadcasted_iota(jnp.int32, (tile + PAD, 1), 0)
    keep_rows = jnp.where(row_id < PAD, keep, 1.0)
    if fresh:
        scale = lax.rsqrt(jnp.mean(rows * rows, axis=1, keepdims=True) + EPS)
        normed = (rows * scale * gain[...]).astype(BF)
        own = normed[PAD:]
        normed_o[...] = own

        ps = dot(normed, ws[...]) * keep_rows
        ps_o[...] = ps[PAD:]
        pspre = ps[PAD:] * cs[TAPS - 1 : TAPS]
        for j in range(1, TAPS):
            pspre = pspre + shifted(ps, PAD - j, tile) * cs[TAPS - 1 - j : TAPS - j]
        pspre_o[...] = pspre
        bc = pspre * sigmoid(pspre)
        bc_o[...] = bc

        @pl.when(at == 0)
        def _():
            nedge_o[...] = normed[:PAD]
            psh_o[...] = ps[:PAD]

    else:
        normed = rows.astype(BF)
        own = tokens_r[...]
        bc = bc_r[...]

    z = dot(own, wst[...]) + hv_s[0:1]
    dt = jnp.maximum(z, 0.0) + jnp.log1p(jnp.exp(-jnp.abs(z)))
    a2 = dt * hv_s[1:2]
    lane = lanes_of(SPAN)
    if final:
        sig = sigmoid(z)
    wmix, bts = [], []
    for b in range(blocks):
        sl = slice(b * SPAN, (b + 1) * SPAN)
        ab = a2[sl]
        ca = jnp.dot(tri[...], ab, precision=lax.Precision.HIGHEST, preferred_element_type=F32)
        ce = ca - ab
        if final:
            col = jnp.where(
                lane < 32, ca, jnp.where(lane < 64, ce, jnp.where(lane < 96, dt[sl], sig[sl]))
            )
            col_o[sl, :] = col
            row_o[sl, :] = jnp.transpose(col)
        end = ca[SPAN - 1 : SPAN]
        w = jnp.exp2(jnp.where(lane < 32, end - ca, ce)) * dt[sl]
        dec = jnp.broadcast_to(jnp.exp2(end), (8, 128))
        high = dec.astype(BF).astype(F32)
        wmix.append(jnp.concatenate([w, high, dec - high], axis=0).astype(BF))
        bts.append(jnp.transpose(bc[sl])[:STATE].astype(BF))

    for c in range(width // chunk):
        cl = slice(c * chunk, (c + 1) * chunk)
        parts = []
        for h in range(c * chunk // HEAD_DIM, (c + 1) * chunk // HEAD_DIM, 2):
            both = dot(normed, side(slabs[h], slabs[h + 1]))
            parts.append(unpaired(both[:, :128], both[:, 128:]))
        gates = jnp.concatenate([part[0][PAD:] for part in parts], axis=1)
        gate_o[:, cl] = gates.astype(BF)
        v = jnp.concatenate([part[1] for part in parts], axis=1) * keep_rows
        v_o[:, cl] = v[PAD:].astype(BF)

        @pl.when(at == 0)
        def _():
            vh_o[:, cl] = v[:PAD]

        xpre = v[PAD:] * cv[TAPS - 1 : TAPS, cl]
        for j in range(1, TAPS):
            xpre = xpre + shifted(v, PAD - j, tile) * cv[TAPS - 1 - j : TAPS - j, cl]
        xpre_o[:, cl] = xpre.astype(BF)
        x = xpre * sigmoid(xpre)
        for b in reversed(range(blocks)):
            sl = slice(b * SPAN, (b + 1) * SPAN)
            we = dot(wmix[b], e0[:, cl])
            wbe = dot(wmix[b][:SPAN], e1[:, cl])
            dec = we[SPAN : SPAN + 1] + we[SPAN + 8 : SPAN + 9]
            xb = x[sl]
            fresh_f = dot(bts[b], (xb * we[:SPAN]).astype(BF))
            fresh_b = dot(bts[b], (xb * wbe).astype(BF))
            place = start + b * SPAN
            first = jnp.where(lax.rem(place, length) == 0, 0.0, 1.0)
            last = jnp.where(lax.rem(place + SPAN, length) == 0, 0.0, 1.0)
            ff_o[b, :, cl] = fresh_f.astype(BF)
            pf = pf_s[0:1, cl]
            sf_s[:, cl] = sf_s[:, cl] + pf * fresh_f
            pf_s[:, cl] = jnp.broadcast_to(pf * dec * first, (8, chunk))
            held = sb_s[:, cl] * last
            pb = pb_s[0:1, cl] * last
            sb_o[b, :, cl] = held.astype(BF)
            pb_o[b, :, cl] = jnp.broadcast_to(pb, (8, chunk))
            sb_s[:, cl] = held * dec + fresh_b
            pb_s[:, cl] = jnp.broadcast_to(pb * dec, (8, chunk))

    @pl.when(at == 0)
    def _():
        sft_o[...] = sf_s[...]
        sbt_o[...] = sb_s[...]
        pft_o[...] = pf_s[...]
        pbt_o[...] = pb_s[...]
        hand_o[...] = jnp.where(sc[0] == 0, sf_s[...], sb_s[...]).astype(BF)


def project(sc, source, edge, slabs, steps_t, cv, hv, e0, e1, maps=None, bc=None, final=True):
    fresh = maps is not None
    tokens, width_in = source.shape
    width = slabs.shape[0] * HEAD_DIM
    tile = min(256, tokens)
    tiles = tokens // tile
    per = tile // SPAN
    blocks = tokens // SPAN
    chunk = 256 if width % 256 == 0 else 128
    tri = np.tril(np.ones((SPAN, SPAN), np.float32))

    def back(shape):
        rank = len(shape)
        return pl.BlockSpec(shape, lambda i: (tiles - 1 - i,) + (0,) * (rank - 1))

    sds = jax.ShapeDtypeStruct
    wide = (sds((tokens, width), BF), back((tile, width)))
    narrow = (sds((tokens, 128), F32), back((tile, 128)))
    held = (sds((blocks, STATE, width), BF), back((per, STATE, width)))
    total = (sds((STATE, width), F32), full((STATE, width)))
    passed = (sds((8, width), F32), full((8, width)))
    outs = [wide, wide, wide, held, held, (sds((blocks, 8, width), F32), back((per, 8, width)))]
    outs += [total, total, passed, passed, (sds((STATE, width), BF), full((STATE, width)))]
    outs += [(sds((PAD, width), F32), full((PAD, width)))]
    if fresh:
        outs += [
            (sds((tokens, width_in), BF), back((tile, width_in))),
            (sds((PAD, width_in), BF), full((PAD, width_in))),
            narrow,
            narrow,
            narrow,
            (sds((PAD, 128), F32), full((PAD, 128))),
        ]
    if final:
        outs += [narrow, narrow]
    steps = tile // PAD
    args = [sc, source, source, edge, slabs, steps_t, cv, hv, placing(hv.shape[1]), tri, e0, e1]
    in_specs = [
        SMEM,
        back((tile, width_in)),
        pl.BlockSpec((PAD, width_in), lambda i: (jnp.maximum((tiles - 1 - i) * steps - 1, 0), 0)),
    ] + [full(a.shape) for a in args[3:]]
    if fresh:
        args += list(maps)
        in_specs += [full(a.shape) for a in maps]
    else:
        args += [bc]
        in_specs += [back((tile, 128))]
    return pl.pallas_call(
        functools.partial(project_kernel, fresh, final, tile, chunk),
        grid=(tiles,),
        in_specs=in_specs,
        out_specs=[spec for _, spec in outs],
        out_shape=[shape for shape, _ in outs],
        scratch_shapes=[
            pltpu.VMEM((STATE, width), F32),
            pltpu.VMEM((8, width), F32),
            pltpu.VMEM((STATE, width), F32),
            pltpu.VMEM((8, width), F32),
            pltpu.VMEM((width_in, 128), BF),
            pltpu.VMEM((8, 128), F32),
        ],
        compiler_params=pltpu.CompilerParams(vmem_limit_bytes=58 * 1024 * 1024),
        cost_estimate=cost(28),
        name="project",
    )(*args)


def split_refs(refs, groups, kinds):
    taken = [[refs.pop(0) for _ in range(groups)] for _ in range(kinds)]
    return [functools.partial(pick, refs_of) for refs_of in taken]


def pick(refs_of, p):
    per = refs_of[0].shape[-1] // 128
    return refs_of[p // per], slice((p % per) * 128, (p % per + 1) * 128)


def mix_kernel(groups, *refs):
    refs = list(refs)
    sc = refs.pop(0)
    gates, xpres, ffs, sbls, pbs, sfds, sbds = split_refs(refs, groups, 7)
    mix_body(sc, gates, xpres, ffs, sbls, pbs, sfds, sbds, *refs)


def mix_body(
    sc, gates, xpres, ffs, sbls, pbs, sfds, sbds,
    bc_r, col_r, row_r, hid, gout, ow, owt, ggain, skip, e01,
    out_o, gnorm_o, dy_o, dgate_o, sf_o, sb_o, gbl_o, pg_o, dff_o,
    gft_o, gbt_o, pgf_o, pgb_o, hand_o, ggain_o, skip_o,
    sf_s, gb_s, gf_s, pg_s, q_s, y_s, dgn_s, exp_s,
):
    i = pl.program_id(0)
    length = sc[1]
    place = sc[0] + i * SPAN
    first = jnp.where(lax.rem(place, length) == 0, 0.0, 1.0)
    last = jnp.where(lax.rem(place + SPAN, length) == 0, 0.0, 1.0)
    live = jnp.where(lax.div(place, length) < sc[2], 1.0, 0.0)
    width = e01.shape[1] // 2
    pairs = width // 128

    @pl.when(i == 0)
    def _():
        enters_f = jnp.where(sc[3] == 1, 1.0, 0.0)
        for p in range(pairs):
            ref, at = sfds(p)
            sf_s[:, p * 128 : (p + 1) * 128] = ref[:, at].astype(F32) * enters_f
        gb_s[...] = jnp.zeros_like(gb_s)
        gf_s[...] = jnp.zeros_like(gf_s)
        pg_s[...] = jnp.ones_like(pg_s)
        q_s[...] = jnp.ones_like(q_s)
        ggain_o[...] = jnp.zeros_like(ggain_o)
        skip_o[...] = jnp.zeros_like(skip_o)

    enters_b = jnp.where(sc[4] == 1, 1.0, 0.0)
    glow = gout[...].astype(F32) * live
    gl = glow.astype(BF)
    dgn_s[...] = dot(gl, owt[...])

    lane = lanes_of(SPAN)
    low_half = lane < HEAD_DIM
    col = col_r[...]
    row = row_r[...]
    end = jnp.broadcast_to(col[SPAN - 1 : SPAN], (8, 128))
    end1 = pltpu.roll(end, GROUP, 1)
    w = jnp.exp2(jnp.where(lane < 32, col, jnp.where(lane < 64, end1[0:1] - col, 0.0)))
    dec = jnp.exp2(jnp.where(lanes_of(8) < 32, end, 0.0))
    high = dec.astype(BF).astype(F32)
    wmix = jnp.concatenate([w, pltpu.roll(col, 64, 1), high, dec - high], axis=0).astype(BF)
    bc = bc_r[...]
    bmf, cmf = bc[:, :STATE], bc[:, STATE:]
    cm = cmf.astype(BF)
    ct = jnp.transpose(bc)[STATE:].astype(BF)
    square_r = lax.broadcasted_iota(jnp.int32, (SPAN, SPAN), 0)
    aff = jnp.where(square_r == lane, 0.0, fine_nt(cmf, bmf))

    squares = jnp.zeros((SPAN, 128), F32)
    for p in range(pairs):
        sl = slice(p * 128, (p + 1) * 128)
        efd = dot(wmix, e01[:, p * 256 : (p + 1) * 256])
        ef, eb = efd[:SPAN, :128], efd[:SPAN, 128:]
        dte = efd[SPAN : 2 * SPAN, :128]
        exp_s[0, :, sl] = ef
        exp_s[1, :, sl] = eb
        decay = efd[2 * SPAN : 2 * SPAN + 1, :128] + efd[2 * SPAN + 8 : 2 * SPAN + 9, :128]
        exp_s[2, 0:8, sl] = jnp.broadcast_to(decay, (8, 128))
        sf = sf_s[:, sl] * first
        sfb = sf.astype(BF)
        sf_o[0, :, sl] = sfb
        sbl, at = sbls(p)
        pb, sbd, ff, xpre, gate = (r(p)[0] for r in (pbs, sbds, ffs, xpres, gates))
        arrived = sbd[:, at].astype(F32) * enters_b
        sb = (sbl[0, :, at].astype(F32) + pb[0, 0:1, at] * arrived) * last
        sbb = sb.astype(BF)
        sb_o[0, :, sl] = sbb
        sf_s[:, sl] = sf * decay + ff[0, :, at].astype(F32)
        xp = xpre[:, at].astype(F32)
        x = xp * sigmoid(xp)
        xd = x * dte
        bd = jnp.concatenate(
            [jnp.where(low_half, xd, 0.0), jnp.where(low_half, 0.0, xd)], axis=0
        ).astype(BF)
        ms = []
        for h in (2 * p, 2 * p + 1):
            spread = jnp.minimum(
                col[:, h : h + 1] - row[h : h + 1, :],
                row[GROUP + h : GROUP + h + 1, :] - col[:, GROUP + h : GROUP + h + 1],
            )
            ms.append((aff * jnp.exp2(spread)).astype(BF))
        y = dot(jnp.concatenate(ms, axis=1), bd)
        carried = dot(cm, side(sfb, sbb))
        y = y + ef * carried[:, :128] + eb * carried[:, 128:] + skip[:, sl] * x
        y_s[:, sl] = y
        g = gate[:, at].astype(F32)
        gated = y * (g * sigmoid(g))
        squares = squares + gated * gated

    gsc = lax.rsqrt(jnp.sum(squares, axis=1, keepdims=True) * (1.0 / width) + EPS)
    inner = jnp.zeros((SPAN, 128), F32)
    for p in range(pairs):
        sl = slice(p * 128, (p + 1) * 128)
        gate, at = gates(p)
        g = gate[:, at].astype(F32)
        gunit = y_s[:, sl] * (g * sigmoid(g)) * gsc
        gnorm_o[:, sl] = (gunit * ggain[:, sl]).astype(BF)
        dgn = dgn_s[:, sl]
        dgu = dgn * gunit
        ggain_o[:, sl] += jnp.sum(dgu, axis=0, keepdims=True)
        inner = inner + dgu * ggain[:, sl]
    mean = jnp.sum(inner, axis=1, keepdims=True) * (1.0 / width)
    out_o[...] = (hid[...].astype(F32) + live * dot(gnorm_o[...], ow[...])).astype(BF)

    for p in range(pairs):
        sl = slice(p * 128, (p + 1) * 128)
        gate, at = gates(p)
        g = gate[:, at].astype(F32)
        sg = sigmoid(g)
        act = g * sg
        y = y_s[:, sl]
        gunit = y * act * gsc
        dgated = gsc * (dgn_s[:, sl] * ggain[:, sl] - gunit * mean)
        dy = dgated * act
        dy_o[:, sl] = dy.astype(BF)
        dgate_o[:, sl] = (dgated * y * (sg * (1.0 + g * (1.0 - sg)))).astype(BF)
        xp = xpres(p)[0][:, at].astype(F32)
        skip_o[:, sl] += jnp.sum(dy * (xp * sigmoid(xp)), axis=0, keepdims=True)
        decay = exp_s[2, 0:1, sl]
        states = dot(ct, side(exp_s[0, :, sl] * dy, exp_s[1, :, sl] * dy).astype(BF))
        dff, dfb = states[:, :128], states[:, 128:]
        dff_o[0, :, sl] = dff.astype(BF)
        q = q_s[0:1, sl]
        gf_s[:, sl] = gf_s[:, sl] + q * dff
        q_s[:, sl] = jnp.broadcast_to(q * decay * last, (8, 128))
        gb = gb_s[:, sl] * first
        pg = pg_s[0:1, sl] * first
        gbl_o[0, :, sl] = gb.astype(BF)
        pg_o[0, :, sl] = jnp.broadcast_to(pg, (8, 128))
        gb_s[:, sl] = gb * decay + dfb
        pg_s[:, sl] = jnp.broadcast_to(pg * decay, (8, 128))

    @pl.when(i == pl.num_programs(0) - 1)
    def _():
        gft_o[...] = gf_s[...]
        gbt_o[...] = gb_s[...]
        pgf_o[...] = q_s[...]
        pgb_o[...] = pg_s[...]
        hand_o[...] = jnp.where(sc[0] == 0, gb_s[...], gf_s[...]).astype(BF)


def mix(sc, split, bc, col, row, hidden, out_grad, ow, owt, ggain, skip, e01):
    tokens, width_in = hidden.shape
    groups = len(split[0])
    width = e01.shape[1] // 2
    part = width // groups
    blocks = tokens // SPAN

    def ahead(shape):
        rank = len(shape)
        return pl.BlockSpec(shape, lambda i: (i,) + (0,) * (rank - 1))

    sds = jax.ShapeDtypeStruct
    state = (1, STATE, width)
    outs = [
        (sds((tokens, width_in), BF), ahead((SPAN, width_in))),
        (sds((tokens, width), BF), ahead((SPAN, width))),
        (sds((tokens, width), BF), ahead((SPAN, width))),
        (sds((tokens, width), BF), ahead((SPAN, width))),
        (sds((blocks, STATE, width), BF), ahead(state)),
        (sds((blocks, STATE, width), BF), ahead(state)),
        (sds((blocks, STATE, width), BF), ahead(state)),
        (sds((blocks, 8, width), F32), ahead((1, 8, width))),
        (sds((blocks, STATE, width), BF), ahead(state)),
        (sds((STATE, width), F32), full((STATE, width))),
        (sds((STATE, width), F32), full((STATE, width))),
        (sds((8, width), F32), full((8, width))),
        (sds((8, width), F32), full((8, width))),
        (sds((STATE, width), BF), full((STATE, width))),
        (sds((1, width), F32), full((1, width))),
        (sds((1, width), F32), full((1, width))),
    ]
    shared = [ow, owt, ggain, skip, e01]
    in_specs = [SMEM]
    for shape in (
        (SPAN, part), (SPAN, part), (1, STATE, part), (1, STATE, part), (1, 8, part),
    ):
        in_specs += [ahead(shape)] * groups
    in_specs += [full((STATE, part))] * (2 * groups)
    in_specs += [ahead((SPAN, 128))] * 3 + [ahead((SPAN, width_in))] * 2
    in_specs += [full(a.shape) for a in shared]
    return pl.pallas_call(
        functools.partial(mix_kernel, groups),
        grid=(blocks,),
        in_specs=in_specs,
        out_specs=[spec for _, spec in outs],
        out_shape=[shape for shape, _ in outs],
        scratch_shapes=[
            pltpu.VMEM((STATE, width), F32),
            pltpu.VMEM((STATE, width), F32),
            pltpu.VMEM((STATE, width), F32),
            pltpu.VMEM((8, width), F32),
            pltpu.VMEM((8, width), F32),
            pltpu.VMEM((SPAN, width), F32),
            pltpu.VMEM((SPAN, width), F32),
            pltpu.VMEM((3, SPAN, width), F32),
        ],
        compiler_params=pltpu.CompilerParams(vmem_limit_bytes=58 * 1024 * 1024),
        cost_estimate=cost(60),
        name="mix",
    )(sc, *[a for kind in split for a in kind], bc, col, row, hidden, out_grad, *shared)


def back_kernel(heads, groups, *refs):
    refs = list(refs)
    sc = refs.pop(0)
    xpres, vs, gfds, gbds = split_refs(refs, groups, 4)
    back_body(heads, sc, xpres, vs, gfds, gbds, *refs)


def back_body(
    heads, sc, xpres, vs, gfds, gbds,
    dy_r, bc_r, ps_r, pspre_r, col_r, row_r, sf_r, sb_r, gbl, pg, dff,
    skip, cv, cs, hv, spot, e01, seg4, seg2, segs, tris,
    dv_o, dst_o, dz_o, cvg_o, csg_o, head_o, edge_o, edges_o,
    gf_s, edge_s, edges_s, da_s, cross_s, nad_s,
):
    step = pl.program_id(0)
    blocks = pl.num_programs(0)
    i = blocks - 1 - step
    length = sc[1]
    place = sc[0] + i * SPAN
    last = jnp.where(lax.rem(place + SPAN, length) == 0, 0.0, 1.0)
    width = e01.shape[1] // 2
    pairs = width // 128

    @pl.when(step == 0)
    def _():
        enters_f = jnp.where(sc[5] == 1, 1.0, 0.0)
        for p in range(pairs):
            ref, at = gfds(p)
            gf_s[:, p * 128 : (p + 1) * 128] = ref[:, at].astype(F32) * enters_f
        edge_s[...] = jnp.zeros_like(edge_s)
        edges_s[...] = jnp.zeros_like(edges_s)
        da_s[...] = jnp.zeros_like(da_s)
        nad_s[...] = jnp.broadcast_to(-jnp.exp(fine(hv[...], spot[...])[1:2]), (8, 128))
        cvg_o[...] = jnp.zeros_like(cvg_o)
        csg_o[...] = jnp.zeros_like(csg_o)
        head_o[...] = jnp.zeros_like(head_o)

    lane = lanes_of(SPAN)
    low_half = lane < HEAD_DIM
    col = col_r[...]
    row = row_r[...]
    end = jnp.broadcast_to(col[SPAN - 1 : SPAN], (8, 128))
    end1 = pltpu.roll(end, GROUP, 1)
    w = jnp.exp2(jnp.where(lane < 32, col, jnp.where(lane < 64, end1[0:1] - col, 0.0)))
    dec = jnp.exp2(jnp.where(lanes_of(8) < 32, end, 0.0))
    high = dec.astype(BF).astype(F32)
    inner = jnp.exp2(jnp.where(lane < 32, end[0:1] - col, jnp.where(lane < 64, col, 0.0)))
    steps = pltpu.roll(col, 64, 1)
    wall = jnp.concatenate([w, inner, steps, high, dec - high], axis=0).astype(BF)
    bc = bc_r[...]
    bmf, cmf = bc[:, :STATE], bc[:, STATE:]
    bm, cm = bmf.astype(BF), cmf.astype(BF)
    nad = nad_s[0:1]
    enters_b = jnp.where(sc[6] == 1, 1.0, 0.0)
    square_r = lax.broadcasted_iota(jnp.int32, (SPAN, SPAN), 0)
    off = square_r != lane
    aff = jnp.where(off, fine_nt(bmf, cmf), 0.0)

    daff = jnp.zeros((SPAN, SPAN), F32)
    red = jnp.zeros((SPAN, 128), F32)
    whole = jnp.zeros((SPAN, 128), F32)
    ddt = jnp.zeros((SPAN, 128), F32)
    dc = jnp.zeros((SPAN, STATE), F32)
    db = jnp.zeros((SPAN, STATE), F32)
    for p in range(pairs):
        sl = slice(p * 128, (p + 1) * 128)
        two = slice(p * 256, (p + 1) * 256)
        efd = dot(wall, e01[:, two])
        ef, eb = efd[:SPAN, :128], efd[:SPAN, 128:]
        wf, wb = efd[SPAN : 2 * SPAN, :128], efd[SPAN : 2 * SPAN, 128:]
        dte = efd[2 * SPAN : 3 * SPAN, :128]
        decay = efd[3 * SPAN : 3 * SPAN + 1, :128] + efd[3 * SPAN + 8 : 3 * SPAN + 9, :128]
        sf, sb = sf_r[0, :, sl], sb_r[0, :, sl]
        gf32 = gf_s[:, sl] * last
        gbd, at = gbds(p)
        arrived = gbd[:, at].astype(F32) * enters_b
        gb32 = gbl[0, :, sl].astype(F32) + pg[0, 0:1, sl] * arrived
        gf, gb = gf32.astype(BF), gb32.astype(BF)
        gf_s[:, sl] = gf32 * decay + dff[0, :, sl].astype(F32)
        cross = (sf.astype(F32) * gf32 + sb.astype(F32) * gb32) * decay
        cross_s[:, sl] = jnp.broadcast_to(jnp.sum(cross, axis=0, keepdims=True), (8, 128))
        xp = xpres(p)[0][:, at].astype(F32)
        sg = sigmoid(xp)
        x = xp * sg
        xd = x * dte
        dy = dy_r[:, sl].astype(F32)
        efdy, ebdy = ef * dy, eb * dy
        wfxd, wbxd = wf * xd, wb * xd
        s_both, g_both = side(sf, sb), side(gf, gb)
        fed = dot(bm, g_both)
        cf, cb = wf * fed[:, :128], wb * fed[:, 128:]
        carried = dot(cm, s_both)
        edy = side(efdy, ebdy)
        dc = dc + dot_nt(edy.astype(BF), s_both)
        db = db + dot_nt(side(wfxd, wbxd).astype(BF), g_both)
        products = side((edy * carried).astype(BF), side(xd * cf, xd * cb).astype(BF))
        red = red + dot(products, seg4[p * 512 : (p + 1) * 512, :])
        bd = jnp.concatenate(
            [jnp.where(low_half, dy, 0.0), jnp.where(low_half, 0.0, dy)], axis=0
        ).astype(BF)
        dm = dot_nt(xd.astype(BF), bd)
        ms = []
        for k in range(2):
            h = 2 * p + k
            spread = jnp.minimum(
                row[h : h + 1, :] - col[:, h : h + 1],
                col[:, GROUP + h : GROUP + h + 1] - row[GROUP + h : GROUP + h + 1, :],
            )
            f = jnp.exp2(spread)
            m = aff * f
            ms.append(m.astype(BF))
            dmh = dm[:, k * 128 : (k + 1) * 128]
            daff = daff + f * dmh
            q = m * dmh
            ql = jnp.where(square_r < lane, q, 0.0)
            qu = q - ql
            da_s[h : h + 1, :] = jnp.sum(ql, axis=0, keepdims=True)
            da_s[GROUP + h : GROUP + h + 1, :] = jnp.sum(qu, axis=0, keepdims=True)
            whole = jnp.where(lane == h, jnp.sum(ql, axis=1, keepdims=True), whole)
            whole = jnp.where(lane == GROUP + h, jnp.sum(qu, axis=1, keepdims=True), whole)
        dxd = dot(jnp.concatenate(ms, axis=1), bd) + cf + cb
        ddt = ddt + dot(high_low(x * dxd), seg2[two, :])
        dx = dte * dxd + skip[:, sl] * dy
        dxp = dx * (sg * (1.0 + xp * (1.0 - sg)))
        ext = jnp.concatenate([dxp, edge_s[:, sl] * last], axis=0)
        edge_s[:, sl] = dxp[:8]
        v = vs(p)[0][:, at].astype(F32)
        dv = jnp.zeros((SPAN, 128), F32)
        for j in range(TAPS):
            moved = shifted(ext, j, SPAN)
            k = TAPS - 1 - j
            dv = dv + moved * cv[k : k + 1, sl]
            cvg_o[k : k + 1, sl] += jnp.sum(v * moved, axis=0, keepdims=True)
        dv_o[:, sl] = dv.astype(BF)

    dafb = jnp.where(off, daff, 0.0).astype(BF)
    db = db + dot(dafb, cm)
    dc = dc + dot_tn(dafb, bm)
    dbc = jnp.concatenate([db, dc], axis=1)
    pp = pspre_r[...]
    sp = sigmoid(pp)
    dpp = dbc * (sp * (1.0 + pp * (1.0 - sp)))
    ext = jnp.concatenate([dpp, edges_s[...] * last], axis=0)
    edges_s[...] = dpp[:8]
    ps = ps_r[...]
    dst = jnp.zeros((SPAN, 128), F32)
    for j in range(TAPS):
        moved = shifted(ext, j, SPAN)
        k = TAPS - 1 - j
        dst = dst + moved * cs[k : k + 1, :]
        csg_o[k : k + 1, :] += jnp.sum(ps * moved, axis=0, keepdims=True)
    dst_o[...] = dst.astype(BF)

    red = red - whole + jnp.transpose(da_s[...])
    hi = red.astype(BF)
    lo = (red - hi.astype(F32)).astype(BF)
    summed = dot(tris[...], hi) + dot(tris[...], lo)
    parts = [summed[g * SPAN : (g + 1) * SPAN] for g in range(4)]
    picked = jnp.where(
        lane < 32, parts[0], jnp.where(lane < 64, parts[1], jnp.where(lane < 96, parts[2], parts[3]))
    )
    total = picked + pltpu.roll(picked, 64, 1)
    total = total + pltpu.roll(total, 32, 1)
    crossed = cross_s[...]
    crossed_hi = crossed.astype(BF)
    crossed_lo = (crossed - crossed_hi.astype(F32)).astype(BF)
    da = total + (dot(crossed_hi, segs[...]) + dot(crossed_lo, segs[...]))[0:1]
    dz = (ddt + da * nad) * col
    dz = jnp.where((lane >= 96) & (lane < 96 + heads), dz, 0.0)
    dz_o[...] = dz.astype(BF)
    head_o[0:1, :] += jnp.sum(da * col * nad, axis=0, keepdims=True)
    head_o[1:2, :] += jnp.sum(dz, axis=0, keepdims=True)

    @pl.when(i == 0)
    def _():
        edge_o[...] = edge_s[...]
        edges_o[...] = edges_s[...]


def back(heads, sc, split, dy, bc, ps, pspre, col, row, sf, sb, gbl, pg, dff, skip, cv, cs, hv, spot):
    tokens, width = dy.shape
    groups = len(split[0])
    part = width // groups
    blocks = tokens // SPAN
    maps = expanders(heads)
    every = sum(maps)
    seg4 = by_pairs([m.T for m in maps], 0)
    seg2 = by_pairs([every.T, every.T], 0)
    segs = every.T
    at = np.arange(SPAN)
    row_at, col_at = at[:, None], at[None, :]
    tris = np.concatenate(
        [col_at >= row_at, col_at <= row_at, col_at < row_at, col_at > row_at], axis=0
    ).astype(np.float32)
    e01 = by_pairs(maps[:2], 1)

    def rev(shape):
        rank = len(shape)
        return pl.BlockSpec(shape, lambda i: (blocks - 1 - i,) + (0,) * (rank - 1))

    sds = jax.ShapeDtypeStruct
    state = (1, STATE, width)
    outs = [
        (sds((tokens, width), BF), rev((SPAN, width))),
        (sds((tokens, 128), BF), rev((SPAN, 128))),
        (sds((tokens, 128), BF), rev((SPAN, 128))),
        (sds((TAPS, width), F32), full((TAPS, width))),
        (sds((TAPS, 128), F32), full((TAPS, 128))),
        (sds((8, 128), F32), full((8, 128))),
        (sds((8, width), F32), full((8, width))),
        (sds((8, 128), F32), full((8, 128))),
    ]
    shared = [skip, cv, cs, hv, spot]
    shared += [jnp.asarray(m, BF) for m in (e01, seg4, seg2, segs, tris)]
    in_specs = [SMEM] + [rev((SPAN, part))] * (2 * groups)
    in_specs += [full((STATE, part))] * (2 * groups)
    in_specs += [rev((SPAN, width))] + [rev((SPAN, 128))] * 5
    in_specs += [rev(state)] * 3 + [rev((1, 8, width)), rev(state)]
    in_specs += [full(a.shape) for a in shared]
    return pl.pallas_call(
        functools.partial(back_kernel, heads, groups),
        grid=(blocks,),
        in_specs=in_specs,
        out_specs=[spec for _, spec in outs],
        out_shape=[shape for shape, _ in outs],
        scratch_shapes=[
            pltpu.VMEM((STATE, width), F32),
            pltpu.VMEM((8, width), F32),
            pltpu.VMEM((8, 128), F32),
            pltpu.VMEM((128, 128), F32),
            pltpu.VMEM((8, width), F32),
            pltpu.VMEM((8, 128), F32),
        ],
        compiler_params=pltpu.CompilerParams(vmem_limit_bytes=58 * 1024 * 1024),
        cost_estimate=cost(100),
        name="back",
    )(
        sc, *[a for kind in split for a in kind],
        dy, bc, ps, pspre, col, row, sf, sb, gbl, pg, dff, *shared,
    )


def input_kernel(groups, *refs):
    refs = list(refs)
    slabs = refs[:groups]
    dgate, dv, dst, dz, ws, steps_t, gain, place, hid, gout, grad_o, gain_o, wg, wv, wst = refs[groups:]

    @pl.when(pl.program_id(0) == 0)
    def _():
        gain_o[...] = jnp.zeros_like(gain_o)
        wst[...] = dot_tn(place[...].astype(BF), steps_t[...]).astype(BF)
        pairs_in = slabs[0].shape[0] // 2
        for p in range(groups * pairs_in):
            slab, h = slabs[p // pairs_in], 2 * (p % pairs_in)
            g, v = unpaired(slab[h].astype(F32), slab[h + 1].astype(F32))
            wg[:, p * 128 : (p + 1) * 128] = g.astype(BF)
            wv[:, p * 128 : (p + 1) * 128] = v.astype(BF)

    dn = dot_nt(dst[...], ws[...]) + dot(dz[...], wst[...])
    dn = dn + dot_nt(dgate[...], wg[...]) + dot_nt(dv[...], wv[...])
    u = hid[...].astype(F32)
    scale = lax.rsqrt(jnp.mean(u * u, axis=1, keepdims=True) + EPS)
    unit = u * scale
    gain_o[...] += jnp.sum(dn * unit, axis=0, keepdims=True)
    du = dn * gain[...]
    inner = jnp.mean(du * unit, axis=1, keepdims=True)
    grad_o[...] = (gout[...].astype(F32) + scale * (du - unit * inner)).astype(BF)


def input_side(slabs, dgate, dv, dst, dz, ws, steps_t, gain, hidden, out_grad):
    tokens, width_in = hidden.shape
    tile = min(512, tokens)

    def rows(a):
        return pl.BlockSpec((tile, a.shape[1]), lambda i: (i, 0))

    sds = jax.ShapeDtypeStruct
    fixed = list(slabs)
    width = dgate.shape[1]
    streams = [dgate, dv, dst, dz]
    specs = [full(a.shape) for a in fixed] + [rows(a) for a in streams]
    place = placing(steps_t.shape[0], (3,))
    specs += [full(a.shape) for a in (ws, steps_t, gain, place)] + [rows(hidden), rows(out_grad)]
    return pl.pallas_call(
        functools.partial(input_kernel, len(slabs)),
        grid=(tokens // tile,),
        in_specs=specs,
        out_specs=[rows(hidden), full((1, width_in))],
        out_shape=[sds((tokens, width_in), BF), sds((1, width_in), F32)],
        scratch_shapes=[pltpu.VMEM((width_in, width), BF)] * 2 + [pltpu.VMEM((128, width_in), BF)],
        compiler_params=pltpu.CompilerParams(vmem_limit_bytes=58 * 1024 * 1024),
        cost_estimate=cost(15),
        name="input_side",
    )(*fixed, *streams, ws, steps_t, gain, place, hidden, out_grad)


def reduce_kernel(bits, lanes, mats, *refs):
    n_mats = len(mats)
    srcs, both, tiny = refs[:n_mats], refs[n_mats], refs[n_mats + 1]
    paired_o, last_o, both_o, tiny_o = refs[n_mats + 2 : n_mats + 6]
    outs = (*refs[n_mats + 6 : n_mats + 8], last_o)
    scratch = refs[n_mats + 8 :]
    own_r, sent = scratch[0], scratch[1]
    halves, parts = scratch[2 : 2 + bits], scratch[2 + bits : 1 + 2 * bits]
    tiny_r, tiny_s, send_s, recv_s, tsend_s, trecv_s = scratch[1 + 2 * bits :]
    rows = srcs[0].shape[0] if mats[0] == "cols" else srcs[0].shape[0] // 2
    width = outs[0].shape[1]
    me = lax.axis_index("dp")
    chan = lax.axis_index("chan")
    bit = [lax.rem(lax.div(me, 2**k), 2) for k in range(bits)]
    partner = [{"dp": me + (1 - 2 * bit[k]) * 2**k} for k in range(bits)]
    across = {"chan": 1 - chan}
    stages = [partner[0], across] + partner[1:]

    barrier = pltpu.get_barrier_semaphore()
    for device in stages:
        pl.semaphore_signal(barrier, inc=1, device_id=device, device_id_type=pl.DeviceIdType.MESH)
    pl.semaphore_wait(barrier, bits + 1)

    chunks = [(m, s) for m in range(n_mats) for s in range(0, width, lanes)]
    mains = len(chunks)
    n = mains + both.shape[1] // lanes
    half = rows // 2

    def mult(v):
        return pl.multiple_of(v, 16)

    def source(c, which, part):
        if c >= mains:
            return both.at[pl.ds(mult(part * half), half), pl.ds((c - mains) * lanes, lanes)]
        m, s = chunks[c]
        if mats[m] == "cols":
            return srcs[m].at[pl.ds(mult(part * half), half), pl.ds(which * width + s, lanes)]
        return srcs[m].at[pl.ds(mult(which * rows + part * half), half), pl.ds(s, lanes)]

    def target(c, start, size):
        if c >= mains:
            return both_o.at[pl.ds(mult(start), size), pl.ds((c - mains) * lanes, lanes)]
        m, s = chunks[c]
        return outs[m].at[pl.ds(mult(start), size), pl.ds(s, lanes)]

    def copy(src, dst, c, k, device):
        return pltpu.make_async_remote_copy(
            src_ref=src,
            dst_ref=dst,
            send_sem=send_s.at[c, k],
            recv_sem=recv_s.at[c, k],
            device_id=device,
            device_id_type=pl.DeviceIdType.MESH,
        )

    offset = [bit[0] * half]
    for k in range(1, bits):
        offset.append(offset[-1] + bit[k] * (half >> k))

    def first(c, which):
        if c >= mains and which == 0:
            return None
        slot = own_r.at[c, which]
        return copy(source(c, which, 1 - bit[0]), slot, c, which, partner[0])

    def second(c):
        return copy(sent.at[c], halves[0].at[c], c, 2, across)

    def halving(c, k):
        size = half >> k
        src = parts[k - 1].at[c, pl.ds(mult((1 - bit[k]) * size), size), :]
        return copy(src, halves[k].at[c], c, 2 + k, partner[k])

    def doubling(c, k):
        size = half >> k
        place = target(c, offset[k], size)
        return copy(place, place, c, 2 + bits + k, partner[k])

    def f32(ref):
        return ref[...].astype(F32)

    def stage(c, s):
        if s == 0:
            for which in (0, 1):
                rdma = first(c, which)
                if rdma is not None:
                    rdma.start()
        elif s == 1:
            first(c, 1).wait_recv()
            sent[c] = (f32(source(c, 1, bit[0])) + f32(own_r.at[c, 1])).astype(BF)
            second(c).start()
        elif s == 2:
            second(c).wait_recv()
            if c >= mains:
                total = f32(sent.at[c]) + f32(halves[0].at[c])
            else:
                first(c, 0).wait_recv()
                total = f32(source(c, 0, bit[0])) + f32(own_r.at[c, 0]) + f32(halves[0].at[c])
            parts[0][c] = total.astype(BF)
            halving(c, 1).start()
        elif s < bits + 2:
            k = s - 2
            size = half >> k
            halving(c, k).wait_recv()
            kept = parts[k - 1].at[c, pl.ds(mult(bit[k] * size), size), :]
            total = (f32(kept) + f32(halves[k].at[c])).astype(BF)
            if k < bits - 1:
                parts[k][c] = total
                halving(c, k + 1).start()
            else:
                target(c, offset[k], size)[...] = total
                doubling(c, k).start()
        else:
            k = 2 * bits + 1 - s
            doubling(c, k).wait_recv()
            if k > 0:
                doubling(c, k - 1).start()

    def tiny_copy(k):
        return pltpu.make_async_remote_copy(
            src_ref=tiny if k == 0 else tiny_s.at[k - 1],
            dst_ref=tiny_r.at[k],
            send_sem=tsend_s.at[k],
            recv_sem=trecv_s.at[k],
            device_id=stages[k],
            device_id_type=pl.DeviceIdType.MESH,
        )

    tiny_copy(0).start()
    last = 2 * bits + 1
    for tick in range(n + SLACK * last):
        for s in range(last, -1, -1):
            c = tick - SLACK * s
            if 0 <= c < n:
                stage(c, s)
        if 1 <= tick <= bits + 1:
            k = tick - 1
            tiny_copy(k).wait_recv()
            before = tiny[...] if k == 0 else tiny_s[k - 1]
            total = before + tiny_r[k]
            if k < bits:
                tiny_s[k] = total
                tiny_copy(k + 1).start()
            else:
                tiny_o[...] = total

    low_half = lanes_of(rows) < HEAD_DIM
    for p in range(width // 128):
        sl = slice(p * 128, (p + 1) * 128)
        g, v = f32(outs[0].at[:, sl]), f32(outs[1].at[:, sl])
        paired_o[2 * p] = jnp.where(low_half, g, pltpu.roll(v, 64, 1))
        paired_o[2 * p + 1] = jnp.where(low_half, pltpu.roll(g, 64, 1), v)

    for c in range(n):
        for which in (0, 1):
            rdma = first(c, which)
            if rdma is not None:
                rdma.wait_send()
        second(c).wait_send()
        for k in range(1, bits):
            halving(c, k).wait_send()
        for k in range(bits):
            doubling(c, k).wait_send()
    for k in range(bits + 1):
        tiny_copy(k).wait_send()


def reduce_all(bits, mats, both, tiny, lanes):
    kinds = [kind for _, kind in mats]
    arrays = [a for a, _ in mats]
    rows = arrays[0].shape[0] if kinds[0] == "cols" else arrays[0].shape[0] // 2
    width = arrays[0].shape[1] // 2 if kinds[0] == "cols" else arrays[0].shape[1]
    half = rows // 2
    n = len(arrays) * (width // lanes) + both.shape[1] // lanes
    vmem = pl.BlockSpec(memory_space=pltpu.VMEM)
    sds = jax.ShapeDtypeStruct
    scratch = [pltpu.VMEM((rows, width), BF)] * 2
    scratch += [pltpu.VMEM((n, 2, half, lanes), BF), pltpu.VMEM((n, half, lanes), BF)]
    scratch += [pltpu.VMEM((n, half >> k, lanes), BF) for k in range(bits)]
    scratch += [pltpu.VMEM((n, half >> k, lanes), BF) for k in range(bits - 1)]
    scratch += [
        pltpu.VMEM((bits + 1,) + tiny.shape, F32),
        pltpu.VMEM((bits,) + tiny.shape, F32),
        pltpu.SemaphoreType.DMA((n, 2 + 2 * bits)),
        pltpu.SemaphoreType.DMA((n, 2 + 2 * bits)),
        pltpu.SemaphoreType.DMA((bits + 1,)),
        pltpu.SemaphoreType.DMA((bits + 1,)),
    ]
    return pl.pallas_call(
        functools.partial(reduce_kernel, bits, lanes, kinds),
        out_shape=[
            sds((width // HEAD_DIM, rows, 128), F32), sds((rows, width), BF), sds(both.shape, BF), sds(tiny.shape, F32)
        ],
        in_specs=[vmem] * (len(arrays) + 2),
        out_specs=[vmem] * 4,
        scratch_shapes=scratch,
        compiler_params=pltpu.CompilerParams(
            collective_id=0, has_side_effects=True, vmem_limit_bytes=58 * 1024 * 1024
        ),
        name="reduce_all",
    )(*arrays, both, tiny)


def handed(total, passed, shards, up):
    pairs = [(k, k + 1) if up else (k + 1, k) for k in range(shards - 1)]
    entering = lax.ppermute(total.astype(BF), "chan", pairs)
    for _ in range(shards - 2):
        now = total + passed[0:1] * entering.astype(F32)
        entering = lax.ppermute(now.astype(BF), "chan", pairs)
    return entering


def swap(v):
    return lax.ppermute(v, "chan", [(0, 1), (1, 0)])


def core_swap(v):
    size = lax.axis_size("dp")
    return lax.ppermute(v, "dp", [(k, k ^ 1) for k in range(size)])


def on_device(
    hidden_in, norm_gain, gate_value_weight, state_weight, step_weight, value_conv, state_conv,
    step_bias, decay_log, skip_gain, gate_gain, out_weight, seq_length, seq_count, out_grad,
):
    tokens, width_in = hidden_in.shape
    channel = lax.axis_index("chan")
    shards = lax.axis_size("chan")
    groups_dp = lax.axis_size("dp")
    length, count = seq_length[0], seq_count[0]
    local_heads = gate_value_weight.shape[1]
    local = local_heads * HEAD_DIM
    heads = local_heads * shards
    width = heads * HEAD_DIM
    paired = shards == 2 and local_heads % 4 == 0 and groups_dp % 2 == 0
    one = jnp.ones((), jnp.int32)
    flags = [channel, 1 - channel, 1 - channel, channel] if paired else [one] * 4
    sc = jnp.stack([channel * tokens, length, count] + flags).astype(jnp.int32)
    ups = [(k, k + 1) for k in range(shards - 1)]
    downs = [(k + 1, k) for k in range(shards - 1)]
    gain = norm_gain[None]

    slab = gate_value_weight.transpose(1, 0, 2)
    edge = lax.ppermute(hidden_in[tokens - PAD :], "chan", ups)
    hv = jnp.stack([step_bias, decay_log, skip_gain])
    small = jnp.concatenate(
        [
            value_conv,
            gate_gain[None],
            jnp.pad(hv, ((0, 0), (0, local - local_heads))),
        ]
    )

    each_map = expanders(heads)
    e0, e1, _, _ = [jnp.asarray(e, BF) for e in each_map]
    e01 = jnp.asarray(by_pairs(each_map[:2], 1), BF)
    maps = (gain, state_weight, state_conv)
    if paired:
        core = lax.axis_index("dp") % 2
        half = lax.dynamic_slice_in_dim(slab, core * (local_heads // 2), local_heads // 2, 0)
        payload, edge = lax.optimization_barrier((half, edge))
        come = swap(payload)
        small_b, wstep_b, ow_b = swap(small), swap(step_weight), swap(out_weight)
        gate, v, xpre, ff, sbl, pb, _, _, _, _, hand, vh, normed, nedge, ps, pspre, bc, psh = project(
            sc, hidden_in, edge, slab, step_weight.T, value_conv, hv,
            e0[:, :local], e1[:, :local], maps=maps, final=False,
        )
        come, small_b, wstep_b, ow_b, nedge, hand = lax.optimization_barrier(
            (come, small_b, wstep_b, ow_b, nedge, hand)
        )
        also = core_swap(come)
        enter_b = swap(hand)
        halves = jnp.where(core == 0, jnp.stack([come, also]), jnp.stack([also, come]))
        slabs = [slab, halves.reshape(slab.shape)]
        smalls = [small, small_b]
        steps_t = jnp.concatenate([step_weight.T, wstep_b.T], axis=0)
        ow = jnp.concatenate([out_weight, ow_b], axis=0)
    else:
        slabs = [lax.all_gather(slab, "chan", axis=0, tiled=True)]
        gathered = lax.all_gather(small, "chan", axis=0)
        smalls = [gathered[k] for k in range(shards)]
        steps_t = lax.all_gather(step_weight.T, "chan", axis=0, tiled=True)
        ow = lax.all_gather(out_weight, "chan", axis=0, tiled=True)

    hv_all = jnp.concatenate([p[TAPS + 1 :, :local_heads] for p in smalls], axis=1)
    cv = jnp.concatenate([p[:TAPS] for p in smalls], axis=1)
    ggain = jnp.concatenate([p[TAPS : TAPS + 1] for p in smalls], axis=1)
    skip = jnp.repeat(hv_all[2:3], HEAD_DIM, axis=1)

    if paired:
        gate2, v2, xpre2, ff2, sbl2, pb2, _, _, _, _, hand2, vh2, col, row = project(
            sc, normed, nedge, slabs[1], steps_t, smalls[1][:TAPS], hv_all,
            e0[:, local:], e1[:, local:], bc=bc, final=True,
        )
        enter = [swap(hand2), enter_b]
        split = [[gate, gate2], [xpre, xpre2], [ff, ff2], [sbl, sbl2], [pb, pb2], enter, enter]
        vs, xs = [v, v2], [xpre, xpre2]
        vh = jnp.concatenate([vh, vh2], axis=1)
    else:
        (
            gate, v, xpre, ff, sbl, pb, sft, sbt, pft, pbt, _, vh, normed, nedge, ps, pspre, bc, psh,
            col, row,
        ) = project(
            sc, hidden_in, edge, slabs[0], steps_t, cv, hv_all, e0, e1, maps=maps,
        )
        sfd = handed(sft, pft, shards, True)
        sbd = handed(sbt, pbt, shards, False)
        split = [[gate], [xpre], [ff], [sbl], [pb], [sfd], [sbd]]
        vs, xs = [v], [xpre]
    (
        output, gnorm, dy, dgate, sf, sb, gbl, pg, dff, gft, gbt, pgf, pgb, hand, ggain_grad, skip_grad,
    ) = mix(sc, split, bc, col, row, hidden_in, out_grad, ow, ow.T, ggain, skip, e01)
    if paired:
        enter = swap(hand)
        enter = [enter[:, local:], enter[:, :local]]
        gfds = gbds = enter
    else:
        gfds = [handed(gft, pgf, shards, False)]
        gbds = [handed(gbt, pgb, shards, True)]

    own_ids = channel * tokens + jnp.arange(tokens, dtype=jnp.int32)
    live = jnp.where(own_ids // length < count, 1.0, 0.0)[:, None].astype(BF)
    ow_grad = dot_tn(gnorm, out_grad * live).astype(BF)
    dwg = dot_tn(normed, dgate).astype(BF)

    def absolute(parts, axis):
        if not paired:
            return jnp.concatenate(parts, axis=axis)
        a = jnp.concatenate(parts, axis=axis)
        b = jnp.concatenate(parts[::-1], axis=axis)
        return jnp.where(channel == 0, a, b)

    def shared(v, axis):
        if paired:
            a, b = jnp.split(v, 2, axis=axis)
            v = (a.astype(F32) + swap(b).astype(F32)).astype(BF)
        else:
            v = lax.psum_scatter(v, "chan", scatter_dimension=axis, tiled=True)
        return lax.psum(v, "dp")

    dv, dst, dz, cvg, csg, head_sums, edge_g, edges_g = back(
        heads, sc, [xs, vs, gfds, gbds], dy, bc, ps, pspre, col, row, sf, sb, gbl, pg, dff, skip, cv,
        state_conv, hv_all, placing(heads),
    )

    if paired:
        turned = jnp.concatenate([edge_g[:, local:], edge_g[:, :local]], axis=1)
    else:
        turned = edge_g
    kernel = jnp.concatenate([cv, state_conv], axis=1)
    past = jnp.concatenate([vh, psh], axis=1)
    reach = TAPS - 1
    after = lax.ppermute(jnp.concatenate([turned, edges_g], axis=1), "chan", downs)[:reach]
    joined = jnp.concatenate([edge_g, edges_g], axis=1)
    after = after * jnp.where(((channel + 1) * tokens) % length == 0, 0.0, 1.0)
    patch = jnp.zeros((reach, joined.shape[1]), F32)
    taps = []
    for j in range(TAPS):
        if j:
            moved = jnp.pad(after[:j], ((reach - j, 0), (0, 0)))
            patch = patch + moved * kernel[TAPS - 1 - j][None]
        taps.append(jnp.sum(joined[:j] * past[PAD - j :], axis=0))
    cross_taps = jnp.stack(taps[::-1])
    tail = jnp.pad(patch, ((PAD - reach, 0), (0, 0))).astype(BF)
    dv = dv.at[tokens - PAD :].add(tail[:, :width])
    dst = dst.at[tokens - PAD :].add(tail[:, width:])
    cvg = cvg + cross_taps[:, :width]
    csg = csg + cross_taps[:, width:]

    dwv = dot_tn(normed, dv).astype(BF)
    dws = dot_tn(normed, dst)
    dwst = dot_tn(normed, dz)[:, 96 : 96 + heads]
    input_grad, norm_gain_grad = input_side(
        slabs, dgate, dv, dst, dz, state_weight, steps_t, gain, hidden_in, out_grad
    )

    bias_sum = head_sums[1, 96 : 96 + heads]
    dlog_sum = head_sums[0, 64 : 64 + heads]
    skip_sum = skip_grad.reshape(heads, HEAD_DIM).sum(axis=1)

    def by_shard(k):
        cut, hcut = slice(k * local, (k + 1) * local), slice(k * local_heads, (k + 1) * local_heads)
        return jnp.concatenate(
            [cvg[:, cut].reshape(-1), ggain_grad[0, cut], bias_sum[hcut], dlog_sum[hcut], skip_sum[hcut]]
        )

    each = (TAPS + 1) * local + 3 * local_heads
    pad_each = -each % 128
    tiny = absolute([jnp.pad(by_shard(k), (0, pad_each)) for k in range(shards)], 0)
    tiny = jnp.concatenate([tiny, norm_gain_grad[0], csg.reshape(-1)])
    tiny = jnp.pad(tiny, (0, -tiny.shape[0] % 1024)).reshape(-1, 128)
    dwst = absolute([dwst[:, k * local_heads : (k + 1) * local_heads] for k in range(shards)], 1)
    both = jnp.concatenate([dws, jnp.pad(dwst, ((0, 0), (0, 128 - heads)))], axis=1).astype(BF)

    bits = groups_dp.bit_length() - 1
    if paired and groups_dp == 2**bits and bits >= 2 and width_in % (16 * groups_dp) == 0:
        gvw, owg, both, tiny = reduce_all(
            bits, [(dwg, "cols"), (dwv, "cols"), (ow_grad, "rows")], both, tiny, LANES
        )
        gvw = gvw.transpose(1, 0, 2)
        owg = owg.astype(F32)
    else:
        dwg, dwv, owg = shared(dwg, 1), shared(dwv, 1), shared(ow_grad, 0).astype(F32)
        both, tiny = lax.psum((both, tiny), ("dp", "chan"))
        pieces = [a.reshape(width_in, local_heads, HEAD_DIM) for a in (dwg, dwv)]
        gvw = jnp.concatenate(pieces, axis=2).astype(F32)
    both = both.astype(F32)
    flat = tiny.reshape(-1)
    base = (each + pad_each) * shards
    mine = lax.dynamic_slice_in_dim(flat, channel * (each + pad_each), each, 0)
    cuts = np.cumsum([TAPS * local, local, local_heads, local_heads])
    dwst = lax.dynamic_slice_in_dim(both[:, 128:], channel * local_heads, local_heads, 1)
    return (
        output,
        input_grad,
        flat[base : base + width_in],
        gvw,
        both[:, :128],
        dwst,
        mine[: cuts[0]].reshape(TAPS, local),
        flat[base + width_in : base + width_in + TAPS * 128].reshape(TAPS, 128),
        mine[cuts[1] : cuts[2]],
        mine[cuts[2] : cuts[3]],
        mine[cuts[3] :],
        mine[cuts[0] : cuts[1]],
        owg,
    )


def solution(mesh):
    in_specs = (
        P(("dp", "chan"), None),
        P(),
        P(None, "chan", None),
        P(),
        P(None, "chan"),
        P(None, "chan"),
        P(),
        P("chan"),
        P("chan"),
        P("chan"),
        P("chan"),
        P("chan", None),
        P("dp"),
        P("dp"),
        P(("dp", "chan"), None),
    )
    out_specs = (
        P(("dp", "chan"), None),
        P(("dp", "chan"), None),
        P(),
        P(None, "chan", None),
        P(),
        P(None, "chan"),
        P(None, "chan"),
        P(),
        P("chan"),
        P("chan"),
        P("chan"),
        P("chan"),
        P("chan", None),
    )
    return jax.shard_map(
        on_device, mesh=mesh, in_specs=in_specs, out_specs=out_specs, check_vma=False
    )
```

```python
import functools

import jax
import jax.numpy as jnp
import numpy as np
from jax import lax
from jax.experimental import pallas as pl
from jax.experimental.pallas import tpu as pltpu
from jax.sharding import PartitionSpec as P

HEAD_DIM = 64
STATE = 64
SPAN = 128
PAD = 16
GROUP = 32
TAPS = 4
LANES = 128
SLACK = 2
EPS = 1e-05
LOG2E = float(np.log2(np.e))
BF = jnp.bfloat16
F32 = jnp.float32


def dot(a, b):
    return jnp.dot(a, b, preferred_element_type=F32)


def dot_nt(a, b):
    return lax.dot_general(a, b, (((1,), (1,)), ((), ())), preferred_element_type=F32)


def dot_tn(a, b):
    return lax.dot_general(a, b, (((0,), (0,)), ((), ())), preferred_element_type=F32)


def fine_nt(a, b):
    return lax.dot_general(
        a, b, (((1,), (1,)), ((), ())), precision=lax.Precision.HIGHEST, preferred_element_type=F32
    )


def fine(a, b):
    return jnp.dot(a, b, precision=lax.Precision.HIGHEST, preferred_element_type=F32)


def sigmoid(v):
    return 0.5 + 0.5 * jnp.tanh(0.5 * v)


def lanes_of(rows):
    return lax.broadcasted_iota(jnp.int32, (rows, 128), 1)


def shifted(ext, offset, rows):
    return ext[offset : offset + rows]


def full(shape):
    rank = len(shape)
    return pl.BlockSpec(shape, lambda i: (0,) * rank)


SMEM = pl.BlockSpec(memory_space=pltpu.SMEM)


def placing(heads, groups=range(4)):
    lane, head = np.arange(128)[None], np.arange(heads)[:, None]
    hits = sum((lane == GROUP * g + head).astype(np.float32) for g in groups)
    return jnp.asarray(hits)


def cost(micros):
    return pl.CostEstimate(flops=int(micros * 1e9), bytes_accessed=1024, transcendentals=0)


def side(a, b):
    return jnp.concatenate([a, b], axis=1)


def high_low(v):
    hi = v.astype(BF)
    return side(hi, (v - hi.astype(F32)).astype(BF))


def by_pairs(maps, axis):
    pairs = maps[0].shape[axis] // 128
    pieces = [np.split(m, pairs, axis=axis) for m in maps]
    return np.concatenate([piece[p] for p in range(pairs) for piece in pieces], axis=axis)


def unpaired(a, b):
    low = lanes_of(a.shape[0]) < HEAD_DIM
    return jnp.where(low, a, pltpu.roll(b, 64, 1)), jnp.where(low, pltpu.roll(a, 64, 1), b)


def expanders(heads):
    channel = np.arange(heads * HEAD_DIM) // HEAD_DIM
    lane = np.arange(128)[:, None]
    return [np.asarray(lane == GROUP * g + channel[None], np.float32) for g in range(4)]


def project_kernel(fresh, final, tile, chunk, *refs):
    refs = list(refs)

    def take(count):
        return [refs.pop(0) for _ in range(count)]

    sc, tokens_r, halo, edge, slabs, steps_t, cv, hv, place_r, tri, e0, e1 = take(12)
    if fresh:
        gain, ws, cs = take(3)
    else:
        (bc_r,) = take(1)
    gate_o, v_o, xpre_o, ff_o, sb_o, pb_o, sft_o, sbt_o, pft_o, pbt_o, hand_o, vh_o = take(12)
    if fresh:
        normed_o, nedge_o, ps_o, pspre_o, bc_o, psh_o = take(6)
    if final:
        col_o, row_o = take(2)
    sb_s, pb_s, sf_s, pf_s, wst, hv_s = take(6)

    step = pl.program_id(0)
    tiles = pl.num_programs(0)
    at = tiles - 1 - step
    length = sc[1]
    start = sc[0] + at * tile
    width = e0.shape[1]
    blocks = tile // SPAN

    @pl.when(step == 0)
    def _():
        sb_s[...] = jnp.zeros_like(sb_s)
        sf_s[...] = jnp.zeros_like(sf_s)
        pb_s[...] = jnp.ones_like(pb_s)
        pf_s[...] = jnp.ones_like(pf_s)
        wst[...] = dot_tn(steps_t[...], place_r[...].astype(BF)).astype(BF)
        rows_hv = fine(hv[...], place_r[...])
        hv_s[0:1] = rows_hv[0:1]
        hv_s[1:2] = -LOG2E * jnp.exp(rows_hv[1:2])

    before = jnp.where(at == 0, edge[...].astype(F32), halo[...].astype(F32))
    rows = jnp.concatenate([before, tokens_r[...].astype(F32)], axis=0)
    keep = jnp.where(lax.rem(start, length) == 0, 0.0, 1.0)
    row_id = lax.broadcasted_iota(jnp.int32, (tile + PAD, 1), 0)
    keep_rows = jnp.where(row_id < PAD, keep, 1.0)
    if fresh:
        scale = lax.rsqrt(jnp.mean(rows * rows, axis=1, keepdims=True) + EPS)
        normed = (rows * scale * gain[...]).astype(BF)
        own = normed[PAD:]
        normed_o[...] = own

        ps = dot(normed, ws[...]) * keep_rows
        ps_o[...] = ps[PAD:]
        pspre = ps[PAD:] * cs[TAPS - 1 : TAPS]
        for j in range(1, TAPS):
            pspre = pspre + shifted(ps, PAD - j, tile) * cs[TAPS - 1 - j : TAPS - j]
        pspre_o[...] = pspre
        bc = pspre * sigmoid(pspre)
        bc_o[...] = bc

        @pl.when(at == 0)
        def _():
            nedge_o[...] = normed[:PAD]
            psh_o[...] = ps[:PAD]

    else:
        normed = rows.astype(BF)
        own = tokens_r[...]
        bc = bc_r[...]

    z = dot(own, wst[...]) + hv_s[0:1]
    dt = jnp.maximum(z, 0.0) + jnp.log1p(jnp.exp(-jnp.abs(z)))
    a2 = dt * hv_s[1:2]
    lane = lanes_of(SPAN)
    if final:
        sig = sigmoid(z)
    wmix, bts = [], []
    for b in range(blocks):
        sl = slice(b * SPAN, (b + 1) * SPAN)
        ab = a2[sl]
        ca = jnp.dot(tri[...], ab, precision=lax.Precision.HIGHEST, preferred_element_type=F32)
        ce = ca - ab
        if final:
            col = jnp.where(
                lane < 32, ca, jnp.where(lane < 64, ce, jnp.where(lane < 96, dt[sl], sig[sl]))
            )
            col_o[sl, :] = col
            row_o[sl, :] = jnp.transpose(col)
        end = ca[SPAN - 1 : SPAN]
        w = jnp.exp2(jnp.where(lane < 32, end - ca, ce)) * dt[sl]
        dec = jnp.broadcast_to(jnp.exp2(end), (8, 128))
        high = dec.astype(BF).astype(F32)
        wmix.append(jnp.concatenate([w, high, dec - high], axis=0).astype(BF))
        bts.append(jnp.transpose(bc[sl])[:STATE].astype(BF))

    for c in range(width // chunk):
        cl = slice(c * chunk, (c + 1) * chunk)
        parts = []
        for h in range(c * chunk // HEAD_DIM, (c + 1) * chunk // HEAD_DIM, 2):
            both = dot(normed, side(slabs[h], slabs[h + 1]))
            parts.append(unpaired(both[:, :128], both[:, 128:]))
        gates = jnp.concatenate([part[0][PAD:] for part in parts], axis=1)
        gate_o[:, cl] = gates.astype(BF)
        v = jnp.concatenate([part[1] for part in parts], axis=1) * keep_rows
        v_o[:, cl] = v[PAD:].astype(BF)

        @pl.when(at == 0)
        def _():
            vh_o[:, cl] = v[:PAD]

        xpre = v[PAD:] * cv[TAPS - 1 : TAPS, cl]
        for j in range(1, TAPS):
            xpre = xpre + shifted(v, PAD - j, tile) * cv[TAPS - 1 - j : TAPS - j, cl]
        xpre_o[:, cl] = xpre.astype(BF)
        x = xpre * sigmoid(xpre)
        for b in reversed(range(blocks)):
            sl = slice(b * SPAN, (b + 1) * SPAN)
            we = dot(wmix[b], e0[:, cl])
            wbe = dot(wmix[b][:SPAN], e1[:, cl])
            dec = we[SPAN : SPAN + 1] + we[SPAN + 8 : SPAN + 9]
            xb = x[sl]
            fresh_f = dot(bts[b], (xb * we[:SPAN]).astype(BF))
            fresh_b = dot(bts[b], (xb * wbe).astype(BF))
            place = start + b * SPAN
            first = jnp.where(lax.rem(place, length) == 0, 0.0, 1.0)
            last = jnp.where(lax.rem(place + SPAN, length) == 0, 0.0, 1.0)
            ff_o[b, :, cl] = fresh_f.astype(BF)
            pf = pf_s[0:1, cl]
            sf_s[:, cl] = sf_s[:, cl] + pf * fresh_f
            pf_s[:, cl] = jnp.broadcast_to(pf * dec * first, (8, chunk))
            held = sb_s[:, cl] * last
            pb = pb_s[0:1, cl] * last
            sb_o[b, :, cl] = held.astype(BF)
            pb_o[b, :, cl] = jnp.broadcast_to(pb, (8, chunk))
            sb_s[:, cl] = held * dec + fresh_b
            pb_s[:, cl] = jnp.broadcast_to(pb * dec, (8, chunk))

    @pl.when(at == 0)
    def _():
        sft_o[...] = sf_s[...]
        sbt_o[...] = sb_s[...]
        pft_o[...] = pf_s[...]
        pbt_o[...] = pb_s[...]
        hand_o[...] = jnp.where(sc[0] == 0, sf_s[...], sb_s[...]).astype(BF)


def project(sc, source, edge, slabs, steps_t, cv, hv, e0, e1, maps=None, bc=None, final=True):
    fresh = maps is not None
    tokens, width_in = source.shape
    width = slabs.shape[0] * HEAD_DIM
    tile = min(512, tokens)
    tiles = tokens // tile
    per = tile // SPAN
    blocks = tokens // SPAN
    chunk = 256 if width % 256 == 0 else 128
    tri = np.tril(np.ones((SPAN, SPAN), np.float32))

    def back(shape):
        rank = len(shape)
        return pl.BlockSpec(shape, lambda i: (tiles - 1 - i,) + (0,) * (rank - 1))

    sds = jax.ShapeDtypeStruct
    wide = (sds((tokens, width), BF), back((tile, width)))
    narrow = (sds((tokens, 128), F32), back((tile, 128)))
    held = (sds((blocks, STATE, width), BF), back((per, STATE, width)))
    total = (sds((STATE, width), F32), full((STATE, width)))
    passed = (sds((8, width), F32), full((8, width)))
    outs = [wide, wide, wide, held, held, (sds((blocks, 8, width), F32), back((per, 8, width)))]
    outs += [total, total, passed, passed, (sds((STATE, width), BF), full((STATE, width)))]
    outs += [(sds((PAD, width), F32), full((PAD, width)))]
    if fresh:
        outs += [
            (sds((tokens, width_in), BF), back((tile, width_in))),
            (sds((PAD, width_in), BF), full((PAD, width_in))),
            narrow,
            narrow,
            narrow,
            (sds((PAD, 128), F32), full((PAD, 128))),
        ]
    if final:
        outs += [narrow, narrow]
    steps = tile // PAD
    args = [sc, source, source, edge, slabs, steps_t, cv, hv, placing(hv.shape[1]), tri, e0, e1]
    in_specs = [
        SMEM,
        back((tile, width_in)),
        pl.BlockSpec((PAD, width_in), lambda i: (jnp.maximum((tiles - 1 - i) * steps - 1, 0), 0)),
    ] + [full(a.shape) for a in args[3:]]
    if fresh:
        args += list(maps)
        in_specs += [full(a.shape) for a in maps]
    else:
        args += [bc]
        in_specs += [back((tile, 128))]
    return pl.pallas_call(
        functools.partial(project_kernel, fresh, final, tile, chunk),
        grid=(tiles,),
        in_specs=in_specs,
        out_specs=[spec for _, spec in outs],
        out_shape=[shape for shape, _ in outs],
        scratch_shapes=[
            pltpu.VMEM((STATE, width), F32),
            pltpu.VMEM((8, width), F32),
            pltpu.VMEM((STATE, width), F32),
            pltpu.VMEM((8, width), F32),
            pltpu.VMEM((width_in, 128), BF),
            pltpu.VMEM((8, 128), F32),
        ],
        compiler_params=pltpu.CompilerParams(vmem_limit_bytes=58 * 1024 * 1024),
        cost_estimate=cost(28),
        name="project",
    )(*args)


def split_refs(refs, groups, kinds):
    taken = [[refs.pop(0) for _ in range(groups)] for _ in range(kinds)]
    return [functools.partial(pick, refs_of) for refs_of in taken]


def pick(refs_of, p):
    per = refs_of[0].shape[-1] // 128
    return refs_of[p // per], slice((p % per) * 128, (p % per + 1) * 128)


def mix_kernel(groups, *refs):
    refs = list(refs)
    sc = refs.pop(0)
    gates, xpres, ffs, sbls, pbs, sfds, sbds = split_refs(refs, groups, 7)
    mix_body(sc, gates, xpres, ffs, sbls, pbs, sfds, sbds, *refs)


def mix_body(
    sc, gates, xpres, ffs, sbls, pbs, sfds, sbds,
    bc_r, col_r, row_r, hid, gout, ow, owt, ggain, skip, e01,
    out_o, gnorm_o, dy_o, dgate_o, sf_o, sb_o, gbl_o, pg_o, dff_o,
    gft_o, gbt_o, pgf_o, pgb_o, hand_o, ggain_o, skip_o,
    sf_s, gb_s, gf_s, pg_s, q_s, y_s, dgn_s, exp_s,
):
    i = pl.program_id(0)
    length = sc[1]
    place = sc[0] + i * SPAN
    first = jnp.where(lax.rem(place, length) == 0, 0.0, 1.0)
    last = jnp.where(lax.rem(place + SPAN, length) == 0, 0.0, 1.0)
    live = jnp.where(lax.div(place, length) < sc[2], 1.0, 0.0)
    width = e01.shape[1] // 2
    pairs = width // 128

    @pl.when(i == 0)
    def _():
        enters_f = jnp.where(sc[3] == 1, 1.0, 0.0)
        for p in range(pairs):
            ref, at = sfds(p)
            sf_s[:, p * 128 : (p + 1) * 128] = ref[:, at].astype(F32) * enters_f
        gb_s[...] = jnp.zeros_like(gb_s)
        gf_s[...] = jnp.zeros_like(gf_s)
        pg_s[...] = jnp.ones_like(pg_s)
        q_s[...] = jnp.ones_like(q_s)
        ggain_o[...] = jnp.zeros_like(ggain_o)
        skip_o[...] = jnp.zeros_like(skip_o)

    enters_b = jnp.where(sc[4] == 1, 1.0, 0.0)
    glow = gout[...].astype(F32) * live
    gl = glow.astype(BF)
    dgn_s[...] = dot(gl, owt[...])

    lane = lanes_of(SPAN)
    low_half = lane < HEAD_DIM
    col = col_r[...]
    row = row_r[...]
    end = jnp.broadcast_to(col[SPAN - 1 : SPAN], (8, 128))
    end1 = pltpu.roll(end, GROUP, 1)
    w = jnp.exp2(jnp.where(lane < 32, col, jnp.where(lane < 64, end1[0:1] - col, 0.0)))
    dec = jnp.exp2(jnp.where(lanes_of(8) < 32, end, 0.0))
    high = dec.astype(BF).astype(F32)
    wmix = jnp.concatenate([w, pltpu.roll(col, 64, 1), high, dec - high], axis=0).astype(BF)
    bc = bc_r[...]
    bmf, cmf = bc[:, :STATE], bc[:, STATE:]
    cm = cmf.astype(BF)
    ct = jnp.transpose(bc)[STATE:].astype(BF)
    square_r = lax.broadcasted_iota(jnp.int32, (SPAN, SPAN), 0)
    aff = jnp.where(square_r == lane, 0.0, fine_nt(cmf, bmf))

    squares = jnp.zeros((SPAN, 128), F32)
    for p in range(pairs):
        sl = slice(p * 128, (p + 1) * 128)
        efd = dot(wmix, e01[:, p * 256 : (p + 1) * 256])
        ef, eb = efd[:SPAN, :128], efd[:SPAN, 128:]
        dte = efd[SPAN : 2 * SPAN, :128]
        exp_s[0, :, sl] = ef
        exp_s[1, :, sl] = eb
        decay = efd[2 * SPAN : 2 * SPAN + 1, :128] + efd[2 * SPAN + 8 : 2 * SPAN + 9, :128]
        exp_s[2, 0:8, sl] = jnp.broadcast_to(decay, (8, 128))
        sf = sf_s[:, sl] * first
        sfb = sf.astype(BF)
        sf_o[0, :, sl] = sfb
        sbl, at = sbls(p)
        pb, sbd, ff, xpre, gate = (r(p)[0] for r in (pbs, sbds, ffs, xpres, gates))
        arrived = sbd[:, at].astype(F32) * enters_b
        sb = (sbl[0, :, at].astype(F32) + pb[0, 0:1, at] * arrived) * last
        sbb = sb.astype(BF)
        sb_o[0, :, sl] = sbb
        sf_s[:, sl] = sf * decay + ff[0, :, at].astype(F32)
        xp = xpre[:, at].astype(F32)
        x = xp * sigmoid(xp)
        xd = x * dte
        bd = jnp.concatenate(
            [jnp.where(low_half, xd, 0.0), jnp.where(low_half, 0.0, xd)], axis=0
        ).astype(BF)
        ms = []
        for h in (2 * p, 2 * p + 1):
            spread = jnp.minimum(
                col[:, h : h + 1] - row[h : h + 1, :],
                row[GROUP + h : GROUP + h + 1, :] - col[:, GROUP + h : GROUP + h + 1],
            )
            ms.append((aff * jnp.exp2(spread)).astype(BF))
        y = dot(jnp.concatenate(ms, axis=1), bd)
        carried = dot(cm, side(sfb, sbb))
        y = y + ef * carried[:, :128] + eb * carried[:, 128:] + skip[:, sl] * x
        y_s[:, sl] = y
        g = gate[:, at].astype(F32)
        gated = y * (g * sigmoid(g))
        squares = squares + gated * gated

    gsc = lax.rsqrt(jnp.sum(squares, axis=1, keepdims=True) * (1.0 / width) + EPS)
    inner = jnp.zeros((SPAN, 128), F32)
    for p in range(pairs):
        sl = slice(p * 128, (p + 1) * 128)
        gate, at = gates(p)
        g = gate[:, at].astype(F32)
        gunit = y_s[:, sl] * (g * sigmoid(g)) * gsc
        gnorm_o[:, sl] = (gunit * ggain[:, sl]).astype(BF)
        dgn = dgn_s[:, sl]
        dgu = dgn * gunit
        ggain_o[:, sl] += jnp.sum(dgu, axis=0, keepdims=True)
        inner = inner + dgu * ggain[:, sl]
    mean = jnp.sum(inner, axis=1, keepdims=True) * (1.0 / width)
    out_o[...] = (hid[...].astype(F32) + live * dot(gnorm_o[...], ow[...])).astype(BF)

    for p in range(pairs):
        sl = slice(p * 128, (p + 1) * 128)
        gate, at = gates(p)
        g = gate[:, at].astype(F32)
        sg = sigmoid(g)
        act = g * sg
        y = y_s[:, sl]
        gunit = y * act * gsc
        dgated = gsc * (dgn_s[:, sl] * ggain[:, sl] - gunit * mean)
        dy = dgated * act
        dy_o[:, sl] = dy.astype(BF)
        dgate_o[:, sl] = (dgated * y * (sg * (1.0 + g * (1.0 - sg)))).astype(BF)
        xp = xpres(p)[0][:, at].astype(F32)
        skip_o[:, sl] += jnp.sum(dy * (xp * sigmoid(xp)), axis=0, keepdims=True)
        decay = exp_s[2, 0:1, sl]
        states = dot(ct, side(exp_s[0, :, sl] * dy, exp_s[1, :, sl] * dy).astype(BF))
        dff, dfb = states[:, :128], states[:, 128:]
        dff_o[0, :, sl] = dff.astype(BF)
        q = q_s[0:1, sl]
        gf_s[:, sl] = gf_s[:, sl] + q * dff
        q_s[:, sl] = jnp.broadcast_to(q * decay * last, (8, 128))
        gb = gb_s[:, sl] * first
        pg = pg_s[0:1, sl] * first
        gbl_o[0, :, sl] = gb.astype(BF)
        pg_o[0, :, sl] = jnp.broadcast_to(pg, (8, 128))
        gb_s[:, sl] = gb * decay + dfb
        pg_s[:, sl] = jnp.broadcast_to(pg * decay, (8, 128))

    @pl.when(i == pl.num_programs(0) - 1)
    def _():
        gft_o[...] = gf_s[...]
        gbt_o[...] = gb_s[...]
        pgf_o[...] = q_s[...]
        pgb_o[...] = pg_s[...]
        hand_o[...] = jnp.where(sc[0] == 0, gb_s[...], gf_s[...]).astype(BF)


def mix(sc, split, bc, col, row, hidden, out_grad, ow, owt, ggain, skip, e01):
    tokens, width_in = hidden.shape
    groups = len(split[0])
    width = e01.shape[1] // 2
    part = width // groups
    blocks = tokens // SPAN

    def ahead(shape):
        rank = len(shape)
        return pl.BlockSpec(shape, lambda i: (i,) + (0,) * (rank - 1))

    sds = jax.ShapeDtypeStruct
    state = (1, STATE, width)
    outs = [
        (sds((tokens, width_in), BF), ahead((SPAN, width_in))),
        (sds((tokens, width), BF), ahead((SPAN, width))),
        (sds((tokens, width), BF), ahead((SPAN, width))),
        (sds((tokens, width), BF), ahead((SPAN, width))),
        (sds((blocks, STATE, width), BF), ahead(state)),
        (sds((blocks, STATE, width), BF), ahead(state)),
        (sds((blocks, STATE, width), BF), ahead(state)),
        (sds((blocks, 8, width), F32), ahead((1, 8, width))),
        (sds((blocks, STATE, width), BF), ahead(state)),
        (sds((STATE, width), F32), full((STATE, width))),
        (sds((STATE, width), F32), full((STATE, width))),
        (sds((8, width), F32), full((8, width))),
        (sds((8, width), F32), full((8, width))),
        (sds((STATE, width), BF), full((STATE, width))),
        (sds((1, width), F32), full((1, width))),
        (sds((1, width), F32), full((1, width))),
    ]
    shared = [ow, owt, ggain, skip, e01]
    in_specs = [SMEM]
    for shape in (
        (SPAN, part), (SPAN, part), (1, STATE, part), (1, STATE, part), (1, 8, part),
    ):
        in_specs += [ahead(shape)] * groups
    in_specs += [full((STATE, part))] * (2 * groups)
    in_specs += [ahead((SPAN, 128))] * 3 + [ahead((SPAN, width_in))] * 2
    in_specs += [full(a.shape) for a in shared]
    return pl.pallas_call(
        functools.partial(mix_kernel, groups),
        grid=(blocks,),
        in_specs=in_specs,
        out_specs=[spec for _, spec in outs],
        out_shape=[shape for shape, _ in outs],
        scratch_shapes=[
            pltpu.VMEM((STATE, width), F32),
            pltpu.VMEM((STATE, width), F32),
            pltpu.VMEM((STATE, width), F32),
            pltpu.VMEM((8, width), F32),
            pltpu.VMEM((8, width), F32),
            pltpu.VMEM((SPAN, width), F32),
            pltpu.VMEM((SPAN, width), F32),
            pltpu.VMEM((3, SPAN, width), F32),
        ],
        compiler_params=pltpu.CompilerParams(vmem_limit_bytes=58 * 1024 * 1024),
        cost_estimate=cost(60),
        name="mix",
    )(sc, *[a for kind in split for a in kind], bc, col, row, hidden, out_grad, *shared)


def back_kernel(heads, groups, *refs):
    refs = list(refs)
    sc = refs.pop(0)
    xpres, vs, gfds, gbds = split_refs(refs, groups, 4)
    back_body(heads, sc, xpres, vs, gfds, gbds, *refs)


def back_body(
    heads, sc, xpres, vs, gfds, gbds,
    dy_r, bc_r, ps_r, pspre_r, col_r, row_r, sf_r, sb_r, gbl, pg, dff,
    skip, cv, cs, hv, spot, e01, seg4, seg2, segs, tris,
    dv_o, dst_o, dz_o, cvg_o, csg_o, head_o, edge_o, edges_o,
    gf_s, edge_s, edges_s, da_s, cross_s, nad_s,
):
    step = pl.program_id(0)
    blocks = pl.num_programs(0)
    i = blocks - 1 - step
    length = sc[1]
    place = sc[0] + i * SPAN
    last = jnp.where(lax.rem(place + SPAN, length) == 0, 0.0, 1.0)
    width = e01.shape[1] // 2
    pairs = width // 128

    @pl.when(step == 0)
    def _():
        enters_f = jnp.where(sc[5] == 1, 1.0, 0.0)
        for p in range(pairs):
            ref, at = gfds(p)
            gf_s[:, p * 128 : (p + 1) * 128] = ref[:, at].astype(F32) * enters_f
        edge_s[...] = jnp.zeros_like(edge_s)
        edges_s[...] = jnp.zeros_like(edges_s)
        da_s[...] = jnp.zeros_like(da_s)
        nad_s[...] = jnp.broadcast_to(-jnp.exp(fine(hv[...], spot[...])[1:2]), (8, 128))
        cvg_o[...] = jnp.zeros_like(cvg_o)
        csg_o[...] = jnp.zeros_like(csg_o)
        head_o[...] = jnp.zeros_like(head_o)

    lane = lanes_of(SPAN)
    low_half = lane < HEAD_DIM
    col = col_r[...]
    row = row_r[...]
    end = jnp.broadcast_to(col[SPAN - 1 : SPAN], (8, 128))
    end1 = pltpu.roll(end, GROUP, 1)
    w = jnp.exp2(jnp.where(lane < 32, col, jnp.where(lane < 64, end1[0:1] - col, 0.0)))
    dec = jnp.exp2(jnp.where(lanes_of(8) < 32, end, 0.0))
    high = dec.astype(BF).astype(F32)
    inner = jnp.exp2(jnp.where(lane < 32, end[0:1] - col, jnp.where(lane < 64, col, 0.0)))
    steps = pltpu.roll(col, 64, 1)
    wall = jnp.concatenate([w, inner, steps, high, dec - high], axis=0).astype(BF)
    bc = bc_r[...]
    bmf, cmf = bc[:, :STATE], bc[:, STATE:]
    bm, cm = bmf.astype(BF), cmf.astype(BF)
    nad = nad_s[0:1]
    enters_b = jnp.where(sc[6] == 1, 1.0, 0.0)
    square_r = lax.broadcasted_iota(jnp.int32, (SPAN, SPAN), 0)
    off = square_r != lane
    aff = jnp.where(off, fine_nt(bmf, cmf), 0.0)

    daff = jnp.zeros((SPAN, SPAN), F32)
    red = jnp.zeros((SPAN, 128), F32)
    whole = jnp.zeros((SPAN, 128), F32)
    ddt = jnp.zeros((SPAN, 128), F32)
    dc = jnp.zeros((SPAN, STATE), F32)
    db = jnp.zeros((SPAN, STATE), F32)
    for p in range(pairs):
        sl = slice(p * 128, (p + 1) * 128)
        two = slice(p * 256, (p + 1) * 256)
        efd = dot(wall, e01[:, two])
        ef, eb = efd[:SPAN, :128], efd[:SPAN, 128:]
        wf, wb = efd[SPAN : 2 * SPAN, :128], efd[SPAN : 2 * SPAN, 128:]
        dte = efd[2 * SPAN : 3 * SPAN, :128]
        decay = efd[3 * SPAN : 3 * SPAN + 1, :128] + efd[3 * SPAN + 8 : 3 * SPAN + 9, :128]
        sf, sb = sf_r[0, :, sl], sb_r[0, :, sl]
        gf32 = gf_s[:, sl] * last
        gbd, at = gbds(p)
        arrived = gbd[:, at].astype(F32) * enters_b
        gb32 = gbl[0, :, sl].astype(F32) + pg[0, 0:1, sl] * arrived
        gf, gb = gf32.astype(BF), gb32.astype(BF)
        gf_s[:, sl] = gf32 * decay + dff[0, :, sl].astype(F32)
        cross = (sf.astype(F32) * gf32 + sb.astype(F32) * gb32) * decay
        cross_s[:, sl] = jnp.broadcast_to(jnp.sum(cross, axis=0, keepdims=True), (8, 128))
        xp = xpres(p)[0][:, at].astype(F32)
        sg = sigmoid(xp)
        x = xp * sg
        xd = x * dte
        dy = dy_r[:, sl].astype(F32)
        efdy, ebdy = ef * dy, eb * dy
        wfxd, wbxd = wf * xd, wb * xd
        s_both, g_both = side(sf, sb), side(gf, gb)
        fed = dot(bm, g_both)
        cf, cb = wf * fed[:, :128], wb * fed[:, 128:]
        carried = dot(cm, s_both)
        edy = side(efdy, ebdy)
        dc = dc + dot_nt(edy.astype(BF), s_both)
        db = db + dot_nt(side(wfxd, wbxd).astype(BF), g_both)
        products = side((edy * carried).astype(BF), side(xd * cf, xd * cb).astype(BF))
        red = red + dot(products, seg4[p * 512 : (p + 1) * 512, :])
        bd = jnp.concatenate(
            [jnp.where(low_half, dy, 0.0), jnp.where(low_half, 0.0, dy)], axis=0
        ).astype(BF)
        dm = dot_nt(xd.astype(BF), bd)
        ms = []
        for k in range(2):
            h = 2 * p + k
            spread = jnp.minimum(
                row[h : h + 1, :] - col[:, h : h + 1],
                col[:, GROUP + h : GROUP + h + 1] - row[GROUP + h : GROUP + h + 1, :],
            )
            f = jnp.exp2(spread)
            m = aff * f
            ms.append(m.astype(BF))
            dmh = dm[:, k * 128 : (k + 1) * 128]
            daff = daff + f * dmh
            q = m * dmh
            ql = jnp.where(square_r < lane, q, 0.0)
            qu = q - ql
            da_s[h : h + 1, :] = jnp.sum(ql, axis=0, keepdims=True)
            da_s[GROUP + h : GROUP + h + 1, :] = jnp.sum(qu, axis=0, keepdims=True)
            whole = jnp.where(lane == h, jnp.sum(ql, axis=1, keepdims=True), whole)
            whole = jnp.where(lane == GROUP + h, jnp.sum(qu, axis=1, keepdims=True), whole)
        dxd = dot(jnp.concatenate(ms, axis=1), bd) + cf + cb
        ddt = ddt + dot(high_low(x * dxd), seg2[two, :])
        dx = dte * dxd + skip[:, sl] * dy
        dxp = dx * (sg * (1.0 + xp * (1.0 - sg)))
        ext = jnp.concatenate([dxp, edge_s[:, sl] * last], axis=0)
        edge_s[:, sl] = dxp[:8]
        v = vs(p)[0][:, at].astype(F32)
        dv = jnp.zeros((SPAN, 128), F32)
        for j in range(TAPS):
            moved = shifted(ext, j, SPAN)
            k = TAPS - 1 - j
            dv = dv + moved * cv[k : k + 1, sl]
            cvg_o[k : k + 1, sl] += jnp.sum(v * moved, axis=0, keepdims=True)
        dv_o[:, sl] = dv.astype(BF)

    dafb = jnp.where(off, daff, 0.0).astype(BF)
    db = db + dot(dafb, cm)
    dc = dc + dot_tn(dafb, bm)
    dbc = jnp.concatenate([db, dc], axis=1)
    pp = pspre_r[...]
    sp = sigmoid(pp)
    dpp = dbc * (sp * (1.0 + pp * (1.0 - sp)))
    ext = jnp.concatenate([dpp, edges_s[...] * last], axis=0)
    edges_s[...] = dpp[:8]
    ps = ps_r[...]
    dst = jnp.zeros((SPAN, 128), F32)
    for j in range(TAPS):
        moved = shifted(ext, j, SPAN)
        k = TAPS - 1 - j
        dst = dst + moved * cs[k : k + 1, :]
        csg_o[k : k + 1, :] += jnp.sum(ps * moved, axis=0, keepdims=True)
    dst_o[...] = dst.astype(BF)

    red = red - whole + jnp.transpose(da_s[...])
    hi = red.astype(BF)
    lo = (red - hi.astype(F32)).astype(BF)
    summed = dot(tris[...], hi) + dot(tris[...], lo)
    parts = [summed[g * SPAN : (g + 1) * SPAN] for g in range(4)]
    picked = jnp.where(
        lane < 32, parts[0], jnp.where(lane < 64, parts[1], jnp.where(lane < 96, parts[2], parts[3]))
    )
    total = picked + pltpu.roll(picked, 64, 1)
    total = total + pltpu.roll(total, 32, 1)
    crossed = cross_s[...]
    crossed_hi = crossed.astype(BF)
    crossed_lo = (crossed - crossed_hi.astype(F32)).astype(BF)
    da = total + (dot(crossed_hi, segs[...]) + dot(crossed_lo, segs[...]))[0:1]
    dz = (ddt + da * nad) * col
    dz = jnp.where((lane >= 96) & (lane < 96 + heads), dz, 0.0)
    dz_o[...] = dz.astype(BF)
    head_o[0:1, :] += jnp.sum(da * col * nad, axis=0, keepdims=True)
    head_o[1:2, :] += jnp.sum(dz, axis=0, keepdims=True)

    @pl.when(i == 0)
    def _():
        edge_o[...] = edge_s[...]
        edges_o[...] = edges_s[...]


def back(heads, sc, split, dy, bc, ps, pspre, col, row, sf, sb, gbl, pg, dff, skip, cv, cs, hv, spot):
    tokens, width = dy.shape
    groups = len(split[0])
    part = width // groups
    blocks = tokens // SPAN
    maps = expanders(heads)
    every = sum(maps)
    seg4 = by_pairs([m.T for m in maps], 0)
    seg2 = by_pairs([every.T, every.T], 0)
    segs = every.T
    at = np.arange(SPAN)
    row_at, col_at = at[:, None], at[None, :]
    tris = np.concatenate(
        [col_at >= row_at, col_at <= row_at, col_at < row_at, col_at > row_at], axis=0
    ).astype(np.float32)
    e01 = by_pairs(maps[:2], 1)

    def rev(shape):
        rank = len(shape)
        return pl.BlockSpec(shape, lambda i: (blocks - 1 - i,) + (0,) * (rank - 1))

    sds = jax.ShapeDtypeStruct
    state = (1, STATE, width)
    outs = [
        (sds((tokens, width), BF), rev((SPAN, width))),
        (sds((tokens, 128), BF), rev((SPAN, 128))),
        (sds((tokens, 128), BF), rev((SPAN, 128))),
        (sds((TAPS, width), F32), full((TAPS, width))),
        (sds((TAPS, 128), F32), full((TAPS, 128))),
        (sds((8, 128), F32), full((8, 128))),
        (sds((8, width), F32), full((8, width))),
        (sds((8, 128), F32), full((8, 128))),
    ]
    shared = [skip, cv, cs, hv, spot]
    shared += [jnp.asarray(m, BF) for m in (e01, seg4, seg2, segs, tris)]
    in_specs = [SMEM] + [rev((SPAN, part))] * (2 * groups)
    in_specs += [full((STATE, part))] * (2 * groups)
    in_specs += [rev((SPAN, width))] + [rev((SPAN, 128))] * 5
    in_specs += [rev(state)] * 3 + [rev((1, 8, width)), rev(state)]
    in_specs += [full(a.shape) for a in shared]
    return pl.pallas_call(
        functools.partial(back_kernel, heads, groups),
        grid=(blocks,),
        in_specs=in_specs,
        out_specs=[spec for _, spec in outs],
        out_shape=[shape for shape, _ in outs],
        scratch_shapes=[
            pltpu.VMEM((STATE, width), F32),
            pltpu.VMEM((8, width), F32),
            pltpu.VMEM((8, 128), F32),
            pltpu.VMEM((128, 128), F32),
            pltpu.VMEM((8, width), F32),
            pltpu.VMEM((8, 128), F32),
        ],
        compiler_params=pltpu.CompilerParams(vmem_limit_bytes=58 * 1024 * 1024),
        cost_estimate=cost(100),
        name="back",
    )(
        sc, *[a for kind in split for a in kind],
        dy, bc, ps, pspre, col, row, sf, sb, gbl, pg, dff, *shared,
    )


def input_kernel(groups, *refs):
    refs = list(refs)
    slabs = refs[:groups]
    dgate, dv, dst, dz, ws, steps_t, gain, place, hid, gout, grad_o, gain_o, wg, wv, wst = refs[groups:]

    @pl.when(pl.program_id(0) == 0)
    def _():
        gain_o[...] = jnp.zeros_like(gain_o)
        wst[...] = dot_tn(place[...].astype(BF), steps_t[...]).astype(BF)
        pairs_in = slabs[0].shape[0] // 2
        for p in range(groups * pairs_in):
            slab, h = slabs[p // pairs_in], 2 * (p % pairs_in)
            g, v = unpaired(slab[h].astype(F32), slab[h + 1].astype(F32))
            wg[:, p * 128 : (p + 1) * 128] = g.astype(BF)
            wv[:, p * 128 : (p + 1) * 128] = v.astype(BF)

    dn = dot_nt(dst[...], ws[...]) + dot(dz[...], wst[...])
    dn = dn + dot_nt(dgate[...], wg[...]) + dot_nt(dv[...], wv[...])
    u = hid[...].astype(F32)
    scale = lax.rsqrt(jnp.mean(u * u, axis=1, keepdims=True) + EPS)
    unit = u * scale
    gain_o[...] += jnp.sum(dn * unit, axis=0, keepdims=True)
    du = dn * gain[...]
    inner = jnp.mean(du * unit, axis=1, keepdims=True)
    grad_o[...] = (gout[...].astype(F32) + scale * (du - unit * inner)).astype(BF)


def input_side(slabs, dgate, dv, dst, dz, ws, steps_t, gain, hidden, out_grad):
    tokens, width_in = hidden.shape
    tile = min(512, tokens)

    def rows(a):
        return pl.BlockSpec((tile, a.shape[1]), lambda i: (i, 0))

    sds = jax.ShapeDtypeStruct
    fixed = list(slabs)
    width = dgate.shape[1]
    streams = [dgate, dv, dst, dz]
    specs = [full(a.shape) for a in fixed] + [rows(a) for a in streams]
    place = placing(steps_t.shape[0], (3,))
    specs += [full(a.shape) for a in (ws, steps_t, gain, place)] + [rows(hidden), rows(out_grad)]
    return pl.pallas_call(
        functools.partial(input_kernel, len(slabs)),
        grid=(tokens // tile,),
        in_specs=specs,
        out_specs=[rows(hidden), full((1, width_in))],
        out_shape=[sds((tokens, width_in), BF), sds((1, width_in), F32)],
        scratch_shapes=[pltpu.VMEM((width_in, width), BF)] * 2 + [pltpu.VMEM((128, width_in), BF)],
        compiler_params=pltpu.CompilerParams(vmem_limit_bytes=58 * 1024 * 1024),
        cost_estimate=cost(15),
        name="input_side",
    )(*fixed, *streams, ws, steps_t, gain, place, hidden, out_grad)


def reduce_kernel(bits, lanes, mats, *refs):
    n_mats = len(mats)
    srcs, both, tiny = refs[:n_mats], refs[n_mats], refs[n_mats + 1]
    paired_o, last_o, both_o, tiny_o = refs[n_mats + 2 : n_mats + 6]
    outs = (*refs[n_mats + 6 : n_mats + 8], last_o)
    scratch = refs[n_mats + 8 :]
    own_r, sent = scratch[0], scratch[1]
    halves, parts = scratch[2 : 2 + bits], scratch[2 + bits : 1 + 2 * bits]
    tiny_r, tiny_s, send_s, recv_s, tsend_s, trecv_s = scratch[1 + 2 * bits :]
    rows = srcs[0].shape[0] if mats[0] == "cols" else srcs[0].shape[0] // 2
    width = outs[0].shape[1]
    me = lax.axis_index("dp")
    chan = lax.axis_index("chan")
    bit = [lax.rem(lax.div(me, 2**k), 2) for k in range(bits)]
    partner = [{"dp": me + (1 - 2 * bit[k]) * 2**k} for k in range(bits)]
    across = {"chan": 1 - chan}
    stages = [partner[0], across] + partner[1:]

    barrier = pltpu.get_barrier_semaphore()
    for device in stages:
        pl.semaphore_signal(barrier, inc=1, device_id=device, device_id_type=pl.DeviceIdType.MESH)
    pl.semaphore_wait(barrier, bits + 1)

    chunks = [(m, s) for m in range(n_mats) for s in range(0, width, lanes)]
    mains = len(chunks)
    n = mains + both.shape[1] // lanes
    half = rows // 2

    def mult(v):
        return pl.multiple_of(v, 16)

    def source(c, which, part):
        if c >= mains:
            return both.at[pl.ds(mult(part * half), half), pl.ds((c - mains) * lanes, lanes)]
        m, s = chunks[c]
        if mats[m] == "cols":
            return srcs[m].at[pl.ds(mult(part * half), half), pl.ds(which * width + s, lanes)]
        return srcs[m].at[pl.ds(mult(which * rows + part * half), half), pl.ds(s, lanes)]

    def target(c, start, size):
        if c >= mains:
            return both_o.at[pl.ds(mult(start), size), pl.ds((c - mains) * lanes, lanes)]
        m, s = chunks[c]
        return outs[m].at[pl.ds(mult(start), size), pl.ds(s, lanes)]

    def copy(src, dst, c, k, device):
        return pltpu.make_async_remote_copy(
            src_ref=src,
            dst_ref=dst,
            send_sem=send_s.at[c, k],
            recv_sem=recv_s.at[c, k],
            device_id=device,
            device_id_type=pl.DeviceIdType.MESH,
        )

    offset = [bit[0] * half]
    for k in range(1, bits):
        offset.append(offset[-1] + bit[k] * (half >> k))

    def first(c, which):
        if c >= mains and which == 0:
            return None
        slot = own_r.at[c, which]
        return copy(source(c, which, 1 - bit[0]), slot, c, which, partner[0])

    def second(c):
        return copy(sent.at[c], halves[0].at[c], c, 2, across)

    def halving(c, k):
        size = half >> k
        src = parts[k - 1].at[c, pl.ds(mult((1 - bit[k]) * size), size), :]
        return copy(src, halves[k].at[c], c, 2 + k, partner[k])

    def doubling(c, k):
        size = half >> k
        place = target(c, offset[k], size)
        return copy(place, place, c, 2 + bits + k, partner[k])

    def f32(ref):
        return ref[...].astype(F32)

    def stage(c, s):
        if s == 0:
            for which in (0, 1):
                rdma = first(c, which)
                if rdma is not None:
                    rdma.start()
        elif s == 1:
            first(c, 1).wait_recv()
            sent[c] = (f32(source(c, 1, bit[0])) + f32(own_r.at[c, 1])).astype(BF)
            second(c).start()
        elif s == 2:
            second(c).wait_recv()
            if c >= mains:
                total = f32(sent.at[c]) + f32(halves[0].at[c])
            else:
                first(c, 0).wait_recv()
                total = f32(source(c, 0, bit[0])) + f32(own_r.at[c, 0]) + f32(halves[0].at[c])
            parts[0][c] = total.astype(BF)
            halving(c, 1).start()
        elif s < bits + 2:
            k = s - 2
            size = half >> k
            halving(c, k).wait_recv()
            kept = parts[k - 1].at[c, pl.ds(mult(bit[k] * size), size), :]
            total = (f32(kept) + f32(halves[k].at[c])).astype(BF)
            if k < bits - 1:
                parts[k][c] = total
                halving(c, k + 1).start()
            else:
                target(c, offset[k], size)[...] = total
                doubling(c, k).start()
        else:
            k = 2 * bits + 1 - s
            doubling(c, k).wait_recv()
            if k > 0:
                doubling(c, k - 1).start()

    def tiny_copy(k):
        return pltpu.make_async_remote_copy(
            src_ref=tiny if k == 0 else tiny_s.at[k - 1],
            dst_ref=tiny_r.at[k],
            send_sem=tsend_s.at[k],
            recv_sem=trecv_s.at[k],
            device_id=stages[k],
            device_id_type=pl.DeviceIdType.MESH,
        )

    tiny_copy(0).start()
    last = 2 * bits + 1
    for tick in range(n + SLACK * last):
        for s in range(last, -1, -1):
            c = tick - SLACK * s
            if 0 <= c < n:
                stage(c, s)
        if 1 <= tick <= bits + 1:
            k = tick - 1
            tiny_copy(k).wait_recv()
            before = tiny[...] if k == 0 else tiny_s[k - 1]
            total = before + tiny_r[k]
            if k < bits:
                tiny_s[k] = total
                tiny_copy(k + 1).start()
            else:
                tiny_o[...] = total

    low_half = lanes_of(rows) < HEAD_DIM
    for p in range(width // 128):
        sl = slice(p * 128, (p + 1) * 128)
        g, v = f32(outs[0].at[:, sl]), f32(outs[1].at[:, sl])
        paired_o[2 * p] = jnp.where(low_half, g, pltpu.roll(v, 64, 1))
        paired_o[2 * p + 1] = jnp.where(low_half, pltpu.roll(g, 64, 1), v)

    for c in range(n):
        for which in (0, 1):
            rdma = first(c, which)
            if rdma is not None:
                rdma.wait_send()
        second(c).wait_send()
        for k in range(1, bits):
            halving(c, k).wait_send()
        for k in range(bits):
            doubling(c, k).wait_send()
    for k in range(bits + 1):
        tiny_copy(k).wait_send()


def reduce_all(bits, mats, both, tiny, lanes):
    kinds = [kind for _, kind in mats]
    arrays = [a for a, _ in mats]
    rows = arrays[0].shape[0] if kinds[0] == "cols" else arrays[0].shape[0] // 2
    width = arrays[0].shape[1] // 2 if kinds[0] == "cols" else arrays[0].shape[1]
    half = rows // 2
    n = len(arrays) * (width // lanes) + both.shape[1] // lanes
    vmem = pl.BlockSpec(memory_space=pltpu.VMEM)
    sds = jax.ShapeDtypeStruct
    scratch = [pltpu.VMEM((rows, width), BF)] * 2
    scratch += [pltpu.VMEM((n, 2, half, lanes), BF), pltpu.VMEM((n, half, lanes), BF)]
    scratch += [pltpu.VMEM((n, half >> k, lanes), BF) for k in range(bits)]
    scratch += [pltpu.VMEM((n, half >> k, lanes), BF) for k in range(bits - 1)]
    scratch += [
        pltpu.VMEM((bits + 1,) + tiny.shape, F32),
        pltpu.VMEM((bits,) + tiny.shape, F32),
        pltpu.SemaphoreType.DMA((n, 2 + 2 * bits)),
        pltpu.SemaphoreType.DMA((n, 2 + 2 * bits)),
        pltpu.SemaphoreType.DMA((bits + 1,)),
        pltpu.SemaphoreType.DMA((bits + 1,)),
    ]
    return pl.pallas_call(
        functools.partial(reduce_kernel, bits, lanes, kinds),
        out_shape=[
            sds((width // HEAD_DIM, rows, 128), F32), sds((rows, width), BF), sds(both.shape, BF), sds(tiny.shape, F32)
        ],
        in_specs=[vmem] * (len(arrays) + 2),
        out_specs=[vmem] * 4,
        scratch_shapes=scratch,
        compiler_params=pltpu.CompilerParams(
            collective_id=0, has_side_effects=True, vmem_limit_bytes=58 * 1024 * 1024
        ),
        name="reduce_all",
    )(*arrays, both, tiny)


def handed(total, passed, shards, up):
    pairs = [(k, k + 1) if up else (k + 1, k) for k in range(shards - 1)]
    entering = lax.ppermute(total.astype(BF), "chan", pairs)
    for _ in range(shards - 2):
        now = total + passed[0:1] * entering.astype(F32)
        entering = lax.ppermute(now.astype(BF), "chan", pairs)
    return entering


def swap(v):
    return lax.ppermute(v, "chan", [(0, 1), (1, 0)])


def core_swap(v):
    size = lax.axis_size("dp")
    return lax.ppermute(v, "dp", [(k, k ^ 1) for k in range(size)])


def on_device(
    hidden_in, norm_gain, gate_value_weight, state_weight, step_weight, value_conv, state_conv,
    step_bias, decay_log, skip_gain, gate_gain, out_weight, seq_length, seq_count, out_grad,
):
    tokens, width_in = hidden_in.shape
    channel = lax.axis_index("chan")
    shards = lax.axis_size("chan")
    groups_dp = lax.axis_size("dp")
    length, count = seq_length[0], seq_count[0]
    local_heads = gate_value_weight.shape[1]
    local = local_heads * HEAD_DIM
    heads = local_heads * shards
    width = heads * HEAD_DIM
    paired = shards == 2 and local_heads % 4 == 0 and groups_dp % 2 == 0
    one = jnp.ones((), jnp.int32)
    flags = [channel, 1 - channel, 1 - channel, channel] if paired else [one] * 4
    sc = jnp.stack([channel * tokens, length, count] + flags).astype(jnp.int32)
    ups = [(k, k + 1) for k in range(shards - 1)]
    downs = [(k + 1, k) for k in range(shards - 1)]
    gain = norm_gain[None]

    slab = gate_value_weight.transpose(1, 0, 2)
    edge = lax.ppermute(hidden_in[tokens - PAD :], "chan", ups)
    hv = jnp.stack([step_bias, decay_log, skip_gain])
    small = jnp.concatenate(
        [
            value_conv,
            gate_gain[None],
            jnp.pad(hv, ((0, 0), (0, local - local_heads))),
        ]
    )

    each_map = expanders(heads)
    e0, e1, _, _ = [jnp.asarray(e, BF) for e in each_map]
    e01 = jnp.asarray(by_pairs(each_map[:2], 1), BF)
    maps = (gain, state_weight, state_conv)
    if paired:
        core = lax.axis_index("dp") % 2
        half = lax.dynamic_slice_in_dim(slab, core * (local_heads // 2), local_heads // 2, 0)
        payload, edge = lax.optimization_barrier((half, edge))
        come = swap(payload)
        small_b, wstep_b, ow_b = swap(small), swap(step_weight), swap(out_weight)
        gate, v, xpre, ff, sbl, pb, _, _, _, _, hand, vh, normed, nedge, ps, pspre, bc, psh = project(
            sc, hidden_in, edge, slab, step_weight.T, value_conv, hv,
            e0[:, :local], e1[:, :local], maps=maps, final=False,
        )
        come, small_b, wstep_b, ow_b, nedge, hand = lax.optimization_barrier(
            (come, small_b, wstep_b, ow_b, nedge, hand)
        )
        also = core_swap(come)
        enter_b = swap(hand)
        halves = jnp.where(core == 0, jnp.stack([come, also]), jnp.stack([also, come]))
        slabs = [slab, halves.reshape(slab.shape)]
        smalls = [small, small_b]
        steps_t = jnp.concatenate([step_weight.T, wstep_b.T], axis=0)
        ow = jnp.concatenate([out_weight, ow_b], axis=0)
    else:
        slabs = [lax.all_gather(slab, "chan", axis=0, tiled=True)]
        gathered = lax.all_gather(small, "chan", axis=0)
        smalls = [gathered[k] for k in range(shards)]
        steps_t = lax.all_gather(step_weight.T, "chan", axis=0, tiled=True)
        ow = lax.all_gather(out_weight, "chan", axis=0, tiled=True)

    hv_all = jnp.concatenate([p[TAPS + 1 :, :local_heads] for p in smalls], axis=1)
    cv = jnp.concatenate([p[:TAPS] for p in smalls], axis=1)
    ggain = jnp.concatenate([p[TAPS : TAPS + 1] for p in smalls], axis=1)
    skip = jnp.repeat(hv_all[2:3], HEAD_DIM, axis=1)

    if paired:
        gate2, v2, xpre2, ff2, sbl2, pb2, _, _, _, _, hand2, vh2, col, row = project(
            sc, normed, nedge, slabs[1], steps_t, smalls[1][:TAPS], hv_all,
            e0[:, local:], e1[:, local:], bc=bc, final=True,
        )
        enter = [swap(hand2), enter_b]
        split = [[gate, gate2], [xpre, xpre2], [ff, ff2], [sbl, sbl2], [pb, pb2], enter, enter]
        vs, xs = [v, v2], [xpre, xpre2]
        vh = jnp.concatenate([vh, vh2], axis=1)
    else:
        (
            gate, v, xpre, ff, sbl, pb, sft, sbt, pft, pbt, _, vh, normed, nedge, ps, pspre, bc, psh,
            col, row,
        ) = project(
            sc, hidden_in, edge, slabs[0], steps_t, cv, hv_all, e0, e1, maps=maps,
        )
        sfd = handed(sft, pft, shards, True)
        sbd = handed(sbt, pbt, shards, False)
        split = [[gate], [xpre], [ff], [sbl], [pb], [sfd], [sbd]]
        vs, xs = [v], [xpre]
    (
        output, gnorm, dy, dgate, sf, sb, gbl, pg, dff, gft, gbt, pgf, pgb, hand, ggain_grad, skip_grad,
    ) = mix(sc, split, bc, col, row, hidden_in, out_grad, ow, ow.T, ggain, skip, e01)
    if paired:
        enter = swap(hand)
        enter = [enter[:, local:], enter[:, :local]]
        gfds = gbds = enter
    else:
        gfds = [handed(gft, pgf, shards, False)]
        gbds = [handed(gbt, pgb, shards, True)]

    own_ids = channel * tokens + jnp.arange(tokens, dtype=jnp.int32)
    live = jnp.where(own_ids // length < count, 1.0, 0.0)[:, None].astype(BF)
    ow_grad = dot_tn(gnorm, out_grad * live).astype(BF)
    dwg = dot_tn(normed, dgate).astype(BF)

    def absolute(parts, axis):
        if not paired:
            return jnp.concatenate(parts, axis=axis)
        a = jnp.concatenate(parts, axis=axis)
        b = jnp.concatenate(parts[::-1], axis=axis)
        return jnp.where(channel == 0, a, b)

    def shared(v, axis):
        if paired:
            a, b = jnp.split(v, 2, axis=axis)
            v = (a.astype(F32) + swap(b).astype(F32)).astype(BF)
        else:
            v = lax.psum_scatter(v, "chan", scatter_dimension=axis, tiled=True)
        return lax.psum(v, "dp")

    dv, dst, dz, cvg, csg, head_sums, edge_g, edges_g = back(
        heads, sc, [xs, vs, gfds, gbds], dy, bc, ps, pspre, col, row, sf, sb, gbl, pg, dff, skip, cv,
        state_conv, hv_all, placing(heads),
    )

    if paired:
        turned = jnp.concatenate([edge_g[:, local:], edge_g[:, :local]], axis=1)
    else:
        turned = edge_g
    kernel = jnp.concatenate([cv, state_conv], axis=1)
    past = jnp.concatenate([vh, psh], axis=1)
    reach = TAPS - 1
    after = lax.ppermute(jnp.concatenate([turned, edges_g], axis=1), "chan", downs)[:reach]
    joined = jnp.concatenate([edge_g, edges_g], axis=1)
    after = after * jnp.where(((channel + 1) * tokens) % length == 0, 0.0, 1.0)
    patch = jnp.zeros((reach, joined.shape[1]), F32)
    taps = []
    for j in range(TAPS):
        if j:
            moved = jnp.pad(after[:j], ((reach - j, 0), (0, 0)))
            patch = patch + moved * kernel[TAPS - 1 - j][None]
        taps.append(jnp.sum(joined[:j] * past[PAD - j :], axis=0))
    cross_taps = jnp.stack(taps[::-1])
    tail = jnp.pad(patch, ((PAD - reach, 0), (0, 0))).astype(BF)
    dv = dv.at[tokens - PAD :].add(tail[:, :width])
    dst = dst.at[tokens - PAD :].add(tail[:, width:])
    cvg = cvg + cross_taps[:, :width]
    csg = csg + cross_taps[:, width:]

    dwv = dot_tn(normed, dv).astype(BF)
    dws = dot_tn(normed, dst)
    dwst = dot_tn(normed, dz)[:, 96 : 96 + heads]
    input_grad, norm_gain_grad = input_side(
        slabs, dgate, dv, dst, dz, state_weight, steps_t, gain, hidden_in, out_grad
    )

    bias_sum = head_sums[1, 96 : 96 + heads]
    dlog_sum = head_sums[0, 64 : 64 + heads]
    skip_sum = skip_grad.reshape(heads, HEAD_DIM).sum(axis=1)

    def by_shard(k):
        cut, hcut = slice(k * local, (k + 1) * local), slice(k * local_heads, (k + 1) * local_heads)
        return jnp.concatenate(
            [cvg[:, cut].reshape(-1), ggain_grad[0, cut], bias_sum[hcut], dlog_sum[hcut], skip_sum[hcut]]
        )

    each = (TAPS + 1) * local + 3 * local_heads
    pad_each = -each % 128
    tiny = absolute([jnp.pad(by_shard(k), (0, pad_each)) for k in range(shards)], 0)
    tiny = jnp.concatenate([tiny, norm_gain_grad[0], csg.reshape(-1)])
    tiny = jnp.pad(tiny, (0, -tiny.shape[0] % 1024)).reshape(-1, 128)
    dwst = absolute([dwst[:, k * local_heads : (k + 1) * local_heads] for k in range(shards)], 1)
    both = jnp.concatenate([dws, jnp.pad(dwst, ((0, 0), (0, 128 - heads)))], axis=1).astype(BF)

    bits = groups_dp.bit_length() - 1
    if paired and groups_dp == 2**bits and bits >= 2 and width_in % (16 * groups_dp) == 0:
        gvw, owg, both, tiny = reduce_all(
            bits, [(dwg, "cols"), (dwv, "cols"), (ow_grad, "rows")], both, tiny, LANES
        )
        gvw = gvw.transpose(1, 0, 2)
        owg = owg.astype(F32)
    else:
        dwg, dwv, owg = shared(dwg, 1), shared(dwv, 1), shared(ow_grad, 0).astype(F32)
        both, tiny = lax.psum((both, tiny), ("dp", "chan"))
        pieces = [a.reshape(width_in, local_heads, HEAD_DIM) for a in (dwg, dwv)]
        gvw = jnp.concatenate(pieces, axis=2).astype(F32)
    both = both.astype(F32)
    flat = tiny.reshape(-1)
    base = (each + pad_each) * shards
    mine = lax.dynamic_slice_in_dim(flat, channel * (each + pad_each), each, 0)
    cuts = np.cumsum([TAPS * local, local, local_heads, local_heads])
    dwst = lax.dynamic_slice_in_dim(both[:, 128:], channel * local_heads, local_heads, 1)
    return (
        output,
        input_grad,
        flat[base : base + width_in],
        gvw,
        both[:, :128],
        dwst,
        mine[: cuts[0]].reshape(TAPS, local),
        flat[base + width_in : base + width_in + TAPS * 128].reshape(TAPS, 128),
        mine[cuts[1] : cuts[2]],
        mine[cuts[2] : cuts[3]],
        mine[cuts[3] :],
        mine[cuts[0] : cuts[1]],
        owg,
    )


def solution(mesh):
    in_specs = (
        P(("dp", "chan"), None),
        P(),
        P(None, "chan", None),
        P(),
        P(None, "chan"),
        P(None, "chan"),
        P(),
        P("chan"),
        P("chan"),
        P("chan"),
        P("chan"),
        P("chan", None),
        P("dp"),
        P("dp"),
        P(("dp", "chan"), None),
    )
    out_specs = (
        P(("dp", "chan"), None),
        P(("dp", "chan"), None),
        P(),
        P(None, "chan", None),
        P(),
        P(None, "chan"),
        P(None, "chan"),
        P(),
        P("chan"),
        P("chan"),
        P("chan"),
        P("chan"),
        P("chan", None),
    )
    return jax.shard_map(
        on_device, mesh=mesh, in_specs=in_specs, out_specs=out_specs, check_vma=False
    )
```
